128 devices in a mesh: tm: 4 (over z), height: 16 (over x, y), width: 2 (over core).
Axes of the slice: x: 4, y: 4, z: 4, core: 2. Of those that a mesh axis runs over, the one named last changes fastest.
Arguments:
- latent: bfloat16 [128, 8, 64, 512], P(None, 'tm', 'height', 'width'), may hold values from -64 to 64
- exponents: int32 [32], replicated, may hold values from -1 to 1
- cotangent: bfloat16 [128, 8, 64, 512], P(None, 'tm', 'height', 'width'), may hold values from -6 to 6
- conv_first: bfloat16 [128, 3456], replicated, may hold values from -0.109375 to 0.109375
- conv_second: bfloat16 [128, 3456], replicated, may hold values from -0.109375 to 0.109375
- gain_first: float32 [128], replicated, may hold values from 0.1 to 1.9
- shift_first: float32 [128], replicated, may hold values from -2.5 to 2.5
- gain_second: float32 [128], replicated, may hold values from 0.1 to 1.9
- shift_second: float32 [128], replicated, may hold values from -2.5 to 2.5
Outputs:
- decoded_grad: float32 [128, 8, 64, 512], P(None, 'tm', 'height', 'width')
- conv_first_grad: float32 [128, 3456], replicated
- conv_second_grad: float32 [128, 3456], replicated
The draws below stay inside these ranges and needn't reach their ends.
All inputs are finite; a program needn't handle non-finite values.
Results may differ from the reference program's by a relative error of at most 0.005.
Values may be sent and summed in bfloat16 or wider, within the bound.
A program may use at most 128 MiB of HBM per device.

```python
import jax
import jax.numpy as jnp
from jax import lax

CH = 128
GROUPS = 32
ROWS_DEV = 4
NT = 8
NR = 64
NC = 512


def draw_latent(key, part):
    key = jax.random.fold_in(key, 11)
    row_key, col_key, noise_key = jax.random.split(key, 3)
    frame_place = (jnp.arange(NT, dtype=jnp.float32) / (NT - 1))[None, :, None, None]
    row_scale = jnp.power(10.0, jax.random.uniform(row_key, (1, 1, NR, 1), dtype=jnp.float32))
    col_scale = jnp.power(10.0, jax.random.uniform(col_key, (1, 1, 1, NC), dtype=jnp.float32))
    noise_draw = jnp.clip(jax.random.normal(noise_key, (CH, NT, NR, NC), dtype=jnp.float32), -4.0, 4.0)
    frame_ramp = jnp.sqrt(1.0 + 2.0 * frame_place)
    offset = 5.0 + 10.0 * frame_place
    values = 0.1 * (noise_draw * frame_ramp * row_scale * col_scale + offset)
    return jnp.clip(values, -64.0, 64.0).astype(jnp.bfloat16)


def draw_cotangent(key, part):
    key = jax.random.fold_in(key, 23)
    noise_key, chan_key, frame_key, band_key = jax.random.split(key, 4)
    bands = NR // ROWS_DEV
    noise_draw = jnp.clip(jax.random.normal(noise_key, (CH, NT, NR, NC), dtype=jnp.float32), -4.0, 4.0)
    chan_offset = jax.random.uniform(chan_key, (CH, 1, 1, 1), dtype=jnp.float32, minval=-1.0, maxval=1.0)
    frame_offset = jax.random.uniform(frame_key, (CH, NT, 1, 1), dtype=jnp.float32, minval=-0.7, maxval=0.7)
    band_draw = jax.random.uniform(band_key, (CH, 1, bands, 1), dtype=jnp.float32, minval=-0.7, maxval=0.7)
    band_offset = jnp.repeat(band_draw, ROWS_DEV, axis=2)
    values = noise_draw + (chan_offset + frame_offset + band_offset)
    return jnp.clip(values, -6.0, 6.0).astype(jnp.bfloat16)


def place_ends(array, rng, smallest, top_value):
    place = [jax.random.randint(jax.random.fold_in(rng, axis), (), 0, length) for axis, length in enumerate(array.shape)]
    longest = array.shape.index(max(array.shape))
    beside = place[:longest] + [(place[longest] + 1) % array.shape[longest]] + place[longest + 1:]
    return array.at[tuple(place)].set(smallest).at[tuple(beside)].set(top_value)


def bell_draw(own_key, extent, scale, bound, kind=jnp.bfloat16):
    entries = jax.random.normal(own_key, extent, jnp.float32) * scale
    return jnp.minimum(jnp.maximum(entries, -bound), bound).astype(kind)


def setup_inputs(seed: int = 0) -> dict:
    streams_of = jax.random.split(jax.random.key(seed), 10)
    latent = draw_latent(jax.random.fold_in(streams_of[9], 71), 0)
    exponents = place_ends(jax.random.randint(streams_of[1], (GROUPS,), -1, 2), jax.random.fold_in(streams_of[1], 1), -1, 1).astype(jnp.int32)
    cotangent = draw_cotangent(jax.random.fold_in(streams_of[9], 71), 0)
    conv_first = bell_draw(streams_of[3], (CH, 27 * CH), (27 * CH) ** -0.5, 0.109375)
    conv_second = bell_draw(streams_of[4], (CH, 27 * CH), (27 * CH) ** -0.5, 0.109375)
    gain_first = jnp.clip(1.0 + 0.18 * jax.random.normal(streams_of[5], (CH,), jnp.float32), 0.1, 1.9)
    shift_first = bell_draw(streams_of[6], (CH,), 0.5, 2.5, jnp.float32)
    gain_second = jnp.clip(1.0 + 0.18 * jax.random.normal(streams_of[7], (CH,), jnp.float32), 0.1, 1.9)
    shift_second = bell_draw(streams_of[8], (CH,), 0.5, 2.5, jnp.float32)
    return dict(latent=latent, exponents=exponents, cotangent=cotangent, conv_first=conv_first, conv_second=conv_second, gain_first=gain_first, shift_first=shift_first, gain_second=gain_second, shift_second=shift_second)


epsilon = 1e-05

def convolve(values, weight):
    channels = values.shape[0]
    kernel = weight.reshape(channels, 3, 3, 3, channels).transpose(0, 4, 1, 2, 3)
    result = lax.conv_general_dilated(values[None], kernel, (1, 1, 1), [(2, 0), (1, 1), (1, 1)], dimension_numbers=('NCDHW', 'OIDHW', 'NCDHW'), precision=lax.Precision.HIGHEST)
    return result[0]

def per_channel(stat):
    return jnp.repeat(stat, CH // GROUPS)[:, None, None, None]

def channel(vector):
    return vector[:, None, None, None]

def group_mean(values):
    return lax.optimization_barrier(jnp.mean(values.reshape(GROUPS, -1), axis=1))

def normalize(values):
    mean_value = group_mean(values)
    centered = values - per_channel(mean_value)
    variance = group_mean(centered * centered)
    inverse = 1.0 / jnp.sqrt(variance + epsilon)
    return (centered * per_channel(inverse), inverse)

def silu_slope(pre):
    sigmoid_value = jax.nn.sigmoid(pre)
    return sigmoid_value * (1.0 + pre * (1.0 - sigmoid_value))

def norm_backward(grad, pre, normed, gain, inverse):
    scaled = grad * silu_slope(pre) * channel(gain)
    first_mean = group_mean(scaled)
    second_mean = group_mean(scaled * normed)
    return per_channel(inverse) * (scaled - per_channel(first_mean) - normed * per_channel(second_mean))

def reference(latent, exponents, cotangent, conv_first, conv_second, gain_first, shift_first, gain_second, shift_second):
    scaling = jnp.exp2(exponents.astype(jnp.float32))
    decoded = latent.astype(jnp.float32) * per_channel(scaling)
    normed_first, inverse_first = normalize(decoded)
    pre_first = normed_first * channel(gain_first) + channel(shift_first)
    act_first = jax.nn.silu(pre_first).astype(jnp.bfloat16)
    hidden, pull_first = jax.vjp(convolve, act_first.astype(jnp.float32), conv_first.astype(jnp.float32))
    normed_second, inverse_second = normalize(hidden)
    pre_second = normed_second * channel(gain_second) + channel(shift_second)
    act_second = jax.nn.silu(pre_second).astype(jnp.bfloat16)
    output_value, pull_second = jax.vjp(convolve, act_second.astype(jnp.float32), conv_second.astype(jnp.float32))
    grad_second, conv_second_grad = pull_second(cotangent.astype(jnp.float32))
    hidden_grad = norm_backward(grad_second, pre_second, normed_second, gain_second, inverse_second).astype(jnp.bfloat16)
    grad_first, conv_first_grad = pull_first(hidden_grad.astype(jnp.float32))
    decoded_grad = cotangent.astype(jnp.float32) + norm_backward(grad_first, pre_first, normed_first, gain_first, inverse_first)
    return (decoded_grad, conv_first_grad, conv_second_grad)
```

```python
import functools

import jax
import jax.numpy as jnp
from jax import lax
from jax.experimental import pallas as pl
from jax.experimental.pallas import tpu as pltpu
from jax.sharding import PartitionSpec as P

MESH = pl.DeviceIdType.MESH
EPS = 1e-05
CH = 128
F32 = jnp.float32
BF16 = jnp.bfloat16


def group_sum(row):
    lane = lax.broadcasted_iota(jnp.int32, row.shape, 1)
    pair = row + jnp.where(lane % 2 == 0, pltpu.roll(row, CH - 1, 1), pltpu.roll(row, 1, 1))
    return pair + jnp.where(lane % 4 < 2, pltpu.roll(pair, CH - 2, 1), pltpu.roll(pair, 2, 1))


def fold_rows(cells):
    return jnp.sum(cells.reshape(-1, 8, CH), axis=0)


def total_row(partial):
    return jnp.sum(partial, axis=0, keepdims=True)


def tile_of(first, second):
    place = lax.broadcasted_iota(jnp.int32, (8, CH), 0)
    return jnp.where(place == 0, first, jnp.where(place == 1, second, 0.0))


def sigmoid(value):
    return 1.0 / (1.0 + jnp.exp(-value))


def body(
    sizes,
    xl, cl, w1, w2, scale_ref, gain1_ref, shift1_ref, gain2_ref, shift2_ref,
    out_ref, o1_ref, o2_ref,
    xr, cr, xe, ce, xeb, ceb, xex, cex, s1, sc, sh, hid, g2, g1, nrm, act_t, hg_t, hg, eh, heb,
    wf1, wb1, wb2, pre1, s_out, s_in, rb1, rb2, a, r0, b1, r1, b2, r2, r3, g3,
    in_send, in_recv, in_local, red_send, red_recv, halo_send, halo_recv, back_send, back_recv, back_local,
    ar_send, ar_recv,
):
    nz, nh, nx, ny = sizes
    ns = nx
    fl, rl, cols = xl.shape[0], xl.shape[1], xl.shape[2]
    strip = cols // nz
    frames = fl * nz
    cells = rl * strip
    z, h, w = lax.axis_index("tm"), lax.axis_index("height"), lax.axis_index("width")
    hx, hy = h // ny, h % ny

    def dev(dz, dh, dw):
        return (lax.rem(z + dz + nz, nz), lax.rem(h + dh + nh, nh), lax.rem(w + dw, 2))

    barrier = pltpu.get_barrier_semaphore()
    partners = [(dz, dh, dw) for dz in range(nz) for dh in (-1, 0, 1) for dw in range(2) if (dz, dh, dw) != (0, 0, 0)]
    partners += [(0, dh, 0) for dh in range(2, nh - 1)]
    for offset in partners:
        pl.semaphore_signal(barrier, inc=1, device_id=dev(*offset), device_id_type=MESH)
    pl.semaphore_wait(barrier, len(partners))

    def remote(src, dst, send, recv, where):
        return pltpu.make_async_remote_copy(
            src_ref=src, dst_ref=dst, send_sem=send, recv_sem=recv, device_id=where, device_id_type=MESH
        )

    own_frames = pl.ds(z * fl, fl)
    row_parts = {0: ((0, rl), (1, rl)), 1: ((rl - 1, 1), (0, 1)), -1: ((0, 1), (rl + 1, 1))}

    def main_copies(k, src, dst):
        copies = []
        for dz in range(nz):
            q = lax.rem(z + dz, nz)
            for n, dh in enumerate((0, 1, -1)):
                (r_from, count), (r_to, _) = row_parts[dh]
                source = src.at[:, pl.ds(r_from, count), pl.ds(pl.multiple_of(q * strip, strip), strip), :]
                target = dst.at[own_frames, pl.ds(r_to, count)]
                if dz == 0 and dh == 0:
                    copies.append(pltpu.make_async_copy(source, target, in_local.at[k, 0]))
                else:
                    place = dz * 3 + n
                    copies.append(
                        remote(source, target, in_send.at[k, place], in_recv.at[k, place], dev(dz, dh, 0))
                    )
        return copies

    def build_edges(src, edges):
        def at(f, r, col):
            start = (col // 16) * 16
            return src[f, r, start : start + 16, :].astype(F32)[col % 16 : col % 16 + 1]

        place = lax.broadcasted_iota(jnp.int32, (16, CH), 0)
        for f in range(fl):
            for q in range(nz):
                tile = jnp.zeros((16, CH), F32)
                for r in range(rl):
                    if q > 0:
                        tile = jnp.where(place == 2 * r, at(f, r, q * strip - 1), tile)
                    if q < nz - 1:
                        tile = jnp.where(place == 2 * r + 1, at(f, r, (q + 1) * strip), tile)
                edges[q, f] = tile.astype(BF16)
            tile = jnp.zeros((16, CH), F32)
            for r in range(rl):
                outer = jnp.where(w == 0, at(f, r, cols - 1), at(f, r, 0))
                tile = jnp.where(place // 2 == r, outer, tile)
            edges[nz, f] = tile.astype(BF16)

    def edge_copies(k, edges, landing, landing_out):
        copies = []
        base = 3 * nz
        for dz in range(nz):
            q = lax.rem(z + dz, nz)
            for n, dh in enumerate((0, 1, -1)):
                source = edges.at[q]
                target = landing.at[1 - dh, own_frames]
                place = base + dz * 3 + n
                if dz == 0 and dh == 0:
                    copies.append(pltpu.make_async_copy(source, target, in_local.at[k, 1]))
                else:
                    copies.append(
                        remote(source, target, in_send.at[k, place], in_recv.at[k, place], dev(dz, dh, 0))
                    )
        return copies

    outer_q = (nz - 1) * w
    takes_outer = z == (nz - 1) * (1 - w)

    def outer_sends(k, edges, landing_out):
        copies = []
        base = 6 * nz
        for n, dh in enumerate((0, 1, -1)):
            where = (outer_q, lax.rem(h + dh + nh, nh), 1 - w)
            copies.append(
                remote(
                    edges.at[nz], landing_out.at[1 - dh, own_frames],
                    in_send.at[k, base + n], in_recv.at[k, base + 3 * z + n], where,
                )
            )
        return copies

    def outer_waits(k, edges, landing_out):
        for zs in range(nz):
            for n, dh in enumerate((0, 1, -1)):
                remote(
                    edges.at[nz], landing_out.at[1 - dh, pl.ds(zs * fl, fl)],
                    in_send.at[k, 6 * nz + n], in_recv.at[k, 6 * nz + 3 * zs + n], dev(0, 0, 1),
                ).wait_recv()

    def wait_copies(copies):
        for copy in copies:
            copy.wait()

    x_main = main_copies(0, xl, xr)
    for copy in x_main:
        copy.start()
    build_edges(xl, xe)
    x_edge = edge_copies(0, xe, xeb, xex)
    x_outer = outer_sends(0, xe, xex)
    for copy in x_edge + x_outer:
        copy.start()
    c_main = main_copies(1, cl, cr)
    for copy in c_main:
        copy.start()

    me8 = z * 2 + w

    def red1_copies(k):
        copies = []
        for n, (dz, dw) in enumerate([(dz, dw) for dz in range(nz) for dw in range(2) if (dz, dw) != (0, 0)]):
            slot = rb1.at[k, me8]
            copies.append(remote(slot, slot, red_send.at[k, n], red_recv.at[k, n], dev(dz, 0, dw)))
        return copies

    def red2_copies(k):
        copies = []
        for dh in range(1, nh):
            slot = rb2.at[k, h]
            n = 2 * nz + dh
            copies.append(remote(slot, slot, red_send.at[k, n], red_recv.at[k, n], dev(0, dh, 0)))
        return copies

    def start_all(copies):
        for copy in copies:
            copy.start()

    def red1_start(k, tile):
        rb1[k, me8] = tile
        start_all(red1_copies(k))

    def red2_start(k, tile):
        rb2[k, h] = tile
        start_all(red2_copies(k))

    def moments(buffer, k, count, size):
        mean = jnp.sum(buffer[k, :, 0:1, :], axis=0) / count
        spread = jnp.zeros((1, CH), F32)
        for n in range(count):
            off = buffer[k, n, 0:1, :] - mean
            spread = spread + (buffer[k, n, 1:2, :] + size * off * off)
        return mean, spread

    def plain_sums(buffer, k):
        return jnp.sum(buffer[k], axis=0)

    local_size = 4.0 * fl * rl * cols
    total_size = local_size * 2 * nz * nh

    def moments_mid(k):
        wait_copies(red1_copies(k))
        mean, spread = moments(rb1, k, 2 * nz, local_size)
        red2_start(k, tile_of(mean, spread))

    def moments_end(k):
        wait_copies(red2_copies(k))
        return moments(rb2, k, nh, local_size * 2 * nz)

    def sums_mid(k):
        wait_copies(red1_copies(k))
        red2_start(k, plain_sums(rb1, k))

    def sums_end(k):
        wait_copies(red2_copies(k))
        sums = plain_sums(rb2, k) / total_size
        return sums[0:1], sums[1:2]

    zero8 = jnp.zeros((8, CH), F32)

    def x_sum(n, total):
        return total + fold_rows(xl[n // rl, n % rl].astype(F32))

    local_mean = group_sum(total_row(lax.fori_loop(0, fl * rl, x_sum, zero8))) / local_size

    def x_spread(n, total):
        off = xl[n // rl, n % rl].astype(F32) - local_mean
        return total + fold_rows(off * off)

    local_spread = group_sum(total_row(lax.fori_loop(0, fl * rl, x_spread, zero8)))
    red1_start(0, tile_of(local_mean, local_spread))

    build_edges(cl, ce)
    c_edge = edge_copies(1, ce, ceb, cex)
    c_outer = outer_sends(1, ce, cex)
    start_all(c_edge + c_outer)

    for kt in range(3):
        for kr in range(3):
            for kc in range(3):
                tap = 9 * kt + 3 * kr + kc
                back = ((2 - kr) * 3 + (2 - kc)) * CH
                for source, target in ((w1, wb1), (w2, wb2)):
                    target[back : back + CH, kt * CH : (kt + 1) * CH] = source[:, tap * CH : (tap + 1) * CH]
    moments_mid(0)
    for kt in range(3):
        for kr in range(3):
            for kc in range(3):
                tap = 9 * kt + 3 * kr + kc
                ahead = (kr * 3 + kc) * CH
                block = w1[:, tap * CH : (tap + 1) * CH].astype(F32)
                wf1[ahead : ahead + CH, (2 - kt) * CH : (3 - kt) * CH] = jnp.transpose(block).astype(BF16)
    zero_cells = jnp.zeros((cells, CH), F32)

    def clear(n, _):
        hid[n] = zero_cells
        g2[n] = zero_cells
        g1[n] = zero_cells
        return 0

    lax.fori_loop(0, frames + 2, clear, 0)
    zero_t = jnp.zeros((2 * CH, cells), BF16)
    act_t[0 : 2 * CH] = zero_t
    hg_t[frames * CH : (frames + 2) * CH] = zero_t

    row_place = lax.broadcasted_iota(jnp.int32, (strip, CH), 0)
    left_ok = jnp.logical_not(jnp.logical_and(w == 0, z == 0))
    right_ok = jnp.logical_not(jnp.logical_and(w == 1, z == nz - 1))

    def row_ok(r):
        if r == 0:
            return h > 0
        if r == rl + 1:
            return h < nh - 1
        return None

    def row_source(r):
        if r == 0:
            return 0, rl - 1
        if r == rl + 1:
            return 2, 0
        return 1, r - 1

    def store_stack(stack, f, r, value, left, right):
        ok = row_ok(r)
        left = jnp.where(left_ok if ok is None else jnp.logical_and(left_ok, ok), left, 0.0)
        right = jnp.where(right_ok if ok is None else jnp.logical_and(right_ok, ok), right, 0.0)
        if ok is not None:
            value = jnp.where(ok, value, 0.0)
        before = jnp.where(row_place == 0, left, pltpu.roll(value, 1, 0))
        after = jnp.where(row_place == strip - 1, right, pltpu.roll(value, strip - 1, 0))
        stack[f, r, :, 0:CH] = before.astype(BF16)
        stack[f, r, :, CH : 2 * CH] = value.astype(BF16)
        stack[f, r, :, 2 * CH : 3 * CH] = after.astype(BF16)

    edge_place = lax.broadcasted_iota(jnp.int32, (16, CH), 0)
    outer_mask = jnp.logical_and(takes_outer, edge_place % 2 == 1 - w)

    def input_stack(stack, source, landing, landing_out, apply):
        def step(f, _):
            edges = []
            for d in range(3):
                tile = jnp.where(outer_mask, landing_out[d, f].astype(F32), landing[d, f].astype(F32))
                edges.append(apply(tile))
            for r in range(rl + 2):
                d, row = row_source(r)
                tile = edges[d]
                store_stack(
                    stack, f, r, apply(source[f, r].astype(F32)),
                    tile[2 * row : 2 * row + 1], tile[2 * row + 1 : 2 * row + 2],
                )
            return 0

        lax.fori_loop(0, frames, step, 0)

    def window(stack, f):
        return [stack[f, kr : kr + rl].reshape(cells, 3 * CH) for kr in range(3)]

    def convolve(stack, weight, target):
        def step(f, _):
            product = jnp.dot(
                jnp.concatenate(window(stack, f), axis=1), weight[...], preferred_element_type=F32
            )
            for j in range(3):
                target[f + j] += product[:, j * CH : (j + 1) * CH]
            return 0

        lax.fori_loop(0, frames, step, 0)

    def weight_part(turned, stack, kr):
        left = jnp.concatenate([turned[f * CH : (f + 3) * CH, :] for f in range(frames)], axis=1)
        right = stack[:, kr : kr + rl].reshape(frames * cells, 3 * CH)
        return jnp.dot(left, right, preferred_element_type=F32)

    def peer(axis, j):
        if axis == "z":
            return dev(j, 0, 0)
        if axis == "x":
            return (z, lax.rem(hx + j, nx) * ny + hy, w)
        return (z, hx * ny + lax.rem(hy + j, ny), w)

    coords = {"z": z, "x": hx, "y": hy}
    orders = (("z", "y", "x"), ("y", "x", "z"), ("x", "z", "y"))
    half = 8
    span = half // ns
    tiles = span * 9
    piece = -(-tiles // ns)
    outs = (o1_ref, o2_ref)
    step_at = {"core": 0, "a1": 1, "a2": 1 + (ns - 1), "a3": 1 + 2 * (ns - 1), "g2": 1 + 3 * (ns - 1),
               "g1": 1 + 4 * (ns - 1), "gc": 1 + 5 * (ns - 1)}

    def sems(g, p, stage, n):
        return ar_send.at[g, p, step_at[stage] + n], ar_recv.at[g, p, step_at[stage] + n]

    def core_copy(g, p):
        return remote(a.at[g, p, pl.ds((1 - w) * half, half)], r0.at[g, p], *sems(g, p, "core", 0), dev(0, 0, 1))

    def core_start(g, p):
        core_copy(g, p).start()

    def a1_copies(g, p):
        axis = orders[p][0]
        return [
            remote(
                b1.at[g, p, pl.ds(lax.rem(coords[axis] + j, ns) * span, span)], r1.at[g, p, j - 1],
                *sems(g, p, "a1", j - 1), peer(axis, j),
            )
            for j in range(1, ns)
        ]

    def a1_start(g, p):
        core_copy(g, p).wait()
        b1[g, p] = a[g, p, pl.ds(w * half, half)] + r0[g, p]
        start_all(a1_copies(g, p))

    def a2_copies(g, p):
        axis = orders[p][1]
        return [
            remote(
                b2.at[g, p, pl.ds(lax.rem(coords[axis] + j, ns) * piece, piece)], r2.at[g, p, j - 1],
                *sems(g, p, "a2", j - 1), peer(axis, j),
            )
            for j in range(1, ns)
        ]

    def a2_start(g, p):
        wait_copies(a1_copies(g, p))
        value = b1[g, p, pl.ds(coords[orders[p][0]] * span, span)]
        for j in range(ns - 1):
            value = value + r1[g, p, j]
        b2[g, p, 0:tiles] = value.reshape(tiles, 8, CH)
        if piece * ns > tiles:
            b2[g, p, tiles:] = jnp.zeros((piece * ns - tiles, 8, CH), F32)
        start_all(a2_copies(g, p))

    def a3_copies(g, p):
        axis = orders[p][2]
        slot = r3.at[g, p, coords[axis]]
        return [remote(slot, slot, *sems(g, p, "a3", j - 1), peer(axis, j)) for j in range(1, ns)]

    def a3_start(g, p):
        wait_copies(a2_copies(g, p))
        value = b2[g, p, pl.ds(coords[orders[p][1]] * piece, piece)]
        for j in range(ns - 1):
            value = value + r2[g, p, j]
        r3[g, p, coords[orders[p][2]]] = value
        start_all(a3_copies(g, p))

    def g2_copies(g, p):
        axis = orders[p][1]
        part = g3.at[g, p, pl.ds(coords[axis] * piece, piece)]
        return [remote(part, part, *sems(g, p, "g2", j - 1), peer(axis, j)) for j in range(1, ns)]

    def g2_start(g, p):
        wait_copies(a3_copies(g, p))
        value = r3[g, p, 0]
        for n in range(1, ns):
            value = value + r3[g, p, n]
        g3[g, p, pl.ds(coords[orders[p][1]] * piece, piece)] = value
        start_all(g2_copies(g, p))

    def out_span(g, p, n):
        return outs[g].at[p, pl.ds(w * half + n * span, span)]

    def g1_copies(g, p):
        axis = orders[p][0]
        part = out_span(g, p, coords[axis])
        return [remote(part, part, *sems(g, p, "g1", j - 1), peer(axis, j)) for j in range(1, ns)]

    def gc_copy(g, p, j):
        part = out_span(g, p, lax.rem(coords[orders[p][0]] + ns - j, ns))
        return remote(part, part, *sems(g, p, "gc", j), dev(0, 0, 1))

    def g1_start(g, p):
        wait_copies(g2_copies(g, p))
        outs[g][p, pl.ds(w * half + coords[orders[p][0]] * span, span)] = g3[g, p, 0:tiles].reshape(span, 9, 8, CH)
        start_all(g1_copies(g, p))
        gc_copy(g, p, 0).start()

    def gc_start(g, p):
        for j, copy in enumerate(g1_copies(g, p)):
            copy.wait()
            gc_copy(g, p, j + 1).start()

    def gc_end(g, p):
        for j in range(ns):
            gc_copy(g, p, j).wait()

    def each(stage, g):
        for p in range(3):
            stage(g, p)

    mean1, spread1 = moments_end(0)
    scale = scale_ref[...]
    inv1 = 1.0 / jnp.sqrt(spread1 * (scale * scale) / total_size + EPS)
    factor1 = scale * inv1
    gain1, shift1 = gain1_ref[...], shift1_ref[...]
    gain2, shift2 = gain2_ref[...], shift2_ref[...]

    def rounded(value):
        return value.astype(BF16).astype(F32)

    def act_first(value):
        pre = (value - mean1) * factor1 * gain1 + shift1
        return rounded(pre * sigmoid(pre))

    wait_copies(x_main + x_edge)
    for copy in x_outer:
        copy.wait_send()

    @pl.when(takes_outer)
    def _():
        outer_waits(0, xe, xex)

    input_stack(s1, xr, xeb, xex, act_first)
    convolve(s1, wf1, hid)

    def hid_sum(n, total):
        return total + fold_rows(hid[n])

    mean_l = group_sum(total_row(lax.fori_loop(0, frames, hid_sum, zero8))) / local_size

    def hid_spread(n, total):
        off = hid[n] - mean_l
        return total + fold_rows(off * off)

    red1_start(1, tile_of(mean_l, group_sum(total_row(lax.fori_loop(0, frames, hid_spread, zero8)))))

    wait_copies(c_main + c_edge)
    for copy in c_outer:
        copy.wait_send()

    @pl.when(takes_outer)
    def _():
        outer_waits(1, ce, cex)

    input_stack(sc, cr, ceb, cex, lambda value: value)
    moments_mid(1)
    convolve(sc, wb2, g2)
    mean2, spread2 = moments_end(1)
    inv2 = 1.0 / jnp.sqrt(spread2 / total_size + EPS)

    def second(n, totals):
        first_total, second_total = totals
        normed = (hid[n] - mean2) * inv2
        pre = normed * gain2 + shift2
        sig = sigmoid(pre)
        act_t[pl.ds(pl.multiple_of((n + 2) * CH, CH), CH), :] = jnp.transpose(pre * sig).astype(BF16)
        scaled = g2[n + 2] * (sig * (1.0 + pre * (1.0 - sig))) * gain2
        nrm[n] = normed
        g2[n + 2] = scaled
        return first_total + fold_rows(scaled), second_total + fold_rows(scaled * normed)

    t1, t2 = lax.fori_loop(0, frames, second, (zero8, zero8))
    red1_start(2, tile_of(group_sum(total_row(t1)), group_sum(total_row(t2))))

    def put_second(kr):
        block = weight_part(act_t, sc, kr)
        for kt in range(3):
            for kc in range(3):
                part = block[kt * CH : (kt + 1) * CH, kc * CH : (kc + 1) * CH]
                a[1, 2 - kr, :, kt * 3 + (2 - kc)] = part.reshape(16, 8, CH)
        core_start(1, 2 - kr)

    put_second(0)
    sums_mid(2)
    put_second(1)
    put_second(2)
    m1, m2 = sums_end(2)

    def hidden(n, _):
        value = inv2 * (g2[n + 2] - m1 - nrm[n] * m2)
        hg_t[pl.ds(pl.multiple_of(n * CH, CH), CH), :] = jnp.transpose(value).astype(BF16)
        narrow = value.astype(BF16)
        hg[n, 1 : rl + 1] = narrow.reshape(rl, strip, CH)
        wide = narrow.astype(F32).reshape(rl, strip, CH)
        lefts = jnp.zeros((16, CH), F32)
        rights = jnp.zeros((16, CH), F32)
        for r in range(rl):
            lefts = jnp.where(edge_place == r, wide[r, 0:1], lefts)
            rights = jnp.where(edge_place == r, wide[r, strip - 1 : strip], rights)
        eh[0, n] = lefts.astype(BF16)
        eh[1, n] = rights.astype(BF16)
        return 0

    lax.fori_loop(0, frames, hidden, 0)

    line = w * nz + z

    def beside(ds, dh):
        place = lax.rem(line + ds + 2 * nz, 2 * nz)
        return (lax.rem(place, nz), lax.rem(h + dh + nh, nh), place // nz)

    halo = [
        remote(hg.at[:, pl.ds(rl, 1)], hg.at[:, pl.ds(0, 1)], halo_send.at[0], halo_recv.at[0], dev(0, 1, 0)),
        remote(hg.at[:, pl.ds(1, 1)], hg.at[:, pl.ds(rl + 1, 1)], halo_send.at[1], halo_recv.at[1], dev(0, -1, 0)),
    ]
    for n, dh in enumerate((0, 1, -1)):
        halo.append(remote(eh.at[0], heb.at[1 - dh, 1], halo_send.at[2 + n], halo_recv.at[2 + n], beside(-1, dh)))
        halo.append(remote(eh.at[1], heb.at[1 - dh, 0], halo_send.at[5 + n], halo_recv.at[5 + n], beside(1, dh)))
    start_all(halo)
    each(a1_start, 1)

    def put_first(kr):
        block = weight_part(hg_t, s1, kr)
        for j in range(3):
            for kc in range(3):
                part = block[j * CH : (j + 1) * CH, kc * CH : (kc + 1) * CH]
                a[0, kr, :, (2 - j) * 3 + kc] = part.reshape(16, 8, CH)
        core_start(0, kr)

    for kr in range(3):
        put_first(kr)
    wait_copies(halo)

    def halo_stack(f, _):
        lefts = [heb[d, 0, f].astype(F32) for d in range(3)]
        rights = [heb[d, 1, f].astype(F32) for d in range(3)]
        for r in range(rl + 2):
            d, row = row_source(r)
            store_stack(sh, f, r, hg[f, r].astype(F32), lefts[d][row : row + 1], rights[d][row : row + 1])
        return 0

    lax.fori_loop(0, frames, halo_stack, 0)
    each(a2_start, 1)
    each(a1_start, 0)
    convolve(sh, wb1, g1)
    each(a3_start, 1)
    each(a2_start, 0)

    def first(f, totals):
        first_total, second_total = totals
        for r in range(rl):
            normed = (xr[f, r + 1].astype(F32) - mean1) * factor1
            pre = normed * gain1 + shift1
            sig = sigmoid(pre)
            scaled = g1[f + 2, r * strip : (r + 1) * strip] * (sig * (1.0 + pre * (1.0 - sig))) * gain1
            s_out[f, r] = scaled.astype(BF16)
            first_total = first_total + fold_rows(scaled)
            second_total = second_total + fold_rows(scaled * normed)
        return first_total, second_total

    t1, t2 = lax.fori_loop(0, frames, first, (zero8, zero8))
    red1_start(3, tile_of(group_sum(total_row(t1)), group_sum(total_row(t2))))

    back_copies = []
    for dz in range(nz):
        q = lax.rem(z + dz, nz)
        source = s_out.at[pl.ds(q * fl, fl)]
        target = s_in.at[:, :, pl.ds(pl.multiple_of(z * strip, strip), strip), :]
        if dz == 0:
            back_copies.append(pltpu.make_async_copy(source, target, back_local.at[0]))
        else:
            back_copies.append(remote(source, target, back_send.at[dz], back_recv.at[dz], dev(dz, 0, 0)))
    start_all(back_copies)
    each(g2_start, 1)
    each(a3_start, 0)
    sums_mid(3)
    each(g1_start, 1)
    each(g2_start, 0)
    m1, m2 = sums_end(3)
    wait_copies(back_copies)
    each(g1_start, 0)

    def last(n, _):
        f, r = n // rl, n % rl
        normed = (xl[f, r].astype(F32) - mean1) * factor1
        out_ref[f, r] = cl[f, r].astype(F32) + inv1 * (s_in[f, r].astype(F32) - m1 - normed * m2)
        return 0

    lax.fori_loop(0, fl * rl, last, 0)
    each(gc_start, 1)
    each(gc_start, 0)
    each(gc_end, 1)
    each(gc_end, 0)


def shards(sizes, latent, exponents, cotangent, conv_first, conv_second, gain_first, shift_first, gain_second, shift_second):
    nz, nh, nx, ny = sizes
    channels, fl, rl, cols = latent.shape
    strip = cols // nz
    frames = fl * nz
    cells = rl * strip
    ns = nx
    span = 8 // ns
    tiles = span * 9
    piece = -(-tiles // ns)
    scale = jnp.repeat(jnp.exp2(exponents.astype(F32)), channels // exponents.shape[0])[None]
    xl = jnp.transpose(latent, (1, 2, 3, 0))
    cl = jnp.transpose(cotangent, (1, 2, 3, 0))
    vmem = pl.BlockSpec(memory_space=pltpu.VMEM)
    n_ar = 1 + 5 * (ns - 1) + ns
    n_in = 6 * nz + 3 * nz
    wide = (frames, rl + 2, strip, 3 * CH)
    scratch = [
        pltpu.VMEM((frames, rl + 2, strip, CH), BF16),
        pltpu.VMEM((frames, rl + 2, strip, CH), BF16),
        pltpu.VMEM((nz + 1, fl, 16, CH), BF16),
        pltpu.VMEM((nz + 1, fl, 16, CH), BF16),
        pltpu.VMEM((3, frames, 16, CH), BF16),
        pltpu.VMEM((3, frames, 16, CH), BF16),
        pltpu.VMEM((3, frames, 16, CH), BF16),
        pltpu.VMEM((3, frames, 16, CH), BF16),
        pltpu.VMEM(wide, BF16),
        pltpu.VMEM(wide, BF16),
        pltpu.VMEM(wide, BF16),
        pltpu.VMEM((frames + 2, cells, CH), F32),
        pltpu.VMEM((frames + 2, cells, CH), F32),
        pltpu.VMEM((frames + 2, cells, CH), F32),
        pltpu.VMEM((frames, cells, CH), F32),
        pltpu.VMEM(((frames + 2) * CH, cells), BF16),
        pltpu.VMEM(((frames + 2) * CH, cells), BF16),
        pltpu.VMEM((frames, rl + 2, strip, CH), BF16),
        pltpu.VMEM((2, frames, 16, CH), BF16),
        pltpu.VMEM((3, 2, frames, 16, CH), BF16),
        pltpu.VMEM((9 * CH, 3 * CH), BF16),
        pltpu.VMEM((9 * CH, 3 * CH), BF16),
        pltpu.VMEM((9 * CH, 3 * CH), BF16),
        pltpu.VMEM((8, CH), F32),
        pltpu.VMEM((frames, rl, strip, CH), BF16),
        pltpu.VMEM((fl, rl, cols, CH), BF16),
        pltpu.VMEM((4, 2 * nz, 8, CH), F32),
        pltpu.VMEM((4, nh, 8, CH), F32),
        pltpu.VMEM((2, 3, 16, 9, 8, CH), F32),
        pltpu.VMEM((2, 3, 8, 9, 8, CH), F32),
        pltpu.VMEM((2, 3, 8, 9, 8, CH), F32),
        pltpu.VMEM((2, 3, ns - 1, span, 9, 8, CH), F32),
        pltpu.VMEM((2, 3, piece * ns, 8, CH), F32),
        pltpu.VMEM((2, 3, ns - 1, piece, 8, CH), F32),
        pltpu.VMEM((2, 3, ns, piece, 8, CH), F32),
        pltpu.VMEM((2, 3, piece * ns, 8, CH), F32),
        pltpu.SemaphoreType.DMA((2, n_in)),
        pltpu.SemaphoreType.DMA((2, n_in)),
        pltpu.SemaphoreType.DMA((2, 2)),
        pltpu.SemaphoreType.DMA((4, 2 * nz + nh)),
        pltpu.SemaphoreType.DMA((4, 2 * nz + nh)),
        pltpu.SemaphoreType.DMA((8,)),
        pltpu.SemaphoreType.DMA((8,)),
        pltpu.SemaphoreType.DMA((nz,)),
        pltpu.SemaphoreType.DMA((nz,)),
        pltpu.SemaphoreType.DMA((1,)),
        pltpu.SemaphoreType.DMA((2, 3, n_ar)),
        pltpu.SemaphoreType.DMA((2, 3, n_ar)),
    ]
    grad, first, second = pl.pallas_call(
        functools.partial(body, sizes),
        out_shape=(
            jax.ShapeDtypeStruct((fl, rl, cols, CH), F32),
            jax.ShapeDtypeStruct((3, 16, 9, 8, CH), F32),
            jax.ShapeDtypeStruct((3, 16, 9, 8, CH), F32),
        ),
        in_specs=[vmem] * 9,
        out_specs=(vmem, vmem, vmem),
        scratch_shapes=scratch,
        compiler_params=pltpu.CompilerParams(
            collective_id=0, has_side_effects=True, vmem_limit_bytes=60 * 1024 * 1024
        ),
    )(
        xl, cl, conv_first, conv_second, scale,
        gain_first[None], shift_first[None], gain_second[None], shift_second[None],
    )
    first = first.reshape(3, 16, 3, 3, 8, CH).transpose(1, 4, 2, 0, 3, 5).reshape(CH, 27 * CH)
    second = second.reshape(3, 16, 3, 3, 8, CH).transpose(5, 2, 0, 3, 1, 4).reshape(CH, 27 * CH)
    return jnp.transpose(grad, (3, 0, 1, 2)), first, second


def solution(mesh):
    nz, nh = mesh.shape["tm"], mesh.shape["height"]
    nx = int(round(nh**0.5))
    placed = P(None, "tm", "height", "width")
    return jax.shard_map(
        functools.partial(shards, (nz, nh, nx, nh // nx)),
        mesh=mesh,
        in_specs=(placed, P(), placed, P(), P(), P(), P(), P(), P()),
        out_specs=(placed, P(), P()),
        check_vma=False,
    )
```

```python
import functools

import jax
import jax.numpy as jnp
from jax import lax
from jax.experimental import pallas as pl
from jax.experimental.pallas import tpu as pltpu
from jax.sharding import PartitionSpec as P

MESH = pl.DeviceIdType.MESH
EPS = 1e-05
CH = 128
F32 = jnp.float32
BF16 = jnp.bfloat16


def group_sum(row):
    lane = lax.broadcasted_iota(jnp.int32, row.shape, 1)
    pair = row + jnp.where(lane % 2 == 0, pltpu.roll(row, CH - 1, 1), pltpu.roll(row, 1, 1))
    return pair + jnp.where(lane % 4 < 2, pltpu.roll(pair, CH - 2, 1), pltpu.roll(pair, 2, 1))


def fold_rows(cells):
    return jnp.sum(cells.reshape(-1, 8, CH), axis=0)


def total_row(partial):
    return jnp.sum(partial, axis=0, keepdims=True)


def lanes_low(row):
    return lax.broadcasted_iota(jnp.int32, row.shape, row.ndim - 1) % 4 < 2


def pack_pair(first, second):
    return jnp.where(lanes_low(first), first, second)


def unpack_pair(row):
    low = lanes_low(row)
    return jnp.where(low, row, pltpu.roll(row, 2, 1)), jnp.where(low, pltpu.roll(row, CH - 2, 1), row)


def far_first(n, size):
    if size == 4:
        return (2 + 3 * n + 3 * ((n * (n - 1)) // 2)) % 4
    return size - 1 - n


def sigmoid(value):
    return 1.0 / (1.0 + jnp.exp(-value))


def body(
    sizes,
    xl, cl_hbm, w1_hbm, w2_hbm, exponent_ref, gain1_ref, shift1_ref, gain2_ref, shift2_ref,
    out_hbm, o1_hbm, o2_hbm,
    cl, w1, w2, out_ref, o1_ref, o2_ref,
    xr, cr, xe, ce, xeb, ceb, xex, cex, s1, sc, sh, hid, g2, g1, nrm, act_t, hg_t, hg, eh, heb,
    wf1, wb1, wb2, s_out, s_in, rb, a, r0, b1, r1, b2, r2, r3, g3,
    load_sem, store_sem, in_send, in_recv, red_send, red_recv, halo_send, halo_recv, back_send, back_recv,
    ar_send, ar_recv,
):
    nz, nh, nx, ny = sizes
    ns = nx
    fl, rl, cols = xl.shape[0], xl.shape[1], xl.shape[2]
    strip = cols // nz
    frames = fl * nz
    cells = rl * strip
    z, h, w = lax.axis_index("tm"), lax.axis_index("height"), lax.axis_index("width")
    hx, hy = h // ny, h % ny

    def dev(dz, dh, dw):
        return (lax.rem(z + dz + nz, nz), lax.rem(h + dh + nh, nh), lax.rem(w + dw, 2))

    loads = [
        pltpu.make_async_copy(source, target, load_sem.at[n])
        for n, (source, target) in enumerate(((cl_hbm, cl), (w1_hbm, w1), (w2_hbm, w2)))
    ]
    for copy in loads:
        copy.start()

    heights = [(ox, oy) for ox in range(nx) for oy in range(ny)]
    heights.sort(key=lambda place: -(min(place[0], nx - place[0]) + min(place[1], ny - place[1])))
    targets_h = [lax.rem(hx + ox, nx) * ny + lax.rem(hy + oy, ny) for ox, oy in heights]

    def for_each_device(act):
        def step(n, _):
            dz, dw = far_first(n // 2, nz), 1 - n % 2
            zt, wt = lax.rem(z + dz, nz), lax.rem(w + dw, 2)
            for ht in targets_h[:-1]:
                act((zt, ht, wt))

            @pl.when(n < 2 * nz - 1)
            def _():
                act((zt, h, wt))

            return 0

        lax.fori_loop(0, 2 * nz, step, 0)

    devices = 2 * nz * nh
    barrier = pltpu.get_barrier_semaphore()
    for_each_device(
        lambda where: pl.semaphore_signal(barrier, inc=1, device_id=where, device_id_type=MESH)
    )
    pl.semaphore_wait(barrier, devices - 1)

    def take(ref, sem):
        pltpu.make_async_copy(ref, ref, sem).wait()

    def remote(src, dst, send, recv, where):
        return pltpu.make_async_remote_copy(
            src_ref=src, dst_ref=dst, send_sem=send, recv_sem=recv, device_id=where, device_id_type=MESH
        )

    own_frames = pl.ds(z * fl, fl)
    row_parts = {0: ((0, rl), (1, rl)), 1: ((rl - 1, 1), (0, 1)), -1: ((0, 1), (rl + 1, 1))}

    def main_copies(k, src, dst):
        copies = []
        for dz in range(nz):
            q = lax.rem(z + dz, nz)
            for n, dh in enumerate((0, 1, -1)):
                (r_from, count), (r_to, _) = row_parts[dh]
                source = src.at[:, pl.ds(r_from, count), pl.ds(pl.multiple_of(q * strip, strip), strip), :]
                target = dst.at[own_frames, pl.ds(r_to, count)]
                if dz == 0 and dh == 0:
                    copies.append(pltpu.make_async_copy(source, target, in_recv.at[k, 0]))
                else:
                    copies.append(remote(source, target, in_send.at[k], in_recv.at[k, 0], dev(dz, dh, 0)))
        return copies

    def build_edges(src, edges):
        def at(f, r, col):
            start = (col // 16) * 16
            return src[f, r, start : start + 16, :].astype(F32)[col % 16 : col % 16 + 1]

        place = lax.broadcasted_iota(jnp.int32, (16, CH), 0)
        for f in range(fl):
            for q in range(nz):
                tile = jnp.zeros((16, CH), F32)
                for r in range(rl):
                    if q > 0:
                        tile = jnp.where(place == 2 * r, at(f, r, q * strip - 1), tile)
                    if q < nz - 1:
                        tile = jnp.where(place == 2 * r + 1, at(f, r, (q + 1) * strip), tile)
                edges[q, f] = tile.astype(BF16)
            tile = jnp.zeros((16, CH), F32)
            for r in range(rl):
                outer = jnp.where(w == 0, at(f, r, cols - 1), at(f, r, 0))
                tile = jnp.where(place // 2 == r, outer, tile)
            edges[nz, f] = tile.astype(BF16)

    def edge_copies(k, edges, landing, landing_out):
        copies = []
        for dz in range(nz):
            q = lax.rem(z + dz, nz)
            for n, dh in enumerate((0, 1, -1)):
                source = edges.at[q]
                target = landing.at[1 - dh, own_frames]
                if dz == 0 and dh == 0:
                    copies.append(pltpu.make_async_copy(source, target, in_recv.at[k, 1]))
                else:
                    copies.append(remote(source, target, in_send.at[k], in_recv.at[k, 1], dev(dz, dh, 0)))
        return copies

    outer_q = (nz - 1) * w
    takes_outer = z == (nz - 1) * (1 - w)

    def outer_sends(k, edges, landing_out):
        copies = []
        for dh in (0, 1, -1):
            where = (outer_q, lax.rem(h + dh + nh, nh), 1 - w)
            copies.append(
                remote(edges.at[nz], landing_out.at[1 - dh, own_frames], in_send.at[k], in_recv.at[k, 2], where)
            )
        return copies

    def wait_inputs(k, cells_in, landing, landing_out):
        take(cells_in, in_recv.at[k, 0])
        take(landing, in_recv.at[k, 1])

        @pl.when(takes_outer)
        def _():
            take(landing_out, in_recv.at[k, 2])

    def start_all(copies):
        for copy in copies:
            copy.start()

    def wait_sends(copies):
        for copy in copies:
            copy.wait_send()

    x_main = main_copies(0, xl, xr)
    start_all(x_main)
    build_edges(xl, xe)
    x_edge = edge_copies(0, xe, xeb, xex)
    x_outer = outer_sends(0, xe, xex)
    start_all(x_edge + x_outer)
    loads[0].wait()
    c_main = main_copies(1, cl, cr)
    start_all(c_main)

    me = (z * nh + h) * 2 + w
    local_size = 4.0 * fl * rl * cols
    total_size = local_size * devices

    def red_start(k, first, second):
        rb[k, me] = pack_pair(first, second)
        slot = rb.at[k, me]
        for_each_device(lambda where: remote(slot, slot, red_send.at[k], red_recv.at[k], where).start())

    def red_wait(k):
        take(rb.at[k, pl.ds(0, devices - 1)], red_recv.at[k])

    def moments_end(k):
        red_wait(k)
        rows = rb[k]
        mean, _ = unpack_pair(jnp.sum(rows, axis=0) / devices)
        low = lanes_low(rows)
        off = rows - jnp.where(lanes_low(mean), mean, 0.0)[None]
        between, within = unpack_pair(jnp.sum(jnp.where(low, off * off, off), axis=0))
        return mean, within + local_size * between

    def sums_end(k):
        red_wait(k)
        return unpack_pair(jnp.sum(rb[k], axis=0) / total_size)

    zero8 = jnp.zeros((8, CH), F32)

    def x_sum(n, total):
        return total + fold_rows(xl[n // rl, n % rl].astype(F32))

    local_mean = group_sum(total_row(lax.fori_loop(0, fl * rl, x_sum, zero8))) / local_size

    def x_spread(n, total):
        off = xl[n // rl, n % rl].astype(F32) - local_mean
        return total + fold_rows(off * off)

    local_spread = group_sum(total_row(lax.fori_loop(0, fl * rl, x_spread, zero8)))
    red_start(0, local_mean, local_spread)

    build_edges(cl, ce)
    c_edge = edge_copies(1, ce, ceb, cex)
    c_outer = outer_sends(1, ce, cex)
    start_all(c_edge + c_outer)

    loads[1].wait()
    loads[2].wait()
    for kt in range(3):
        for kr in range(3):
            for kc in range(3):
                tap = 9 * kt + 3 * kr + kc
                back = ((2 - kr) * 3 + (2 - kc)) * CH
                for source, target in ((w1, wb1), (w2, wb2)):
                    target[back : back + CH, kt * CH : (kt + 1) * CH] = source[:, tap * CH : (tap + 1) * CH]
    for kt in range(3):
        for kr in range(3):
            for kc in range(3):
                tap = 9 * kt + 3 * kr + kc
                ahead = (kr * 3 + kc) * CH
                block = w1[:, tap * CH : (tap + 1) * CH].astype(F32)
                wf1[ahead : ahead + CH, (2 - kt) * CH : (3 - kt) * CH] = jnp.transpose(block).astype(BF16)
    zero_cells = jnp.zeros((cells, CH), F32)

    def clear(n, _):
        hid[n] = zero_cells
        g2[n] = zero_cells
        g1[n] = zero_cells
        return 0

    lax.fori_loop(0, frames + 2, clear, 0)
    zero_t = jnp.zeros((2 * CH, cells), BF16)
    act_t[0 : 2 * CH] = zero_t
    hg_t[frames * CH : (frames + 2) * CH] = zero_t

    row_place = lax.broadcasted_iota(jnp.int32, (strip, CH), 0)
    left_ok = jnp.logical_not(jnp.logical_and(w == 0, z == 0))
    right_ok = jnp.logical_not(jnp.logical_and(w == 1, z == nz - 1))

    def row_ok(r):
        if r == 0:
            return h > 0
        if r == rl + 1:
            return h < nh - 1
        return None

    def row_source(r):
        if r == 0:
            return 0, rl - 1
        if r == rl + 1:
            return 2, 0
        return 1, r - 1

    def store_stack(stack, f, r, value, left, right):
        ok = row_ok(r)
        left = jnp.where(left_ok if ok is None else jnp.logical_and(left_ok, ok), left, 0.0)
        right = jnp.where(right_ok if ok is None else jnp.logical_and(right_ok, ok), right, 0.0)
        if ok is not None:
            value = jnp.where(ok, value, 0.0)
        before = jnp.where(row_place == 0, left, pltpu.roll(value, 1, 0))
        after = jnp.where(row_place == strip - 1, right, pltpu.roll(value, strip - 1, 0))
        stack[f, r, :, 0:CH] = before.astype(BF16)
        stack[f, r, :, CH : 2 * CH] = value.astype(BF16)
        stack[f, r, :, 2 * CH : 3 * CH] = after.astype(BF16)

    edge_place = lax.broadcasted_iota(jnp.int32, (16, CH), 0)
    outer_mask = jnp.logical_and(takes_outer, edge_place % 2 == 1 - w)

    def input_stack(stack, source, landing, landing_out, apply):
        def step(f, _):
            edges = []
            for d in range(3):
                tile = jnp.where(outer_mask, landing_out[d, f].astype(F32), landing[d, f].astype(F32))
                edges.append(apply(tile))
            for r in range(rl + 2):
                d, row = row_source(r)
                tile = edges[d]
                store_stack(
                    stack, f, r, apply(source[f, r].astype(F32)),
                    tile[2 * row : 2 * row + 1], tile[2 * row + 1 : 2 * row + 2],
                )
            return 0

        lax.fori_loop(0, frames, step, 0)

    def window(stack, f):
        return [stack[f, kr : kr + rl].reshape(cells, 3 * CH) for kr in range(3)]

    def convolve(stack, weight, target, first=0, last=None):
        def step(f, _):
            product = jnp.dot(
                jnp.concatenate(window(stack, f), axis=1), weight[...], preferred_element_type=F32
            )
            for j in range(3):
                target[f + j] += product[:, j * CH : (j + 1) * CH]
            return 0

        lax.fori_loop(first, frames if last is None else last, step, 0)

    def weight_part(turned, stack, kr):
        left = jnp.concatenate([turned[f * CH : (f + 3) * CH, :] for f in range(frames)], axis=1)
        right = stack[:, kr : kr + rl].reshape(frames * cells, 3 * CH)
        return jnp.dot(left, right, preferred_element_type=F32)

    def peer(axis, j):
        if axis == "z":
            return dev(j, 0, 0)
        if axis == "x":
            return (z, lax.rem(hx + j, nx) * ny + hy, w)
        return (z, hx * ny + lax.rem(hy + j, ny), w)

    coords = {"z": z, "x": hx, "y": hy}
    orders = (("z", "y", "x"), ("y", "x", "z"), ("x", "z", "y"))
    half = 8
    span = half // ns
    tiles = span * 9
    piece = -(-tiles // ns)
    outs = (o1_ref, o2_ref)
    stage_at = {"core": 0, "a1": 1, "a2": 2, "a3": 3, "g2": 4, "g1": 5, "gc": 6}

    def sems(g, p, stage):
        return ar_send.at[g], ar_recv.at[g, p, stage_at[stage]]

    def arrived(g, p, stage, ref):
        take(ref, ar_recv.at[g, p, stage_at[stage]])

    def core_copy(g, p):
        return remote(a.at[g, p, pl.ds((1 - w) * half, half)], r0.at[g, p], *sems(g, p, "core"), dev(0, 0, 1))

    def core_start(g, p):
        core_copy(g, p).start()

    def a1_copies(g, p):
        axis = orders[p][0]
        return [
            remote(
                b1.at[g, p, pl.ds(lax.rem(coords[axis] + j, ns) * span, span)], r1.at[g, p, j - 1],
                *sems(g, p, "a1"), peer(axis, j),
            )
            for j in range(1, ns)
        ]

    def a1_start(g, p):
        arrived(g, p, "core", r0.at[g, p])
        b1[g, p] = a[g, p, pl.ds(w * half, half)] + r0[g, p]
        start_all(a1_copies(g, p))

    def a2_copies(g, p):
        axis = orders[p][1]
        return [
            remote(
                b2.at[g, p, pl.ds(lax.rem(coords[axis] + j, ns) * piece, piece)], r2.at[g, p, j - 1],
                *sems(g, p, "a2"), peer(axis, j),
            )
            for j in range(1, ns)
        ]

    def a2_start(g, p):
        arrived(g, p, "a1", r1.at[g, p])
        value = b1[g, p, pl.ds(coords[orders[p][0]] * span, span)]
        for j in range(ns - 1):
            value = value + r1[g, p, j]
        b2[g, p, 0:tiles] = value.reshape(tiles, 8, CH)
        if piece * ns > tiles:
            b2[g, p, tiles:] = jnp.zeros((piece * ns - tiles, 8, CH), F32)
        start_all(a2_copies(g, p))

    def a3_copies(g, p):
        axis = orders[p][2]
        slot = r3.at[g, p, coords[axis]]
        return [remote(slot, slot, *sems(g, p, "a3"), peer(axis, j)) for j in range(1, ns)]

    def a3_start(g, p):
        arrived(g, p, "a2", r2.at[g, p])
        value = b2[g, p, pl.ds(coords[orders[p][1]] * piece, piece)]
        for j in range(ns - 1):
            value = value + r2[g, p, j]
        r3[g, p, coords[orders[p][2]]] = value
        start_all(a3_copies(g, p))

    def g2_copies(g, p):
        axis = orders[p][1]
        part = g3.at[g, p, pl.ds(coords[axis] * piece, piece)]
        return [remote(part, part, *sems(g, p, "g2"), peer(axis, j)) for j in range(1, ns)]

    def g2_start(g, p):
        arrived(g, p, "a3", r3.at[g, p, pl.ds(0, ns - 1)])
        value = r3[g, p, 0]
        for n in range(1, ns):
            value = value + r3[g, p, n]
        g3[g, p, pl.ds(coords[orders[p][1]] * piece, piece)] = value
        start_all(g2_copies(g, p))

    def out_span(g, p, n):
        return outs[g].at[p, pl.ds(w * half + n * span, span)]

    def g1_copies(g, p):
        axis = orders[p][0]
        part = out_span(g, p, coords[axis])
        return [remote(part, part, *sems(g, p, "g1"), peer(axis, j)) for j in range(1, ns)]

    def gc_copy(g, p, j):
        part = out_span(g, p, lax.rem(coords[orders[p][0]] + ns - j, ns))
        return remote(part, part, *sems(g, p, "gc"), dev(0, 0, 1))

    def g1_start(g, p):
        arrived(g, p, "g2", g3.at[g, p, pl.ds(0, (ns - 1) * piece)])
        outs[g][p, pl.ds(w * half + coords[orders[p][0]] * span, span)] = g3[g, p, 0:tiles].reshape(span, 9, 8, CH)
        start_all(g1_copies(g, p))
        gc_copy(g, p, 0).start()

    def gc_start(g, p):
        arrived(g, p, "g1", outs[g].at[p, pl.ds(0, (ns - 1) * span)])
        for j in range(1, ns):
            gc_copy(g, p, j).start()

    def store_copy(g, p):
        return pltpu.make_async_copy(outs[g].at[p], (o1_hbm, o2_hbm)[g].at[p], store_sem.at[1 + g])

    def gc_end(g, p):
        arrived(g, p, "gc", outs[g].at[p, pl.ds(0, half)])
        store_copy(g, p).start()

    def ar_close(g):
        for p in range(3):
            wait_sends([core_copy(g, p)] + a1_copies(g, p) + a2_copies(g, p) + a3_copies(g, p))
            wait_sends(g2_copies(g, p) + g1_copies(g, p) + [gc_copy(g, p, j) for j in range(ns)])

    def each(stage, g):
        for p in range(3):
            stage(g, p)

    mean1, spread1 = moments_end(0)
    picks = lax.broadcasted_iota(jnp.int32, (CH // 4, CH), 1) // 4 == lax.broadcasted_iota(jnp.int32, (CH // 4, CH), 0)
    spread_exponent = jnp.dot(
        jnp.broadcast_to(exponent_ref[...].astype(F32), (8, CH // 4)), picks.astype(F32), preferred_element_type=F32
    )
    scale = jnp.exp2(spread_exponent[0:1])
    inv1 = 1.0 / jnp.sqrt(spread1 * (scale * scale) / total_size + EPS)
    factor1 = scale * inv1
    gain1, shift1 = gain1_ref[...], shift1_ref[...]
    gain2, shift2 = gain2_ref[...], shift2_ref[...]

    def rounded(value):
        return value.astype(BF16).astype(F32)

    def act_first(value):
        pre = (value - mean1) * factor1 * gain1 + shift1
        return rounded(pre * sigmoid(pre))

    wait_inputs(0, xr, xeb, xex)
    input_stack(s1, xr, xeb, xex, act_first)
    convolve(s1, wf1, hid)

    def hid_sum(n, total):
        return total + fold_rows(hid[n])

    mean_l = group_sum(total_row(lax.fori_loop(0, frames, hid_sum, zero8))) / local_size

    def hid_spread(n, total):
        off = hid[n] - mean_l
        return total + fold_rows(off * off)

    red_start(1, mean_l, group_sum(total_row(lax.fori_loop(0, frames, hid_spread, zero8))))

    wait_inputs(1, cr, ceb, cex)
    input_stack(sc, cr, ceb, cex, lambda value: value)
    convolve(sc, wb2, g2)
    mean2, spread2 = moments_end(1)
    inv2 = 1.0 / jnp.sqrt(spread2 / total_size + EPS)

    def second(n, totals):
        first_total, second_total = totals
        normed = (hid[n] - mean2) * inv2
        pre = normed * gain2 + shift2
        sig = sigmoid(pre)
        act_t[pl.ds(pl.multiple_of((n + 2) * CH, CH), CH), :] = jnp.transpose(pre * sig).astype(BF16)
        scaled = g2[n + 2] * (sig * (1.0 + pre * (1.0 - sig))) * gain2
        nrm[n] = normed
        g2[n + 2] = scaled
        return first_total + fold_rows(scaled), second_total + fold_rows(scaled * normed)

    t1, t2 = lax.fori_loop(0, frames, second, (zero8, zero8))
    red_start(2, group_sum(total_row(t1)), group_sum(total_row(t2)))

    def put_second(kr):
        block = weight_part(act_t, sc, kr)
        for kt in range(3):
            for kc in range(3):
                part = block[kt * CH : (kt + 1) * CH, kc * CH : (kc + 1) * CH]
                a[1, 2 - kr, :, kt * 3 + (2 - kc)] = part.reshape(16, 8, CH)
        core_start(1, 2 - kr)

    for kr in range(3):
        put_second(kr)
    each(a1_start, 1)
    m1, m2 = sums_end(2)

    def hidden(n, _):
        value = inv2 * (g2[n + 2] - m1 - nrm[n] * m2)
        hg_t[pl.ds(pl.multiple_of(n * CH, CH), CH), :] = jnp.transpose(value).astype(BF16)
        narrow = value.astype(BF16)
        hg[n, 1 : rl + 1] = narrow.reshape(rl, strip, CH)
        wide = narrow.astype(F32).reshape(rl, strip, CH)
        lefts = jnp.zeros((16, CH), F32)
        rights = jnp.zeros((16, CH), F32)
        for r in range(rl):
            lefts = jnp.where(edge_place == r, wide[r, 0:1], lefts)
            rights = jnp.where(edge_place == r, wide[r, strip - 1 : strip], rights)
        eh[0, n] = lefts.astype(BF16)
        eh[1, n] = rights.astype(BF16)
        return 0

    lax.fori_loop(0, frames, hidden, 0)

    line = w * nz + z

    def beside(ds, dh):
        place = lax.rem(line + ds + 2 * nz, 2 * nz)
        return (lax.rem(place, nz), lax.rem(h + dh + nh, nh), place // nz)

    halo = [
        remote(hg.at[:, pl.ds(rl, 1)], hg.at[:, pl.ds(0, 1)], halo_send.at[0], halo_recv.at[0], dev(0, 1, 0)),
        remote(hg.at[:, pl.ds(1, 1)], hg.at[:, pl.ds(rl + 1, 1)], halo_send.at[0], halo_recv.at[0], dev(0, -1, 0)),
    ]
    for n, dh in enumerate((0, 1, -1)):
        halo.append(remote(eh.at[0], heb.at[1 - dh, 1], halo_send.at[0], halo_recv.at[1], beside(-1, dh)))
        halo.append(remote(eh.at[1], heb.at[1 - dh, 0], halo_send.at[0], halo_recv.at[1], beside(1, dh)))
    start_all(halo)

    def put_first(kr):
        block = weight_part(hg_t, s1, kr)
        for j in range(3):
            for kc in range(3):
                part = block[j * CH : (j + 1) * CH, kc * CH : (kc + 1) * CH]
                a[0, kr, :, (2 - j) * 3 + kc] = part.reshape(16, 8, CH)
        core_start(0, kr)

    for kr in range(3):
        put_first(kr)
    each(a1_start, 0)
    take(hg.at[:, pl.ds(0, 2)], halo_recv.at[0])
    take(heb, halo_recv.at[1])

    def halo_stack(f, _):
        lefts = [heb[d, 0, f].astype(F32) for d in range(3)]
        rights = [heb[d, 1, f].astype(F32) for d in range(3)]
        for r in range(rl + 2):
            d, row = row_source(r)
            store_stack(sh, f, r, hg[f, r].astype(F32), lefts[d][row : row + 1], rights[d][row : row + 1])
        return 0

    lax.fori_loop(0, frames, halo_stack, 0)
    each(a2_start, 1)
    convolve(sh, wb1, g1, 0, frames // 2)
    each(a2_start, 0)
    convolve(sh, wb1, g1, frames // 2, frames)
    each(a3_start, 1)

    def first(f, totals):
        first_total, second_total = totals
        for r in range(rl):
            normed = (xr[f, r + 1].astype(F32) - mean1) * factor1
            pre = normed * gain1 + shift1
            sig = sigmoid(pre)
            scaled = g1[f + 2, r * strip : (r + 1) * strip] * (sig * (1.0 + pre * (1.0 - sig))) * gain1
            s_out[f, r] = scaled.astype(BF16)
            first_total = first_total + fold_rows(scaled)
            second_total = second_total + fold_rows(scaled * normed)
        return first_total, second_total

    t1, t2 = lax.fori_loop(0, frames, first, (zero8, zero8))
    red_start(3, group_sum(total_row(t1)), group_sum(total_row(t2)))

    back_copies = []
    for dz in range(nz):
        q = lax.rem(z + dz, nz)
        source = s_out.at[pl.ds(q * fl, fl)]
        target = s_in.at[:, :, pl.ds(pl.multiple_of(z * strip, strip), strip), :]
        if dz == 0:
            back_copies.append(pltpu.make_async_copy(source, target, back_recv.at[0]))
        else:
            back_copies.append(remote(source, target, back_send.at[0], back_recv.at[0], dev(dz, 0, 0)))
    start_all(back_copies)
    each(a3_start, 0)
    each(g2_start, 1)
    each(g2_start, 0)
    each(g1_start, 1)
    m1, m2 = sums_end(3)
    take(s_in, back_recv.at[0])

    def out_copy(f):
        return pltpu.make_async_copy(out_ref.at[f], out_hbm.at[f], store_sem.at[0])

    for f in range(fl):

        def last(r, _):
            normed = (xl[f, r].astype(F32) - mean1) * factor1
            out_ref[f, r] = cl[f, r].astype(F32) + inv1 * (s_in[f, r].astype(F32) - m1 - normed * m2)
            return 0

        lax.fori_loop(0, rl, last, 0)
        out_copy(f).start()
    each(g1_start, 0)
    each(gc_start, 1)
    each(gc_end, 1)
    wait_sends(x_main[1:] + x_edge[1:] + x_outer)
    wait_sends(c_main[1:] + c_edge[1:] + c_outer)
    for k in range(4):
        take(rb.at[k, pl.ds(0, devices - 1)], red_send.at[k])
    wait_sends(halo + back_copies[1:])
    ar_close(1)
    each(gc_start, 0)
    each(gc_end, 0)
    ar_close(0)
    for f in range(fl):
        out_copy(f).wait()
    for g in range(2):
        for p in range(3):
            store_copy(g, p).wait()


def shards(sizes, latent, exponents, cotangent, conv_first, conv_second, gain_first, shift_first, gain_second, shift_second):
    nz, nh, nx, ny = sizes
    channels, fl, rl, cols = latent.shape
    strip = cols // nz
    frames = fl * nz
    cells = rl * strip
    ns = nx
    span = 8 // ns
    tiles = span * 9
    piece = -(-tiles // ns)
    xl = jnp.transpose(latent, (1, 2, 3, 0))
    cl = jnp.transpose(cotangent, (1, 2, 3, 0))
    vmem = pl.BlockSpec(memory_space=pltpu.VMEM)
    any_space = pl.BlockSpec(memory_space=pl.ANY)
    part = (3, 16, 9, 8, CH)
    wide = (frames, rl + 2, strip, 3 * CH)
    scratch = [
        pltpu.VMEM((fl, rl, cols, CH), BF16),
        pltpu.VMEM((CH, 27 * CH), BF16),
        pltpu.VMEM((CH, 27 * CH), BF16),
        pltpu.VMEM((fl, rl, cols, CH), F32),
        pltpu.VMEM(part, F32),
        pltpu.VMEM(part, F32),
        pltpu.VMEM((frames, rl + 2, strip, CH), BF16),
        pltpu.VMEM((frames, rl + 2, strip, CH), BF16),
        pltpu.VMEM((nz + 1, fl, 16, CH), BF16),
        pltpu.VMEM((nz + 1, fl, 16, CH), BF16),
        pltpu.VMEM((3, frames, 16, CH), BF16),
        pltpu.VMEM((3, frames, 16, CH), BF16),
        pltpu.VMEM((3, frames, 16, CH), BF16),
        pltpu.VMEM((3, frames, 16, CH), BF16),
        pltpu.VMEM(wide, BF16),
        pltpu.VMEM(wide, BF16),
        pltpu.VMEM(wide, BF16),
        pltpu.VMEM((frames + 2, cells, CH), F32),
        pltpu.VMEM((frames + 2, cells, CH), F32),
        pltpu.VMEM((frames + 2, cells, CH), F32),
        pltpu.VMEM((frames, cells, CH), F32),
        pltpu.VMEM(((frames + 2) * CH, cells), BF16),
        pltpu.VMEM(((frames + 2) * CH, cells), BF16),
        pltpu.VMEM((frames, rl + 2, strip, CH), BF16),
        pltpu.VMEM((2, frames, 16, CH), BF16),
        pltpu.VMEM((3, 2, frames, 16, CH), BF16),
        pltpu.VMEM((9 * CH, 3 * CH), BF16),
        pltpu.VMEM((9 * CH, 3 * CH), BF16),
        pltpu.VMEM((9 * CH, 3 * CH), BF16),
        pltpu.VMEM((frames, rl, strip, CH), BF16),
        pltpu.VMEM((fl, rl, cols, CH), BF16),
        pltpu.VMEM((4, 2 * nz * nh, 1, CH), F32),
        pltpu.VMEM((2, 3, 16, 9, 8, CH), F32),
        pltpu.VMEM((2, 3, 8, 9, 8, CH), F32),
        pltpu.VMEM((2, 3, 8, 9, 8, CH), F32),
        pltpu.VMEM((2, 3, ns - 1, span, 9, 8, CH), F32),
        pltpu.VMEM((2, 3, piece * ns, 8, CH), F32),
        pltpu.VMEM((2, 3, ns - 1, piece, 8, CH), F32),
        pltpu.VMEM((2, 3, ns, piece, 8, CH), F32),
        pltpu.VMEM((2, 3, piece * ns, 8, CH), F32),
        pltpu.SemaphoreType.DMA((3,)),
        pltpu.SemaphoreType.DMA((3,)),
        pltpu.SemaphoreType.DMA((2,)),
        pltpu.SemaphoreType.DMA((2, 3)),
        pltpu.SemaphoreType.DMA((4,)),
        pltpu.SemaphoreType.DMA((4,)),
        pltpu.SemaphoreType.DMA((1,)),
        pltpu.SemaphoreType.DMA((2,)),
        pltpu.SemaphoreType.DMA((1,)),
        pltpu.SemaphoreType.DMA((1,)),
        pltpu.SemaphoreType.DMA((2,)),
        pltpu.SemaphoreType.DMA((2, 3, 7)),
    ]
    grad, first, second = pl.pallas_call(
        functools.partial(body, sizes),
        out_shape=(
            jax.ShapeDtypeStruct((fl, rl, cols, CH), F32),
            jax.ShapeDtypeStruct(part, F32),
            jax.ShapeDtypeStruct(part, F32),
        ),
        in_specs=[vmem] + [any_space] * 3 + [vmem] * 5,
        out_specs=(any_space,) * 3,
        scratch_shapes=scratch,
        compiler_params=pltpu.CompilerParams(
            collective_id=0, has_side_effects=True, vmem_limit_bytes=60 * 1024 * 1024
        ),
    )(
        xl, cl, conv_first, conv_second, exponents[None],
        gain_first[None], shift_first[None], gain_second[None], shift_second[None],
    )
    first = first.reshape(3, 16, 3, 3, 8, CH).transpose(1, 4, 2, 0, 3, 5).reshape(CH, 27 * CH)
    second = second.reshape(3, 16, 3, 3, 8, CH).transpose(5, 2, 0, 3, 1, 4).reshape(CH, 27 * CH)
    return jnp.transpose(grad, (3, 0, 1, 2)), first, second


def solution(mesh):
    nz, nh = mesh.shape["tm"], mesh.shape["height"]
    nx = int(round(nh**0.5))
    placed = P(None, "tm", "height", "width")
    return jax.shard_map(
        functools.partial(shards, (nz, nh, nx, nh // nx)),
        mesh=mesh,
        in_specs=(placed, P(), placed, P(), P(), P(), P(), P(), P()),
        out_specs=(placed, P(), P()),
        check_vma=False,
    )
```

```python
import functools

import jax
import jax.numpy as jnp
from jax import lax
from jax.experimental import pallas as pl
from jax.experimental.pallas import tpu as pltpu
from jax.sharding import PartitionSpec as P

MESH = pl.DeviceIdType.MESH
EPS = 1e-05
CH = 128
F32 = jnp.float32
BF16 = jnp.bfloat16


def group_sum(row):
    lane = lax.broadcasted_iota(jnp.int32, row.shape, 1)
    pair = row + jnp.where(lane % 2 == 0, pltpu.roll(row, CH - 1, 1), pltpu.roll(row, 1, 1))
    return pair + jnp.where(lane % 4 < 2, pltpu.roll(pair, CH - 2, 1), pltpu.roll(pair, 2, 1))


def fold_rows(cells):
    return jnp.sum(cells.reshape(-1, 8, CH), axis=0)


def total_row(partial):
    return jnp.sum(partial, axis=0, keepdims=True)


def lanes_low(row):
    return lax.broadcasted_iota(jnp.int32, row.shape, row.ndim - 1) % 4 < 2


def pack_pair(first, second):
    return jnp.where(lanes_low(first), first, second)


def unpack_pair(row):
    low = lanes_low(row)
    return jnp.where(low, row, pltpu.roll(row, 2, 1)), jnp.where(low, pltpu.roll(row, CH - 2, 1), row)


def far_first(n, size):
    if size == 4:
        return (2 + 3 * n + 3 * ((n * (n - 1)) // 2)) % 4
    return size - 1 - n


def sigmoid(value):
    return 1.0 / (1.0 + jnp.exp(-value))


def body(
    sizes,
    x_hbm, c_hbm, w1_hbm, w2_hbm, exponent_ref, gain1_ref, shift1_ref, gain2_ref, shift2_ref,
    out_hbm, o1_hbm, o2_hbm,
    x_raw, c_raw, xl, cl, w1, w2, out_ref, o1_ref, o2_ref, fin1, fin2,
    xr, cr, xe, ce, xeb, ceb, xex, cex, s1, sc, sh, hid, g2, g1, nrm, act_t, hg_t, hg, eh, heb,
    wf1, wb1, wb2, s_out, s_in, rb, a, r0, b1, r1, b2, r2, r3, g3,
    load_sem, store_sem, in_send, in_recv, red_send, red_recv, halo_send, halo_recv, back_send, back_recv,
    ar_send, ar_recv,
):
    nz, nh, nx, ny = sizes
    ns = nx
    fl, rl, cols = xl.shape[0], xl.shape[1], xl.shape[2]
    strip = cols // nz
    frames = fl * nz
    cells = rl * strip
    z, h, w = lax.axis_index("tm"), lax.axis_index("height"), lax.axis_index("width")
    hx, hy = h // ny, h % ny

    def dev(dz, dh, dw):
        return (lax.rem(z + dz + nz, nz), lax.rem(h + dh + nh, nh), lax.rem(w + dw, 2))

    loads = [
        pltpu.make_async_copy(source, target, load_sem.at[n])
        for n, (source, target) in enumerate(((x_hbm, x_raw), (c_hbm, c_raw), (w1_hbm, w1), (w2_hbm, w2)))
    ]
    for copy in loads:
        copy.start()

    heights = [(ox, oy) for ox in range(nx) for oy in range(ny)]
    heights.sort(key=lambda place: -(min(place[0], nx - place[0]) + min(place[1], ny - place[1])))
    targets_h = [lax.rem(hx + ox, nx) * ny + lax.rem(hy + oy, ny) for ox, oy in heights]

    def for_each_device(act):
        def step(n, _):
            dz, dw = far_first(n // 2, nz), 1 - n % 2
            zt, wt = lax.rem(z + dz, nz), lax.rem(w + dw, 2)
            for ht in targets_h[:-1]:
                act((zt, ht, wt))

            @pl.when(n < 2 * nz - 1)
            def _():
                act((zt, h, wt))

            return 0

        lax.fori_loop(0, 2 * nz, step, 0)

    devices = 2 * nz * nh
    barrier = pltpu.get_barrier_semaphore()
    for dz in reversed(range(nz)):
        for dw in (1, 0):
            zt, wt = lax.rem(z + dz, nz), lax.rem(w + dw, 2)
            for ht in targets_h if (dz, dw) != (0, 0) else targets_h[:-1]:
                pl.semaphore_signal(barrier, inc=1, device_id=(zt, ht, wt), device_id_type=MESH)

    def take(ref, sem):
        pltpu.make_async_copy(ref, ref, sem).wait()

    def remote(src, dst, send, recv, where):
        return pltpu.make_async_remote_copy(
            src_ref=src, dst_ref=dst, send_sem=send, recv_sem=recv, device_id=where, device_id_type=MESH
        )

    own_frames = pl.ds(z * fl, fl)
    row_parts = {0: ((0, rl), (1, rl)), 1: ((rl - 1, 1), (0, 1)), -1: ((0, 1), (rl + 1, 1))}

    def main_copies(k, src, dst):
        copies = []
        for dz in range(nz):
            q = lax.rem(z + dz, nz)
            for n, dh in enumerate((0, 1, -1)):
                (r_from, count), (r_to, _) = row_parts[dh]
                source = src.at[:, pl.ds(r_from, count), pl.ds(pl.multiple_of(q * strip, strip), strip), :]
                target = dst.at[own_frames, pl.ds(r_to, count)]
                if dz == 0 and dh == 0:
                    copies.append(pltpu.make_async_copy(source, target, in_recv.at[k, 0]))
                else:
                    copies.append(remote(source, target, in_send.at[k], in_recv.at[k, 0], dev(dz, dh, 0)))
        return copies

    def build_edges(src, edges):
        def at(f, r, col):
            start = (col // 16) * 16
            return src[f, r, start : start + 16, :].astype(F32)[col % 16 : col % 16 + 1]

        place = lax.broadcasted_iota(jnp.int32, (16, CH), 0)
        for f in range(fl):
            for q in range(nz):
                tile = jnp.zeros((16, CH), F32)
                for r in range(rl):
                    if q > 0:
                        tile = jnp.where(place == 2 * r, at(f, r, q * strip - 1), tile)
                    if q < nz - 1:
                        tile = jnp.where(place == 2 * r + 1, at(f, r, (q + 1) * strip), tile)
                edges[q, f] = tile.astype(BF16)
            tile = jnp.zeros((16, CH), F32)
            for r in range(rl):
                outer = jnp.where(w == 0, at(f, r, cols - 1), at(f, r, 0))
                tile = jnp.where(place // 2 == r, outer, tile)
            edges[nz, f] = tile.astype(BF16)

    def edge_copies(k, edges, landing, landing_out):
        copies = []
        for dz in range(nz):
            q = lax.rem(z + dz, nz)
            for n, dh in enumerate((0, 1, -1)):
                source = edges.at[q]
                target = landing.at[1 - dh, own_frames]
                if dz == 0 and dh == 0:
                    copies.append(pltpu.make_async_copy(source, target, in_recv.at[k, 1]))
                else:
                    copies.append(remote(source, target, in_send.at[k], in_recv.at[k, 1], dev(dz, dh, 0)))
        return copies

    outer_q = (nz - 1) * w
    takes_outer = z == (nz - 1) * (1 - w)

    def outer_sends(k, edges, landing_out):
        copies = []
        for dh in (0, 1, -1):
            where = (outer_q, lax.rem(h + dh + nh, nh), 1 - w)
            copies.append(
                remote(edges.at[nz], landing_out.at[1 - dh, own_frames], in_send.at[k], in_recv.at[k, 2], where)
            )
        return copies

    def wait_inputs(k, cells_in, landing, landing_out):
        take(cells_in, in_recv.at[k, 0])
        take(landing, in_recv.at[k, 1])

        @pl.when(takes_outer)
        def _():
            take(landing_out, in_recv.at[k, 2])

    def start_all(copies):
        for copy in copies:
            copy.start()

    def wait_sends(copies):
        for copy in copies:
            copy.wait_send()

    me = (z * nh + h) * 2 + w
    local_size = 4.0 * fl * rl * cols
    total_size = local_size * devices

    def red_start(k, first, second):
        rb[k, me] = pack_pair(first, second)
        slot = rb.at[k, me]
        for_each_device(lambda where: remote(slot, slot, red_send.at[k], red_recv.at[k], where).start())

    def red_wait(k):
        take(rb.at[k, pl.ds(0, devices - 1)], red_recv.at[k])

    def moments_end(k):
        red_wait(k)
        rows = rb[k]
        mean, _ = unpack_pair(jnp.sum(rows, axis=0) / devices)
        low = lanes_low(rows)
        off = rows - jnp.where(lanes_low(mean), mean, 0.0)[None]
        between, within = unpack_pair(jnp.sum(jnp.where(low, off * off, off), axis=0))
        return mean, within + local_size * between

    def sums_end(k):
        red_wait(k)
        return unpack_pair(jnp.sum(rb[k], axis=0) / total_size)

    def turn(source, target):
        for f in range(fl):
            for r in range(rl):
                target[f, r] = jnp.transpose(source[:, f, r, :].astype(F32)).astype(BF16)

    loads[0].wait()
    turn(x_raw, xl)
    build_edges(xl, xe)
    zero8 = jnp.zeros((8, CH), F32)

    def x_sum(n, total):
        return total + fold_rows(xl[n // rl, n % rl].astype(F32))

    local_mean = group_sum(total_row(lax.fori_loop(0, fl * rl, x_sum, zero8))) / local_size

    def x_spread(n, total):
        off = xl[n // rl, n % rl].astype(F32) - local_mean
        return total + fold_rows(off * off)

    local_spread = group_sum(total_row(lax.fori_loop(0, fl * rl, x_spread, zero8)))

    loads[1].wait()
    turn(c_raw, cl)
    build_edges(cl, ce)
    loads[2].wait()
    loads[3].wait()
    for kt in range(3):
        for kr in range(3):
            for kc in range(3):
                tap = 9 * kt + 3 * kr + kc
                back = ((2 - kr) * 3 + (2 - kc)) * CH
                for source, target in ((w1, wb1), (w2, wb2)):
                    target[back : back + CH, kt * CH : (kt + 1) * CH] = source[:, tap * CH : (tap + 1) * CH]
    for kt in range(3):
        for kr in range(3):
            for kc in range(3):
                tap = 9 * kt + 3 * kr + kc
                ahead = (kr * 3 + kc) * CH
                block = w1[:, tap * CH : (tap + 1) * CH].astype(F32)
                wf1[ahead : ahead + CH, (2 - kt) * CH : (3 - kt) * CH] = jnp.transpose(block).astype(BF16)
    pl.semaphore_wait(barrier, devices - 1)
    x_main = main_copies(0, xl, xr)
    x_edge = edge_copies(0, xe, xeb, xex)
    x_outer = outer_sends(0, xe, xex)
    start_all(x_main + x_edge + x_outer)
    red_start(0, local_mean, local_spread)
    c_main = main_copies(1, cl, cr)
    c_edge = edge_copies(1, ce, ceb, cex)
    c_outer = outer_sends(1, ce, cex)
    start_all(c_main + c_edge + c_outer)
    zero_cells = jnp.zeros((cells, CH), F32)

    def clear(n, _):
        hid[n] = zero_cells
        g2[n] = zero_cells
        g1[n] = zero_cells
        return 0

    lax.fori_loop(0, frames + 2, clear, 0)
    zero_t = jnp.zeros((2 * CH, cells), BF16)
    act_t[0 : 2 * CH] = zero_t
    hg_t[frames * CH : (frames + 2) * CH] = zero_t

    row_place = lax.broadcasted_iota(jnp.int32, (strip, CH), 0)
    left_ok = jnp.logical_not(jnp.logical_and(w == 0, z == 0))
    right_ok = jnp.logical_not(jnp.logical_and(w == 1, z == nz - 1))

    def row_ok(r):
        if r == 0:
            return h > 0
        if r == rl + 1:
            return h < nh - 1
        return None

    def row_source(r):
        if r == 0:
            return 0, rl - 1
        if r == rl + 1:
            return 2, 0
        return 1, r - 1

    def store_stack(stack, f, r, value, left, right):
        ok = row_ok(r)
        left = jnp.where(left_ok if ok is None else jnp.logical_and(left_ok, ok), left, 0.0)
        right = jnp.where(right_ok if ok is None else jnp.logical_and(right_ok, ok), right, 0.0)
        if ok is not None:
            value = jnp.where(ok, value, 0.0)
        before = jnp.where(row_place == 0, left, pltpu.roll(value, 1, 0))
        after = jnp.where(row_place == strip - 1, right, pltpu.roll(value, strip - 1, 0))
        stack[f, r, :, 0:CH] = before.astype(BF16)
        stack[f, r, :, CH : 2 * CH] = value.astype(BF16)
        stack[f, r, :, 2 * CH : 3 * CH] = after.astype(BF16)

    edge_place = lax.broadcasted_iota(jnp.int32, (16, CH), 0)
    outer_mask = jnp.logical_and(takes_outer, edge_place % 2 == 1 - w)

    def input_stack(stack, source, landing, landing_out, apply):
        def step(f, _):
            edges = []
            for d in range(3):
                tile = jnp.where(outer_mask, landing_out[d, f].astype(F32), landing[d, f].astype(F32))
                edges.append(apply(tile))
            for r in range(rl + 2):
                d, row = row_source(r)
                tile = edges[d]
                store_stack(
                    stack, f, r, apply(source[f, r].astype(F32)),
                    tile[2 * row : 2 * row + 1], tile[2 * row + 1 : 2 * row + 2],
                )
            return 0

        lax.fori_loop(0, frames, step, 0)

    def window(stack, f):
        return [stack[f, kr : kr + rl].reshape(cells, 3 * CH) for kr in range(3)]

    def convolve(stack, weight, target, first=0, last=None):
        def step(f, _):
            product = jnp.dot(
                jnp.concatenate(window(stack, f), axis=1), weight[...], preferred_element_type=F32
            )
            for j in range(3):
                target[f + j] += product[:, j * CH : (j + 1) * CH]
            return 0

        lax.fori_loop(first, frames if last is None else last, step, 0)

    def weight_part(turned, stack, kr):
        left = jnp.concatenate([turned[f * CH : (f + 3) * CH, :] for f in range(frames)], axis=1)
        right = stack[:, kr : kr + rl].reshape(frames * cells, 3 * CH)
        return jnp.dot(left, right, preferred_element_type=F32)

    def peer(axis, j):
        if axis == "z":
            return dev(j, 0, 0)
        if axis == "x":
            return (z, lax.rem(hx + j, nx) * ny + hy, w)
        return (z, hx * ny + lax.rem(hy + j, ny), w)

    coords = {"z": z, "x": hx, "y": hy}
    orders = (("z", "y", "x"), ("y", "x", "z"), ("x", "z", "y"))
    half = 8
    span = half // ns
    tiles = span * 9
    piece = -(-tiles // ns)
    outs = (o1_ref, o2_ref)
    stage_at = {"core": 0, "a1": 1, "a2": 2, "a3": 3, "g2": 4, "g1": 5, "gc": 6}

    def sems(g, p, stage):
        return ar_send.at[g], ar_recv.at[g, p, stage_at[stage]]

    def arrived(g, p, stage, ref):
        take(ref, ar_recv.at[g, p, stage_at[stage]])

    def core_copy(g, p):
        return remote(a.at[g, p, pl.ds((1 - w) * half, half)], r0.at[g, p], *sems(g, p, "core"), dev(0, 0, 1))

    def core_start(g, p):
        core_copy(g, p).start()

    def a1_copies(g, p):
        axis = orders[p][0]
        return [
            remote(
                b1.at[g, p, pl.ds(lax.rem(coords[axis] + j, ns) * span, span)], r1.at[g, p, j - 1],
                *sems(g, p, "a1"), peer(axis, j),
            )
            for j in range(1, ns)
        ]

    def a1_start(g, p):
        arrived(g, p, "core", r0.at[g, p])
        b1[g, p] = a[g, p, pl.ds(w * half, half)] + r0[g, p]
        start_all(a1_copies(g, p))

    def a2_copies(g, p):
        axis = orders[p][1]
        return [
            remote(
                b2.at[g, p, pl.ds(lax.rem(coords[axis] + j, ns) * piece, piece)], r2.at[g, p, j - 1],
                *sems(g, p, "a2"), peer(axis, j),
            )
            for j in range(1, ns)
        ]

    def a2_start(g, p):
        arrived(g, p, "a1", r1.at[g, p])
        value = b1[g, p, pl.ds(coords[orders[p][0]] * span, span)]
        for j in range(ns - 1):
            value = value + r1[g, p, j]
        b2[g, p, 0:tiles] = value.reshape(tiles, 8, CH)
        if piece * ns > tiles:
            b2[g, p, tiles:] = jnp.zeros((piece * ns - tiles, 8, CH), F32)
        start_all(a2_copies(g, p))

    def a3_copies(g, p):
        axis = orders[p][2]
        slot = r3.at[g, p, coords[axis]]
        return [remote(slot, slot, *sems(g, p, "a3"), peer(axis, j)) for j in range(1, ns)]

    def a3_start(g, p):
        arrived(g, p, "a2", r2.at[g, p])
        value = b2[g, p, pl.ds(coords[orders[p][1]] * piece, piece)]
        for j in range(ns - 1):
            value = value + r2[g, p, j]
        r3[g, p, coords[orders[p][2]]] = value
        start_all(a3_copies(g, p))

    def g2_copies(g, p):
        axis = orders[p][1]
        part = g3.at[g, p, pl.ds(coords[axis] * piece, piece)]
        return [remote(part, part, *sems(g, p, "g2"), peer(axis, j)) for j in range(1, ns)]

    def g2_start(g, p):
        arrived(g, p, "a3", r3.at[g, p, pl.ds(0, ns - 1)])
        value = r3[g, p, 0]
        for n in range(1, ns):
            value = value + r3[g, p, n]
        g3[g, p, pl.ds(coords[orders[p][1]] * piece, piece)] = value
        start_all(g2_copies(g, p))

    def out_span(g, p, n):
        return outs[g].at[p, pl.ds(w * half + n * span, span)]

    def g1_copies(g, p):
        axis = orders[p][0]
        part = out_span(g, p, coords[axis])
        return [remote(part, part, *sems(g, p, "g1"), peer(axis, j)) for j in range(1, ns)]

    def gc_copy(g, p, j):
        part = out_span(g, p, lax.rem(coords[orders[p][0]] + ns - j, ns))
        return remote(part, part, *sems(g, p, "gc"), dev(0, 0, 1))

    def g1_start(g, p):
        arrived(g, p, "g2", g3.at[g, p, pl.ds(0, (ns - 1) * piece)])
        outs[g][p, pl.ds(w * half + coords[orders[p][0]] * span, span)] = g3[g, p, 0:tiles].reshape(span, 9, 8, CH)
        start_all(g1_copies(g, p))
        gc_copy(g, p, 0).start()

    def gc_start(g, p):
        arrived(g, p, "g1", outs[g].at[p, pl.ds(0, (ns - 1) * span)])
        for j in range(1, ns):
            gc_copy(g, p, j).start()

    def store_copy(g):
        return pltpu.make_async_copy((fin1, fin2)[g], (o1_hbm, o2_hbm)[g], store_sem.at[1 + g])

    def gc_end(g, p):
        arrived(g, p, "gc", outs[g].at[p, pl.ds(0, half)])
        for kt in range(3):
            for kc in range(3):
                block = outs[g][p, :, kt * 3 + kc].reshape(CH, CH)
                tap = 9 * kt + 3 * p + kc
                (fin1, fin2)[g][:, tap * CH : (tap + 1) * CH] = block if g == 0 else jnp.transpose(block)

    def ar_close(g):
        for p in range(3):
            wait_sends([core_copy(g, p)] + a1_copies(g, p) + a2_copies(g, p) + a3_copies(g, p))
            wait_sends(g2_copies(g, p) + g1_copies(g, p) + [gc_copy(g, p, j) for j in range(ns)])

    def each(stage, g):
        for p in range(3):
            stage(g, p)

    mean1, spread1 = moments_end(0)
    picks = lax.broadcasted_iota(jnp.int32, (CH // 4, CH), 1) // 4 == lax.broadcasted_iota(jnp.int32, (CH // 4, CH), 0)
    spread_exponent = jnp.dot(
        jnp.broadcast_to(exponent_ref[...].astype(F32), (8, CH // 4)), picks.astype(F32), preferred_element_type=F32
    )
    scale = jnp.exp2(spread_exponent[0:1])
    inv1 = 1.0 / jnp.sqrt(spread1 * (scale * scale) / total_size + EPS)
    factor1 = scale * inv1
    gain1, shift1 = gain1_ref[...], shift1_ref[...]
    gain2, shift2 = gain2_ref[...], shift2_ref[...]

    def rounded(value):
        return value.astype(BF16).astype(F32)

    def act_first(value):
        pre = (value - mean1) * factor1 * gain1 + shift1
        return rounded(pre * sigmoid(pre))

    wait_inputs(0, xr, xeb, xex)
    input_stack(s1, xr, xeb, xex, act_first)
    convolve(s1, wf1, hid)

    def hid_sum(n, total):
        return total + fold_rows(hid[n])

    mean_l = group_sum(total_row(lax.fori_loop(0, frames, hid_sum, zero8))) / local_size

    def hid_spread(n, total):
        off = hid[n] - mean_l
        return total + fold_rows(off * off)

    red_start(1, mean_l, group_sum(total_row(lax.fori_loop(0, frames, hid_spread, zero8))))

    wait_inputs(1, cr, ceb, cex)
    input_stack(sc, cr, ceb, cex, lambda value: value)
    convolve(sc, wb2, g2)
    mean2, spread2 = moments_end(1)
    inv2 = 1.0 / jnp.sqrt(spread2 / total_size + EPS)

    def second(n, totals):
        first_total, second_total = totals
        normed = (hid[n] - mean2) * inv2
        pre = normed * gain2 + shift2
        sig = sigmoid(pre)
        act_t[pl.ds(pl.multiple_of((n + 2) * CH, CH), CH), :] = jnp.transpose(pre * sig).astype(BF16)
        scaled = g2[n + 2] * (sig * (1.0 + pre * (1.0 - sig))) * gain2
        nrm[n] = normed
        g2[n + 2] = scaled
        return first_total + fold_rows(scaled), second_total + fold_rows(scaled * normed)

    t1, t2 = lax.fori_loop(0, frames, second, (zero8, zero8))
    red_start(2, group_sum(total_row(t1)), group_sum(total_row(t2)))

    def put_second(kr):
        block = weight_part(act_t, sc, kr)
        for kt in range(3):
            for kc in range(3):
                part = block[kt * CH : (kt + 1) * CH, kc * CH : (kc + 1) * CH]
                a[1, 2 - kr, :, kt * 3 + (2 - kc)] = part.reshape(16, 8, CH)
        core_start(1, 2 - kr)

    for kr in range(3):
        put_second(kr)
    each(a1_start, 1)
    m1, m2 = sums_end(2)

    def hidden(n, _):
        value = inv2 * (g2[n + 2] - m1 - nrm[n] * m2)
        hg_t[pl.ds(pl.multiple_of(n * CH, CH), CH), :] = jnp.transpose(value).astype(BF16)
        narrow = value.astype(BF16)
        hg[n, 1 : rl + 1] = narrow.reshape(rl, strip, CH)
        wide = narrow.astype(F32).reshape(rl, strip, CH)
        lefts = jnp.zeros((16, CH), F32)
        rights = jnp.zeros((16, CH), F32)
        for r in range(rl):
            lefts = jnp.where(edge_place == r, wide[r, 0:1], lefts)
            rights = jnp.where(edge_place == r, wide[r, strip - 1 : strip], rights)
        eh[0, n] = lefts.astype(BF16)
        eh[1, n] = rights.astype(BF16)
        return 0

    lax.fori_loop(0, frames, hidden, 0)

    line = w * nz + z

    def beside(ds, dh):
        place = lax.rem(line + ds + 2 * nz, 2 * nz)
        return (lax.rem(place, nz), lax.rem(h + dh + nh, nh), place // nz)

    halo = [
        remote(hg.at[:, pl.ds(rl, 1)], hg.at[:, pl.ds(0, 1)], halo_send.at[0], halo_recv.at[0], dev(0, 1, 0)),
        remote(hg.at[:, pl.ds(1, 1)], hg.at[:, pl.ds(rl + 1, 1)], halo_send.at[0], halo_recv.at[0], dev(0, -1, 0)),
    ]
    for n, dh in enumerate((0, 1, -1)):
        halo.append(remote(eh.at[0], heb.at[1 - dh, 1], halo_send.at[0], halo_recv.at[1], beside(-1, dh)))
        halo.append(remote(eh.at[1], heb.at[1 - dh, 0], halo_send.at[0], halo_recv.at[1], beside(1, dh)))
    start_all(halo)

    def put_first(kr):
        block = weight_part(hg_t, s1, kr)
        for j in range(3):
            for kc in range(3):
                part = block[j * CH : (j + 1) * CH, kc * CH : (kc + 1) * CH]
                a[0, kr, :, (2 - j) * 3 + kc] = part.reshape(16, 8, CH)
        core_start(0, kr)

    for kr in range(3):
        put_first(kr)
    each(a1_start, 0)
    take(hg.at[:, pl.ds(0, 2)], halo_recv.at[0])
    take(heb, halo_recv.at[1])

    def halo_stack(f, _):
        lefts = [heb[d, 0, f].astype(F32) for d in range(3)]
        rights = [heb[d, 1, f].astype(F32) for d in range(3)]
        for r in range(rl + 2):
            d, row = row_source(r)
            store_stack(sh, f, r, hg[f, r].astype(F32), lefts[d][row : row + 1], rights[d][row : row + 1])
        return 0

    lax.fori_loop(0, frames, halo_stack, 0)
    each(a2_start, 1)

    def first(f, totals):
        first_total, second_total = totals
        for r in range(rl):
            normed = (xr[f, r + 1].astype(F32) - mean1) * factor1
            pre = normed * gain1 + shift1
            sig = sigmoid(pre)
            scaled = g1[f + 2, r * strip : (r + 1) * strip] * (sig * (1.0 + pre * (1.0 - sig))) * gain1
            s_out[f, r] = scaled.astype(BF16)
            first_total = first_total + fold_rows(scaled)
            second_total = second_total + fold_rows(scaled * normed)
        return first_total, second_total

    back_from = s_in.at[:, :, pl.ds(pl.multiple_of(z * strip, strip), strip), :]
    back_copies = []

    def send_back(q):
        source = s_out.at[pl.ds(q * fl, fl)]
        far = remote(source, back_from, back_send.at[0], back_recv.at[0], (q, h, w))
        back_copies.append(far)

        @pl.when(z == q)
        def _():
            pltpu.make_async_copy(source, back_from, back_recv.at[0]).start()

        @pl.when(z != q)
        def _():
            far.start()

    convolve(sh, wb1, g1, 0, 2)
    totals = (zero8, zero8)
    for q in range(nz):
        if q * fl + 2 < frames:
            convolve(sh, wb1, g1, q * fl + 2, q * fl + fl + 2)
        totals = lax.fori_loop(q * fl, q * fl + fl, first, totals)
        send_back(q)
        if q == nz // 2 - 1:
            each(a2_start, 0)
    t1, t2 = totals
    red_start(3, group_sum(total_row(t1)), group_sum(total_row(t2)))
    each(a3_start, 1)
    each(a3_start, 0)
    each(g2_start, 1)
    each(g2_start, 0)
    each(g1_start, 1)
    m1, m2 = sums_end(3)
    take(s_in, back_recv.at[0])

    def out_copy(f):
        return pltpu.make_async_copy(out_ref.at[:, f], out_hbm.at[:, f], store_sem.at[0])

    for f in range(fl):
        for r in range(rl):
            normed = (xl[f, r].astype(F32) - mean1) * factor1
            value = cl[f, r].astype(F32) + inv1 * (s_in[f, r].astype(F32) - m1 - normed * m2)
            out_ref[:, f, r, :] = jnp.transpose(value)
        out_copy(f).start()
    each(g1_start, 0)
    each(gc_start, 1)
    each(gc_end, 1)
    store_copy(1).start()
    wait_sends(x_main[1:] + x_edge[1:] + x_outer)
    wait_sends(c_main[1:] + c_edge[1:] + c_outer)
    for k in range(4):
        take(rb.at[k, pl.ds(0, devices - 1)], red_send.at[k])
    wait_sends(halo)
    for q in range(nz):

        @pl.when(z != q)
        def _():
            back_copies[q].wait_send()

    ar_close(1)
    each(gc_start, 0)
    each(gc_end, 0)
    store_copy(0).start()
    ar_close(0)
    for f in range(fl):
        out_copy(f).wait()
    store_copy(0).wait()
    store_copy(1).wait()


def shards(sizes, latent, exponents, cotangent, conv_first, conv_second, gain_first, shift_first, gain_second, shift_second):
    nz, nh, nx, ny = sizes
    channels, fl, rl, cols = latent.shape
    strip = cols // nz
    frames = fl * nz
    cells = rl * strip
    ns = nx
    span = 8 // ns
    tiles = span * 9
    piece = -(-tiles // ns)
    vmem = pl.BlockSpec(memory_space=pltpu.VMEM)
    any_space = pl.BlockSpec(memory_space=pl.ANY)
    part = (3, 16, 9, 8, CH)
    wide = (frames, rl + 2, strip, 3 * CH)
    scratch = [
        pltpu.VMEM((CH, fl, rl, cols), BF16),
        pltpu.VMEM((CH, fl, rl, cols), BF16),
        pltpu.VMEM((fl, rl, cols, CH), BF16),
        pltpu.VMEM((fl, rl, cols, CH), BF16),
        pltpu.VMEM((CH, 27 * CH), BF16),
        pltpu.VMEM((CH, 27 * CH), BF16),
        pltpu.VMEM((CH, fl, rl, cols), F32),
        pltpu.VMEM(part, F32),
        pltpu.VMEM(part, F32),
        pltpu.VMEM((CH, 27 * CH), F32),
        pltpu.VMEM((CH, 27 * CH), F32),
        pltpu.VMEM((frames, rl + 2, strip, CH), BF16),
        pltpu.VMEM((frames, rl + 2, strip, CH), BF16),
        pltpu.VMEM((nz + 1, fl, 16, CH), BF16),
        pltpu.VMEM((nz + 1, fl, 16, CH), BF16),
        pltpu.VMEM((3, frames, 16, CH), BF16),
        pltpu.VMEM((3, frames, 16, CH), BF16),
        pltpu.VMEM((3, frames, 16, CH), BF16),
        pltpu.VMEM((3, frames, 16, CH), BF16),
        pltpu.VMEM(wide, BF16),
        pltpu.VMEM(wide, BF16),
        pltpu.VMEM(wide, BF16),
        pltpu.VMEM((frames + 2, cells, CH), F32),
        pltpu.VMEM((frames + 2, cells, CH), F32),
        pltpu.VMEM((frames + 2, cells, CH), F32),
        pltpu.VMEM((frames, cells, CH), F32),
        pltpu.VMEM(((frames + 2) * CH, cells), BF16),
        pltpu.VMEM(((frames + 2) * CH, cells), BF16),
        pltpu.VMEM((frames, rl + 2, strip, CH), BF16),
        pltpu.VMEM((2, frames, 16, CH), BF16),
        pltpu.VMEM((3, 2, frames, 16, CH), BF16),
        pltpu.VMEM((9 * CH, 3 * CH), BF16),
        pltpu.VMEM((9 * CH, 3 * CH), BF16),
        pltpu.VMEM((9 * CH, 3 * CH), BF16),
        pltpu.VMEM((frames, rl, strip, CH), BF16),
        pltpu.VMEM((fl, rl, cols, CH), BF16),
        pltpu.VMEM((4, 2 * nz * nh, 1, CH), F32),
        pltpu.VMEM((2, 3, 16, 9, 8, CH), F32),
        pltpu.VMEM((2, 3, 8, 9, 8, CH), F32),
        pltpu.VMEM((2, 3, 8, 9, 8, CH), F32),
        pltpu.VMEM((2, 3, ns - 1, span, 9, 8, CH), F32),
        pltpu.VMEM((2, 3, piece * ns, 8, CH), F32),
        pltpu.VMEM((2, 3, ns - 1, piece, 8, CH), F32),
        pltpu.VMEM((2, 3, ns, piece, 8, CH), F32),
        pltpu.VMEM((2, 3, piece * ns, 8, CH), F32),
        pltpu.SemaphoreType.DMA((4,)),
        pltpu.SemaphoreType.DMA((3,)),
        pltpu.SemaphoreType.DMA((2,)),
        pltpu.SemaphoreType.DMA((2, 3)),
        pltpu.SemaphoreType.DMA((4,)),
        pltpu.SemaphoreType.DMA((4,)),
        pltpu.SemaphoreType.DMA((1,)),
        pltpu.SemaphoreType.DMA((2,)),
        pltpu.SemaphoreType.DMA((1,)),
        pltpu.SemaphoreType.DMA((1,)),
        pltpu.SemaphoreType.DMA((2,)),
        pltpu.SemaphoreType.DMA((2, 3, 7)),
    ]
    return pl.pallas_call(
        functools.partial(body, sizes),
        out_shape=(
            jax.ShapeDtypeStruct((CH, fl, rl, cols), F32),
            jax.ShapeDtypeStruct((CH, 27 * CH), F32),
            jax.ShapeDtypeStruct((CH, 27 * CH), F32),
        ),
        in_specs=[any_space] * 4 + [vmem] * 5,
        out_specs=(any_space,) * 3,
        scratch_shapes=scratch,
        compiler_params=pltpu.CompilerParams(
            collective_id=0, has_side_effects=True, vmem_limit_bytes=60 * 1024 * 1024
        ),
    )(
        latent, cotangent, conv_first, conv_second, exponents[None],
        gain_first[None], shift_first[None], gain_second[None], shift_second[None],
    )


def solution(mesh):
    nz, nh = mesh.shape["tm"], mesh.shape["height"]
    nx = int(round(nh**0.5))
    placed = P(None, "tm", "height", "width")
    return jax.shard_map(
        functools.partial(shards, (nz, nh, nx, nh // nx)),
        mesh=mesh,
        in_specs=(placed, P(), placed, P(), P(), P(), P(), P(), P()),
        out_specs=(placed, P(), P()),
        check_vma=False,
    )
```

```python
import functools

import jax
import jax.numpy as jnp
from jax import lax
from jax.experimental import pallas as pl
from jax.experimental.pallas import tpu as pltpu
from jax.sharding import PartitionSpec as P

MESH = pl.DeviceIdType.MESH
EPS = 1e-05
CH = 128
F32 = jnp.float32
BF16 = jnp.bfloat16


def group_sum(row):
    lane = lax.broadcasted_iota(jnp.int32, row.shape, 1)
    pair = row + jnp.where(lane % 2 == 0, pltpu.roll(row, CH - 1, 1), pltpu.roll(row, 1, 1))
    return pair + jnp.where(lane % 4 < 2, pltpu.roll(pair, CH - 2, 1), pltpu.roll(pair, 2, 1))


def fold_rows(cells):
    return jnp.sum(cells.reshape(-1, 8, CH), axis=0)


def total_row(partial):
    return jnp.sum(partial, axis=0, keepdims=True)


def lanes_low(row):
    return lax.broadcasted_iota(jnp.int32, row.shape, row.ndim - 1) % 4 < 2


def pack_pair(first, second):
    return jnp.where(lanes_low(first), first, second)


def unpack_pair(row):
    low = lanes_low(row)
    return jnp.where(low, row, pltpu.roll(row, 2, 1)), jnp.where(low, pltpu.roll(row, CH - 2, 1), row)


def far_first(n, size):
    if size == 4:
        return (2 + 3 * n + 3 * ((n * (n - 1)) // 2)) % 4
    return size - 1 - n


def sigmoid(value):
    return 1.0 / (1.0 + jnp.exp(-value))


def body(
    sizes,
    x_hbm, c_hbm, w1_hbm, w2_hbm, exponent_ref, gain1_ref, shift1_ref, gain2_ref, shift2_ref,
    out_hbm, o1_hbm, o2_hbm,
    x_raw, c_raw, xl, cl, w1, w2, out_ref, o1_ref, o2_ref, fin1, fin2,
    xr, cr, xe, ce, xeb, ceb, xex, cex, s1, sc, sh, hid, g2, g1, nrm, act_t, hg_t, hg, eh, heb,
    wf1, wb1, wb2, s_out, s_in, rb, a, r0, b1, r1, b2, r2, r3, g3,
    load_sem, store_sem, in_send, in_recv, red_send, red_recv, halo_send, halo_recv, back_send, back_recv,
    ar_send, ar_recv,
):
    nz, nh, nx, ny = sizes
    ns = nx
    fl, rl, cols = xl.shape[0], xl.shape[1], xl.shape[2]
    strip = cols // nz
    frames = fl * nz
    cells = rl * strip
    z, h, w = lax.axis_index("tm"), lax.axis_index("height"), lax.axis_index("width")
    hx, hy = h // ny, h % ny

    def dev(dz, dh, dw):
        return (lax.rem(z + dz + nz, nz), lax.rem(h + dh + nh, nh), lax.rem(w + dw, 2))

    loads = [
        pltpu.make_async_copy(source, target, load_sem.at[n])
        for n, (source, target) in enumerate(((x_hbm, x_raw), (c_hbm, c_raw), (w1_hbm, w1), (w2_hbm, w2)))
    ]
    for copy in loads:
        copy.start()

    heights = [(ox, oy) for ox in range(nx) for oy in range(ny)]
    heights.sort(key=lambda place: -(min(place[0], nx - place[0]) + min(place[1], ny - place[1])))
    targets_h = [lax.rem(hx + ox, nx) * ny + lax.rem(hy + oy, ny) for ox, oy in heights]

    def for_each_device(act):
        def step(n, _):
            dz, dw = far_first(n // 2, nz), 1 - n % 2
            zt, wt = lax.rem(z + dz, nz), lax.rem(w + dw, 2)
            for ht in targets_h[:-1]:
                act((zt, ht, wt))

            @pl.when(n < 2 * nz - 1)
            def _():
                act((zt, h, wt))

            return 0

        lax.fori_loop(0, 2 * nz, step, 0)

    devices = 2 * nz * nh
    barrier = pltpu.get_barrier_semaphore()
    for dz in reversed(range(nz)):
        for dw in (1, 0):
            zt, wt = lax.rem(z + dz, nz), lax.rem(w + dw, 2)
            for ht in targets_h if (dz, dw) != (0, 0) else targets_h[:-1]:
                pl.semaphore_signal(barrier, inc=1, device_id=(zt, ht, wt), device_id_type=MESH)

    def take(ref, sem):
        pltpu.make_async_copy(ref, ref, sem).wait()

    def remote(src, dst, send, recv, where):
        return pltpu.make_async_remote_copy(
            src_ref=src, dst_ref=dst, send_sem=send, recv_sem=recv, device_id=where, device_id_type=MESH
        )

    own_frames = pl.ds(z * fl, fl)
    row_parts = {0: ((0, rl), (1, rl)), 1: ((rl - 1, 1), (0, 1)), -1: ((0, 1), (rl + 1, 1))}

    def main_copies(k, src, dst):
        copies = []
        for dz in range(nz):
            q = lax.rem(z + dz, nz)
            for n, dh in enumerate((0, 1, -1)):
                (r_from, count), (r_to, _) = row_parts[dh]
                source = src.at[:, pl.ds(r_from, count), pl.ds(pl.multiple_of(q * strip, strip), strip), :]
                target = dst.at[own_frames, pl.ds(r_to, count)]
                if dz == 0 and dh == 0:
                    copies.append(pltpu.make_async_copy(source, target, in_recv.at[k, 0]))
                else:
                    copies.append(remote(source, target, in_send.at[k], in_recv.at[k, dz], dev(dz, dh, 0)))
        return copies

    def build_edges(src, edges):
        def at(f, r, col):
            start = (col // 16) * 16
            return src[f, r, start : start + 16, :].astype(F32)[col % 16 : col % 16 + 1]

        place = lax.broadcasted_iota(jnp.int32, (16, CH), 0)
        for f in range(fl):
            for q in range(nz):
                tile = jnp.zeros((16, CH), F32)
                for r in range(rl):
                    if q > 0:
                        tile = jnp.where(place == 2 * r, at(f, r, q * strip - 1), tile)
                    if q < nz - 1:
                        tile = jnp.where(place == 2 * r + 1, at(f, r, (q + 1) * strip), tile)
                edges[q, f] = tile.astype(BF16)
            tile = jnp.zeros((16, CH), F32)
            for r in range(rl):
                outer = jnp.where(w == 0, at(f, r, cols - 1), at(f, r, 0))
                tile = jnp.where(place // 2 == r, outer, tile)
            edges[nz, f] = tile.astype(BF16)

    def edge_copies(k, edges, landing, landing_out):
        copies = []
        for dz in range(nz):
            q = lax.rem(z + dz, nz)
            for n, dh in enumerate((0, 1, -1)):
                source = edges.at[q]
                target = landing.at[1 - dh, own_frames]
                if dz == 0 and dh == 0:
                    copies.append(pltpu.make_async_copy(source, target, in_recv.at[k, nz]))
                else:
                    copies.append(remote(source, target, in_send.at[k], in_recv.at[k, nz + dz], dev(dz, dh, 0)))
        return copies

    outer_q = (nz - 1) * w
    takes_outer = z == (nz - 1) * (1 - w)

    def outer_sends(k, edges, landing_out):
        copies = []
        recv = in_recv.at[k, 2 * nz + lax.rem(outer_q - z + nz, nz)]
        for dh in (0, 1, -1):
            where = (outer_q, lax.rem(h + dh + nh, nh), 1 - w)
            copies.append(remote(edges.at[nz], landing_out.at[1 - dh, own_frames], in_send.at[k], recv, where))
        return copies

    near_first = sorted(range(nz), key=lambda dz: min(dz, nz - dz))

    def pair_from(dz):
        return lax.rem(z - dz + nz, nz) * fl

    def wait_pair(k, dz, cells_in, landing, landing_out):
        pair = pl.ds(pair_from(dz), fl)
        take(cells_in.at[pair], in_recv.at[k, dz])
        take(landing.at[:, pair], in_recv.at[k, nz + dz])

        @pl.when(takes_outer)
        def _():
            take(landing_out.at[:, pair], in_recv.at[k, 2 * nz + dz])

    def start_all(copies):
        for copy in copies:
            copy.start()

    def wait_sends(copies):
        for copy in copies:
            copy.wait_send()

    me = (z * nh + h) * 2 + w
    local_size = 4.0 * fl * rl * cols
    total_size = local_size * devices

    def red_start(k, first, second):
        rb[k, me] = pack_pair(first, second)
        slot = rb.at[k, me]
        for_each_device(lambda where: remote(slot, slot, red_send.at[k], red_recv.at[k], where).start())

    def red_wait(k):
        take(rb.at[k, pl.ds(0, devices - 1)], red_recv.at[k])

    def moments_end(k):
        red_wait(k)
        rows = rb[k]
        mean, _ = unpack_pair(jnp.sum(rows, axis=0) / devices)
        low = lanes_low(rows)
        off = rows - jnp.where(lanes_low(mean), mean, 0.0)[None]
        between, within = unpack_pair(jnp.sum(jnp.where(low, off * off, off), axis=0))
        return mean, within + local_size * between

    def sums_end(k):
        red_wait(k)
        return unpack_pair(jnp.sum(rb[k], axis=0) / total_size)

    def turn(source, target):
        for f in range(fl):
            for r in range(rl):
                target[f, r] = jnp.transpose(source[:, f, r, :].astype(F32)).astype(BF16)

    loads[0].wait()
    turn(x_raw, xl)
    build_edges(xl, xe)
    zero8 = jnp.zeros((8, CH), F32)

    def x_sum(n, total):
        return total + fold_rows(xl[n // rl, n % rl].astype(F32))

    local_mean = group_sum(total_row(lax.fori_loop(0, fl * rl, x_sum, zero8))) / local_size

    def x_spread(n, total):
        off = xl[n // rl, n % rl].astype(F32) - local_mean
        return total + fold_rows(off * off)

    local_spread = group_sum(total_row(lax.fori_loop(0, fl * rl, x_spread, zero8)))

    loads[1].wait()
    turn(c_raw, cl)
    build_edges(cl, ce)
    loads[2].wait()
    loads[3].wait()
    for kt in range(3):
        for kr in range(3):
            for kc in range(3):
                tap = 9 * kt + 3 * kr + kc
                back = ((2 - kr) * 3 + (2 - kc)) * CH
                for source, target in ((w1, wb1), (w2, wb2)):
                    target[back : back + CH, kt * CH : (kt + 1) * CH] = source[:, tap * CH : (tap + 1) * CH]
    for kt in range(3):
        for kr in range(3):
            for kc in range(3):
                tap = 9 * kt + 3 * kr + kc
                ahead = (kr * 3 + kc) * CH
                block = w1[:, tap * CH : (tap + 1) * CH].astype(F32)
                wf1[ahead : ahead + CH, (2 - kt) * CH : (3 - kt) * CH] = jnp.transpose(block).astype(BF16)
    pl.semaphore_wait(barrier, devices - 1)
    x_main = main_copies(0, xl, xr)
    x_edge = edge_copies(0, xe, xeb, xex)
    x_outer = outer_sends(0, xe, xex)
    start_all(x_main + x_edge + x_outer)
    red_start(0, local_mean, local_spread)
    c_main = main_copies(1, cl, cr)
    c_edge = edge_copies(1, ce, ceb, cex)
    c_outer = outer_sends(1, ce, cex)
    start_all(c_main + c_edge + c_outer)
    zero_cells = jnp.zeros((cells, CH), F32)

    def clear(n, _):
        hid[n] = zero_cells
        g2[n] = zero_cells
        g1[n] = zero_cells
        return 0

    lax.fori_loop(0, frames + 2, clear, 0)
    zero_t = jnp.zeros((2 * CH, cells), BF16)
    act_t[0 : 2 * CH] = zero_t
    hg_t[frames * CH : (frames + 2) * CH] = zero_t

    row_place = lax.broadcasted_iota(jnp.int32, (strip, CH), 0)
    left_ok = jnp.logical_not(jnp.logical_and(w == 0, z == 0))
    right_ok = jnp.logical_not(jnp.logical_and(w == 1, z == nz - 1))

    def row_ok(r):
        if r == 0:
            return h > 0
        if r == rl + 1:
            return h < nh - 1
        return None

    def row_source(r):
        if r == 0:
            return 0, rl - 1
        if r == rl + 1:
            return 2, 0
        return 1, r - 1

    def store_stack(stack, f, r, value, left, right):
        ok = row_ok(r)
        left = jnp.where(left_ok if ok is None else jnp.logical_and(left_ok, ok), left, 0.0)
        right = jnp.where(right_ok if ok is None else jnp.logical_and(right_ok, ok), right, 0.0)
        if ok is not None:
            value = jnp.where(ok, value, 0.0)
        before = jnp.where(row_place == 0, left, pltpu.roll(value, 1, 0))
        after = jnp.where(row_place == strip - 1, right, pltpu.roll(value, strip - 1, 0))
        stack[f, r, :, 0:CH] = before.astype(BF16)
        stack[f, r, :, CH : 2 * CH] = value.astype(BF16)
        stack[f, r, :, 2 * CH : 3 * CH] = after.astype(BF16)

    edge_place = lax.broadcasted_iota(jnp.int32, (16, CH), 0)
    outer_mask = jnp.logical_and(takes_outer, edge_place % 2 == 1 - w)

    def input_stack(stack, source, landing, landing_out, apply, start):
        def step(f, _):
            edges = []
            for d in range(3):
                tile = jnp.where(outer_mask, landing_out[d, f].astype(F32), landing[d, f].astype(F32))
                edges.append(apply(tile))
            for r in range(rl + 2):
                d, row = row_source(r)
                tile = edges[d]
                store_stack(
                    stack, f, r, apply(source[f, r].astype(F32)),
                    tile[2 * row : 2 * row + 1], tile[2 * row + 1 : 2 * row + 2],
                )
            return 0

        lax.fori_loop(start, start + fl, step, 0)

    def window(stack, f):
        return [stack[f, kr : kr + rl].reshape(cells, 3 * CH) for kr in range(3)]

    def convolve(stack, weight, target, first=0, last=None):
        def step(f, _):
            product = jnp.dot(
                jnp.concatenate(window(stack, f), axis=1), weight[...], preferred_element_type=F32
            )
            for j in range(3):
                target[f + j] += product[:, j * CH : (j + 1) * CH]
            return 0

        lax.fori_loop(first, frames if last is None else last, step, 0)

    def weight_part(turned, stack, kr):
        left = jnp.concatenate([turned[f * CH : (f + 3) * CH, :] for f in range(frames)], axis=1)
        right = stack[:, kr : kr + rl].reshape(frames * cells, 3 * CH)
        return jnp.dot(left, right, preferred_element_type=F32)

    def peer(axis, j):
        if axis == "z":
            return dev(j, 0, 0)
        if axis == "x":
            return (z, lax.rem(hx + j, nx) * ny + hy, w)
        return (z, hx * ny + lax.rem(hy + j, ny), w)

    coords = {"z": z, "x": hx, "y": hy}
    orders = (("z", "y", "x"), ("y", "x", "z"), ("x", "z", "y"))
    half = 8
    span = half // ns
    tiles = span * 9
    piece = -(-tiles // ns)
    outs = (o1_ref, o2_ref)
    stage_at = {"core": 0, "a1": 1, "a2": 2, "a3": 3, "g2": 4, "g1": 5, "gc": 6}

    def sems(g, p, stage):
        return ar_send.at[g], ar_recv.at[g, p, stage_at[stage]]

    def arrived(g, p, stage, ref):
        take(ref, ar_recv.at[g, p, stage_at[stage]])

    def core_copy(g, p):
        return remote(a.at[g, p, pl.ds((1 - w) * half, half)], r0.at[g, p], *sems(g, p, "core"), dev(0, 0, 1))

    def core_start(g, p):
        core_copy(g, p).start()

    def a1_copies(g, p):
        axis = orders[p][0]
        return [
            remote(
                b1.at[g, p, pl.ds(lax.rem(coords[axis] + j, ns) * span, span)], r1.at[g, p, j - 1],
                *sems(g, p, "a1"), peer(axis, j),
            )
            for j in range(1, ns)
        ]

    def a1_start(g, p):
        arrived(g, p, "core", r0.at[g, p])
        b1[g, p] = a[g, p, pl.ds(w * half, half)] + r0[g, p]
        start_all(a1_copies(g, p))

    def a2_copies(g, p):
        axis = orders[p][1]
        return [
            remote(
                b2.at[g, p, pl.ds(lax.rem(coords[axis] + j, ns) * piece, piece)], r2.at[g, p, j - 1],
                *sems(g, p, "a2"), peer(axis, j),
            )
            for j in range(1, ns)
        ]

    def a2_start(g, p):
        arrived(g, p, "a1", r1.at[g, p])
        value = b1[g, p, pl.ds(coords[orders[p][0]] * span, span)]
        for j in range(ns - 1):
            value = value + r1[g, p, j]
        b2[g, p, 0:tiles] = value.reshape(tiles, 8, CH)
        if piece * ns > tiles:
            b2[g, p, tiles:] = jnp.zeros((piece * ns - tiles, 8, CH), F32)
        start_all(a2_copies(g, p))

    def a3_copies(g, p):
        axis = orders[p][2]
        slot = r3.at[g, p, coords[axis]]
        return [remote(slot, slot, *sems(g, p, "a3"), peer(axis, j)) for j in range(1, ns)]

    def a3_start(g, p):
        arrived(g, p, "a2", r2.at[g, p])
        value = b2[g, p, pl.ds(coords[orders[p][1]] * piece, piece)]
        for j in range(ns - 1):
            value = value + r2[g, p, j]
        r3[g, p, coords[orders[p][2]]] = value
        start_all(a3_copies(g, p))

    def g2_copies(g, p):
        axis = orders[p][1]
        part = g3.at[g, p, pl.ds(coords[axis] * piece, piece)]
        return [remote(part, part, *sems(g, p, "g2"), peer(axis, j)) for j in range(1, ns)]

    def g2_start(g, p):
        arrived(g, p, "a3", r3.at[g, p, pl.ds(0, ns - 1)])
        value = r3[g, p, 0]
        for n in range(1, ns):
            value = value + r3[g, p, n]
        g3[g, p, pl.ds(coords[orders[p][1]] * piece, piece)] = value
        start_all(g2_copies(g, p))

    def out_span(g, p, n):
        return outs[g].at[p, pl.ds(w * half + n * span, span)]

    def g1_copies(g, p):
        axis = orders[p][0]
        part = out_span(g, p, coords[axis])
        return [remote(part, part, *sems(g, p, "g1"), peer(axis, j)) for j in range(1, ns)]

    def gc_copy(g, p, j):
        part = out_span(g, p, lax.rem(coords[orders[p][0]] + ns - j, ns))
        return remote(part, part, *sems(g, p, "gc"), dev(0, 0, 1))

    def g1_start(g, p):
        arrived(g, p, "g2", g3.at[g, p, pl.ds(0, (ns - 1) * piece)])
        outs[g][p, pl.ds(w * half + coords[orders[p][0]] * span, span)] = g3[g, p, 0:tiles].reshape(span, 9, 8, CH)
        start_all(g1_copies(g, p))
        gc_copy(g, p, 0).start()

    def gc_start(g, p):
        arrived(g, p, "g1", outs[g].at[p, pl.ds(0, (ns - 1) * span)])
        for j in range(1, ns):
            gc_copy(g, p, j).start()

    def store_copy(g):
        return pltpu.make_async_copy((fin1, fin2)[g], (o1_hbm, o2_hbm)[g], store_sem.at[1 + g])

    def gc_end(g, p):
        arrived(g, p, "gc", outs[g].at[p, pl.ds(0, half)])
        for kt in range(3):
            for kc in range(3):
                block = outs[g][p, :, kt * 3 + kc].reshape(CH, CH)
                tap = 9 * kt + 3 * p + kc
                (fin1, fin2)[g][:, tap * CH : (tap + 1) * CH] = block if g == 0 else jnp.transpose(block)

    def ar_close(g):
        for p in range(3):
            wait_sends([core_copy(g, p)] + a1_copies(g, p) + a2_copies(g, p) + a3_copies(g, p))
            wait_sends(g2_copies(g, p) + g1_copies(g, p) + [gc_copy(g, p, j) for j in range(ns)])

    def each(stage, g):
        for p in range(3):
            stage(g, p)

    mean1, spread1 = moments_end(0)
    picks = lax.broadcasted_iota(jnp.int32, (CH // 4, CH), 1) // 4 == lax.broadcasted_iota(jnp.int32, (CH // 4, CH), 0)
    spread_exponent = jnp.dot(
        jnp.broadcast_to(exponent_ref[...].astype(F32), (8, CH // 4)), picks.astype(F32), preferred_element_type=F32
    )
    scale = jnp.exp2(spread_exponent[0:1])
    inv1 = 1.0 / jnp.sqrt(spread1 * (scale * scale) / total_size + EPS)
    factor1 = scale * inv1
    gain1, shift1 = gain1_ref[...], shift1_ref[...]
    gain2, shift2 = gain2_ref[...], shift2_ref[...]

    def rounded(value):
        return value.astype(BF16).astype(F32)

    def act_first(value):
        pre = (value - mean1) * factor1 * gain1 + shift1
        return rounded(pre * sigmoid(pre))

    for dz in near_first:
        wait_pair(0, dz, xr, xeb, xex)
        start = pair_from(dz)
        input_stack(s1, xr, xeb, xex, act_first, start)
        convolve(s1, wf1, hid, start, start + fl)

    def hid_sum(n, total):
        return total + fold_rows(hid[n])

    mean_l = group_sum(total_row(lax.fori_loop(0, frames, hid_sum, zero8))) / local_size

    def hid_spread(n, total):
        off = hid[n] - mean_l
        return total + fold_rows(off * off)

    red_start(1, mean_l, group_sum(total_row(lax.fori_loop(0, frames, hid_spread, zero8))))

    for dz in near_first:
        wait_pair(1, dz, cr, ceb, cex)
        start = pair_from(dz)
        input_stack(sc, cr, ceb, cex, lambda value: value, start)
        convolve(sc, wb2, g2, start, start + fl)
    mean2, spread2 = moments_end(1)
    inv2 = 1.0 / jnp.sqrt(spread2 / total_size + EPS)

    def second(n, totals):
        first_total, second_total = totals
        normed = (hid[n] - mean2) * inv2
        pre = normed * gain2 + shift2
        sig = sigmoid(pre)
        act_t[pl.ds(pl.multiple_of((n + 2) * CH, CH), CH), :] = jnp.transpose(pre * sig).astype(BF16)
        scaled = g2[n + 2] * (sig * (1.0 + pre * (1.0 - sig))) * gain2
        nrm[n] = normed
        g2[n + 2] = scaled
        return first_total + fold_rows(scaled), second_total + fold_rows(scaled * normed)

    t1, t2 = lax.fori_loop(0, frames, second, (zero8, zero8))
    red_start(2, group_sum(total_row(t1)), group_sum(total_row(t2)))

    def put_second(kr):
        block = weight_part(act_t, sc, kr)
        for kt in range(3):
            for kc in range(3):
                part = block[kt * CH : (kt + 1) * CH, kc * CH : (kc + 1) * CH]
                a[1, 2 - kr, :, kt * 3 + (2 - kc)] = part.reshape(16, 8, CH)
        core_start(1, 2 - kr)

    for kr in range(3):
        put_second(kr)
    each(a1_start, 1)
    m1, m2 = sums_end(2)

    def hidden(n, _):
        value = inv2 * (g2[n + 2] - m1 - nrm[n] * m2)
        hg_t[pl.ds(pl.multiple_of(n * CH, CH), CH), :] = jnp.transpose(value).astype(BF16)
        narrow = value.astype(BF16)
        hg[n, 1 : rl + 1] = narrow.reshape(rl, strip, CH)
        wide = narrow.astype(F32).reshape(rl, strip, CH)
        lefts = jnp.zeros((16, CH), F32)
        rights = jnp.zeros((16, CH), F32)
        for r in range(rl):
            lefts = jnp.where(edge_place == r, wide[r, 0:1], lefts)
            rights = jnp.where(edge_place == r, wide[r, strip - 1 : strip], rights)
        eh[0, n] = lefts.astype(BF16)
        eh[1, n] = rights.astype(BF16)
        return 0

    lax.fori_loop(0, frames, hidden, 0)

    line = w * nz + z

    def beside(ds, dh):
        place = lax.rem(line + ds + 2 * nz, 2 * nz)
        return (lax.rem(place, nz), lax.rem(h + dh + nh, nh), place // nz)

    halo = [
        remote(hg.at[:, pl.ds(rl, 1)], hg.at[:, pl.ds(0, 1)], halo_send.at[0], halo_recv.at[0], dev(0, 1, 0)),
        remote(hg.at[:, pl.ds(1, 1)], hg.at[:, pl.ds(rl + 1, 1)], halo_send.at[0], halo_recv.at[0], dev(0, -1, 0)),
    ]
    for n, dh in enumerate((0, 1, -1)):
        halo.append(remote(eh.at[0], heb.at[1 - dh, 1], halo_send.at[0], halo_recv.at[1], beside(-1, dh)))
        halo.append(remote(eh.at[1], heb.at[1 - dh, 0], halo_send.at[0], halo_recv.at[1], beside(1, dh)))
    start_all(halo)

    def put_first(kr):
        block = weight_part(hg_t, s1, kr)
        for j in range(3):
            for kc in range(3):
                part = block[j * CH : (j + 1) * CH, kc * CH : (kc + 1) * CH]
                a[0, kr, :, (2 - j) * 3 + kc] = part.reshape(16, 8, CH)
        core_start(0, kr)

    put_first(0)
    put_first(1)
    a1_start(0, 0)
    put_first(2)
    a1_start(0, 1)
    a1_start(0, 2)
    take(hg.at[:, pl.ds(0, 2)], halo_recv.at[0])
    take(heb, halo_recv.at[1])

    def halo_stack(f, _):
        lefts = [heb[d, 0, f].astype(F32) for d in range(3)]
        rights = [heb[d, 1, f].astype(F32) for d in range(3)]
        for r in range(rl + 2):
            d, row = row_source(r)
            store_stack(sh, f, r, hg[f, r].astype(F32), lefts[d][row : row + 1], rights[d][row : row + 1])
        return 0

    lax.fori_loop(0, frames, halo_stack, 0)
    each(a2_start, 1)

    def first(f, totals):
        first_total, second_total = totals
        for r in range(rl):
            normed = (xr[f, r + 1].astype(F32) - mean1) * factor1
            pre = normed * gain1 + shift1
            sig = sigmoid(pre)
            scaled = g1[f + 2, r * strip : (r + 1) * strip] * (sig * (1.0 + pre * (1.0 - sig))) * gain1
            s_out[f, r] = scaled.astype(BF16)
            first_total = first_total + fold_rows(scaled)
            second_total = second_total + fold_rows(scaled * normed)
        return first_total, second_total

    back_from = s_in.at[:, :, pl.ds(pl.multiple_of(z * strip, strip), strip), :]
    back_copies = []

    def send_back(q):
        source = s_out.at[pl.ds(q * fl, fl)]
        far = remote(source, back_from, back_send.at[0], back_recv.at[0], (q, h, w))
        back_copies.append(far)

        @pl.when(z == q)
        def _():
            pltpu.make_async_copy(source, back_from, back_recv.at[0]).start()

        @pl.when(z != q)
        def _():
            far.start()

    convolve(sh, wb1, g1, 0, 2)
    totals = (zero8, zero8)
    for q in range(nz):
        if q * fl + 2 < frames:
            convolve(sh, wb1, g1, q * fl + 2, q * fl + fl + 2)
        totals = lax.fori_loop(q * fl, q * fl + fl, first, totals)
        send_back(q)
        if q == nz // 2 - 1:
            each(a2_start, 0)
            each(a3_start, 1)
    t1, t2 = totals
    red_start(3, group_sum(total_row(t1)), group_sum(total_row(t2)))
    each(a3_start, 0)
    each(g2_start, 1)
    each(g2_start, 0)
    each(g1_start, 1)
    m1, m2 = sums_end(3)
    take(s_in, back_recv.at[0])

    def out_copy(f):
        return pltpu.make_async_copy(out_ref.at[:, f], out_hbm.at[:, f], store_sem.at[0])

    for f in range(fl):
        for r in range(rl):
            normed = (xl[f, r].astype(F32) - mean1) * factor1
            value = cl[f, r].astype(F32) + inv1 * (s_in[f, r].astype(F32) - m1 - normed * m2)
            out_ref[:, f, r, :] = jnp.transpose(value)
        out_copy(f).start()
    each(g1_start, 0)
    each(gc_start, 1)
    each(gc_end, 1)
    store_copy(1).start()
    wait_sends(x_main[1:] + x_edge[1:] + x_outer)
    wait_sends(c_main[1:] + c_edge[1:] + c_outer)
    for k in range(4):
        take(rb.at[k, pl.ds(0, devices - 1)], red_send.at[k])
    wait_sends(halo)
    for q in range(nz):

        @pl.when(z != q)
        def _():
            back_copies[q].wait_send()

    ar_close(1)
    each(gc_start, 0)
    each(gc_end, 0)
    store_copy(0).start()
    ar_close(0)
    for f in range(fl):
        out_copy(f).wait()
    store_copy(0).wait()
    store_copy(1).wait()


def copy_body(*refs):
    sources, targets, held = refs[0:3], refs[3:6], refs[6:9]
    load_sem, store_sem = refs[9:]
    loads = [pltpu.make_async_copy(sources[n], held[n], load_sem.at[n]) for n in range(3)]
    stores = [pltpu.make_async_copy(held[n], targets[n], store_sem.at[n]) for n in range(3)]
    for copy in loads:
        copy.start()
    for n in range(3):
        loads[n].wait()
        stores[n].start()
    for copy in stores:
        copy.wait()


def shards(sizes, latent, exponents, cotangent, conv_first, conv_second, gain_first, shift_first, gain_second, shift_second):
    nz, nh, nx, ny = sizes
    channels, fl, rl, cols = latent.shape
    strip = cols // nz
    frames = fl * nz
    cells = rl * strip
    ns = nx
    span = 8 // ns
    tiles = span * 9
    piece = -(-tiles // ns)
    vmem = pl.BlockSpec(memory_space=pltpu.VMEM)
    any_space = pl.BlockSpec(memory_space=pl.ANY)
    part = (3, 16, 9, 8, CH)
    wide = (frames, rl + 2, strip, 3 * CH)
    scratch = [
        pltpu.VMEM((CH, fl, rl, cols), BF16),
        pltpu.VMEM((CH, fl, rl, cols), BF16),
        pltpu.VMEM((fl, rl, cols, CH), BF16),
        pltpu.VMEM((fl, rl, cols, CH), BF16),
        pltpu.VMEM((CH, 27 * CH), BF16),
        pltpu.VMEM((CH, 27 * CH), BF16),
        pltpu.VMEM((CH, fl, rl, cols), F32),
        pltpu.VMEM(part, F32),
        pltpu.VMEM(part, F32),
        pltpu.VMEM((CH, 27 * CH), F32),
        pltpu.VMEM((CH, 27 * CH), F32),
        pltpu.VMEM((frames, rl + 2, strip, CH), BF16),
        pltpu.VMEM((frames, rl + 2, strip, CH), BF16),
        pltpu.VMEM((nz + 1, fl, 16, CH), BF16),
        pltpu.VMEM((nz + 1, fl, 16, CH), BF16),
        pltpu.VMEM((3, frames, 16, CH), BF16),
        pltpu.VMEM((3, frames, 16, CH), BF16),
        pltpu.VMEM((3, frames, 16, CH), BF16),
        pltpu.VMEM((3, frames, 16, CH), BF16),
        pltpu.VMEM(wide, BF16),
        pltpu.VMEM(wide, BF16),
        pltpu.VMEM(wide, BF16),
        pltpu.VMEM((frames + 2, cells, CH), F32),
        pltpu.VMEM((frames + 2, cells, CH), F32),
        pltpu.VMEM((frames + 2, cells, CH), F32),
        pltpu.VMEM((frames, cells, CH), F32),
        pltpu.VMEM(((frames + 2) * CH, cells), BF16),
        pltpu.VMEM(((frames + 2) * CH, cells), BF16),
        pltpu.VMEM((frames, rl + 2, strip, CH), BF16),
        pltpu.VMEM((2, frames, 16, CH), BF16),
        pltpu.VMEM((3, 2, frames, 16, CH), BF16),
        pltpu.VMEM((9 * CH, 3 * CH), BF16),
        pltpu.VMEM((9 * CH, 3 * CH), BF16),
        pltpu.VMEM((9 * CH, 3 * CH), BF16),
        pltpu.VMEM((frames, rl, strip, CH), BF16),
        pltpu.VMEM((fl, rl, cols, CH), BF16),
        pltpu.VMEM((4, 2 * nz * nh, 1, CH), F32),
        pltpu.VMEM((2, 3, 16, 9, 8, CH), F32),
        pltpu.VMEM((2, 3, 8, 9, 8, CH), F32),
        pltpu.VMEM((2, 3, 8, 9, 8, CH), F32),
        pltpu.VMEM((2, 3, ns - 1, span, 9, 8, CH), F32),
        pltpu.VMEM((2, 3, piece * ns, 8, CH), F32),
        pltpu.VMEM((2, 3, ns - 1, piece, 8, CH), F32),
        pltpu.VMEM((2, 3, ns, piece, 8, CH), F32),
        pltpu.VMEM((2, 3, piece * ns, 8, CH), F32),
        pltpu.SemaphoreType.DMA((4,)),
        pltpu.SemaphoreType.DMA((3,)),
        pltpu.SemaphoreType.DMA((2,)),
        pltpu.SemaphoreType.DMA((2, 3 * nz)),
        pltpu.SemaphoreType.DMA((4,)),
        pltpu.SemaphoreType.DMA((4,)),
        pltpu.SemaphoreType.DMA((1,)),
        pltpu.SemaphoreType.DMA((2,)),
        pltpu.SemaphoreType.DMA((1,)),
        pltpu.SemaphoreType.DMA((1,)),
        pltpu.SemaphoreType.DMA((2,)),
        pltpu.SemaphoreType.DMA((2, 3, 7)),
    ]
    results = pl.pallas_call(
        functools.partial(body, sizes),
        out_shape=(
            jax.ShapeDtypeStruct((CH, fl, rl, cols), F32),
            jax.ShapeDtypeStruct((CH, 27 * CH), F32),
            jax.ShapeDtypeStruct((CH, 27 * CH), F32),
        ),
        in_specs=[any_space] * 4 + [vmem] * 5,
        out_specs=(any_space,) * 3,
        scratch_shapes=scratch,
        compiler_params=pltpu.CompilerParams(
            collective_id=0, has_side_effects=True, vmem_limit_bytes=60 * 1024 * 1024
        ),
    )(
        latent, cotangent, conv_first, conv_second, exponents[None],
        gain_first[None], shift_first[None], gain_second[None], shift_second[None],
    )
    return pl.pallas_call(
        copy_body,
        out_shape=[jax.ShapeDtypeStruct(value.shape, F32) for value in results],
        in_specs=[any_space] * 3,
        out_specs=[any_space] * 3,
        scratch_shapes=[pltpu.VMEM(value.shape, F32) for value in results]
        + [pltpu.SemaphoreType.DMA((3,)), pltpu.SemaphoreType.DMA((3,))],
        compiler_params=pltpu.CompilerParams(vmem_limit_bytes=60 * 1024 * 1024),
    )(*results)


def solution(mesh):
    nz, nh = mesh.shape["tm"], mesh.shape["height"]
    nx = int(round(nh**0.5))
    placed = P(None, "tm", "height", "width")
    return jax.shard_map(
        functools.partial(shards, (nz, nh, nx, nh // nx)),
        mesh=mesh,
        in_specs=(placed, P(), placed, P(), P(), P(), P(), P(), P()),
        out_specs=(placed, P(), P()),
        check_vma=False,
    )
```

```python
import functools

import jax
import jax.numpy as jnp
from jax import lax
from jax.experimental import pallas as pl
from jax.experimental.pallas import tpu as pltpu
from jax.sharding import PartitionSpec as P

MESH = pl.DeviceIdType.MESH
EPS = 1e-05
CH = 128
F32 = jnp.float32
BF16 = jnp.bfloat16


def group_sum(row):
    lane = lax.broadcasted_iota(jnp.int32, row.shape, 1)
    pair = row + jnp.where(lane % 2 == 0, pltpu.roll(row, CH - 1, 1), pltpu.roll(row, 1, 1))
    return pair + jnp.where(lane % 4 < 2, pltpu.roll(pair, CH - 2, 1), pltpu.roll(pair, 2, 1))


def fold_rows(cells):
    return jnp.sum(cells.reshape(-1, 8, CH), axis=0)


def total_row(partial):
    return jnp.sum(partial, axis=0, keepdims=True)


def lanes_low(row):
    return lax.broadcasted_iota(jnp.int32, row.shape, row.ndim - 1) % 4 < 2


def pack_pair(first, second):
    return jnp.where(lanes_low(first), first, second)


def unpack_pair(row):
    low = lanes_low(row)
    return jnp.where(low, row, pltpu.roll(row, 2, 1)), jnp.where(low, pltpu.roll(row, CH - 2, 1), row)


def far_first(n, size):
    if size == 4:
        return (2 + 3 * n + 3 * ((n * (n - 1)) // 2)) % 4
    return size - 1 - n


def sigmoid(value):
    return 1.0 / (1.0 + jnp.exp(-value))


def body(
    sizes,
    x_hbm, c_hbm, w1_hbm, w2_hbm, exponent_ref, gain1_ref, shift1_ref, gain2_ref, shift2_ref,
    out_hbm, o1_hbm, o2_hbm,
    x_raw, c_raw, xl, cl, w1, w2, out_ref, o1_ref, o2_ref, fin1, fin2,
    xr, cr, xe, ce, xeb, ceb, xex, cex, s1, sc, sh, hid, g2, g1, nrm, act_t, hg_t, hg, eh, heb,
    wf1, wb1, wb2, s_out, s_in, rb, a, r0, b1, r1, b2, r2, r3, g3,
    load_sem, store_sem, in_send, in_recv, red_send, red_recv, halo_send, halo_recv, back_send, back_recv,
    ar_send, ar_recv,
):
    nz, nh, nx, ny = sizes
    ns = nx
    fl, rl, cols = xl.shape[0], xl.shape[1], xl.shape[2]
    strip = cols // nz
    frames = fl * nz
    cells = rl * strip
    z, h, w = lax.axis_index("tm"), lax.axis_index("height"), lax.axis_index("width")
    hx, hy = h // ny, h % ny

    def dev(dz, dh, dw):
        return (lax.rem(z + dz + nz, nz), lax.rem(h + dh + nh, nh), lax.rem(w + dw, 2))

    loads = [
        pltpu.make_async_copy(source, target, load_sem.at[n])
        for n, (source, target) in enumerate(((x_hbm, x_raw), (c_hbm, c_raw), (w1_hbm, w1), (w2_hbm, w2)))
    ]
    for copy in loads:
        copy.start()

    heights = [(ox, oy) for ox in range(nx) for oy in range(ny)]
    heights.sort(key=lambda place: -(min(place[0], nx - place[0]) + min(place[1], ny - place[1])))
    targets_h = [lax.rem(hx + ox, nx) * ny + lax.rem(hy + oy, ny) for ox, oy in heights]

    def for_each_device(act):
        def step(n, _):
            dz, dw = far_first(n // 2, nz), 1 - n % 2
            zt, wt = lax.rem(z + dz, nz), lax.rem(w + dw, 2)
            for ht in targets_h[:-1]:
                act((zt, ht, wt))

            @pl.when(n < 2 * nz - 1)
            def _():
                act((zt, h, wt))

            return 0

        lax.fori_loop(0, 2 * nz, step, 0)

    devices = 2 * nz * nh
    barrier = pltpu.get_barrier_semaphore()
    for dz in reversed(range(nz)):
        for dw in (1, 0):
            zt, wt = lax.rem(z + dz, nz), lax.rem(w + dw, 2)
            for ht in targets_h if (dz, dw) != (0, 0) else targets_h[:-1]:
                pl.semaphore_signal(barrier, inc=1, device_id=(zt, ht, wt), device_id_type=MESH)

    def take(ref, sem):
        pltpu.make_async_copy(ref, ref, sem).wait()

    def remote(src, dst, send, recv, where):
        return pltpu.make_async_remote_copy(
            src_ref=src, dst_ref=dst, send_sem=send, recv_sem=recv, device_id=where, device_id_type=MESH
        )

    own_frames = pl.ds(z * fl, fl)

    def strip_copies(k, src, dst, edges, landing):
        copies = []
        for dz in sorted(range(nz), key=lambda dz: -min(dz, nz - dz)):
            q = lax.rem(z + dz, nz)
            pieces = (
                (src.at[:, :, pl.ds(pl.multiple_of(q * strip, strip), strip), :],
                 dst.at[own_frames, pl.ds(1, rl)], in_recv.at[k, dz]),
                (edges.at[q], landing.at[1, own_frames], in_recv.at[k, nz + dz]),
            )
            for source, target, recv in pieces:
                if dz == 0:
                    copies.append((False, pltpu.make_async_copy(source, target, recv)))
                else:
                    copies.append((True, remote(source, target, in_send.at[k], recv, dev(dz, 0, 0))))
        return copies

    def build_edges(src, edges):
        def at(f, r, col):
            start = (col // 16) * 16
            return src[f, r, start : start + 16, :].astype(F32)[col % 16 : col % 16 + 1]

        place = lax.broadcasted_iota(jnp.int32, (16, CH), 0)
        for f in range(fl):
            for q in range(nz):
                tile = jnp.zeros((16, CH), F32)
                for r in range(rl):
                    if q > 0:
                        tile = jnp.where(place == 2 * r, at(f, r, q * strip - 1), tile)
                    if q < nz - 1:
                        tile = jnp.where(place == 2 * r + 1, at(f, r, (q + 1) * strip), tile)
                edges[q, f] = tile.astype(BF16)
            tile = jnp.zeros((16, CH), F32)
            for r in range(rl):
                outer = jnp.where(w == 0, at(f, r, cols - 1), at(f, r, 0))
                tile = jnp.where(place // 2 == r, outer, tile)
            edges[nz, f] = tile.astype(BF16)

    outer_q = (nz - 1) * w
    takes_outer = z == (nz - 1) * (1 - w)

    def outer_copy(k, edges, landing_out):
        recv = in_recv.at[k, 2 * nz + lax.rem(outer_q - z + nz, nz)]
        return remote(edges.at[nz], landing_out.at[1, own_frames], in_send.at[k], recv, (outer_q, h, 1 - w))

    def start_inputs(k, src, dst, edges, landing, landing_out):
        copies = strip_copies(k, src, dst, edges, landing)
        for _, copy in copies:
            copy.start()
        outer = outer_copy(k, edges, landing_out)
        outer.start()
        return [copy for far, copy in copies if far] + [outer]

    near_first = sorted(range(nz), key=lambda dz: min(dz, nz - dz))

    def pair_from(dz):
        return lax.rem(z - dz + nz, nz) * fl

    def beside_copies(k, dz, cells_in, landing):
        pair = pl.ds(pair_from(dz), fl)
        copies = []
        for dh, r_from, r_to in ((1, rl, 0), (-1, 1, rl + 1)):
            where = dev(0, dh, 0)
            copies.append(
                remote(cells_in.at[pair, pl.ds(r_from, 1)], cells_in.at[pair, pl.ds(r_to, 1)],
                       in_send.at[k], in_recv.at[k, 3 * nz + dz], where)
            )
            copies.append(
                remote(landing.at[1, pair], landing.at[1 - dh, pair], in_send.at[k], in_recv.at[k, 4 * nz + dz], where)
            )
        return copies

    def beside_outer(k, dz, landing_out):
        pair = pl.ds(pair_from(dz), fl)
        return [
            remote(landing_out.at[1, pair], landing_out.at[1 - dh, pair],
                   in_send.at[k], in_recv.at[k, 5 * nz + dz], dev(0, dh, 0))
            for dh in (1, -1)
        ]

    def hand_on(k, dz, cells_in, landing, landing_out):
        pair = pl.ds(pair_from(dz), fl)
        take(cells_in.at[pair, pl.ds(1, rl)], in_recv.at[k, dz])
        take(landing.at[1, pair], in_recv.at[k, nz + dz])
        start_all(beside_copies(k, dz, cells_in, landing))

        @pl.when(takes_outer)
        def _():
            take(landing_out.at[1, pair], in_recv.at[k, 2 * nz + dz])
            start_all(beside_outer(k, dz, landing_out))

    def wait_pair(k, dz, cells_in, landing, landing_out):
        pair = pl.ds(pair_from(dz), fl)
        take(cells_in.at[pair, pl.ds(0, 2)], in_recv.at[k, 3 * nz + dz])
        take(landing.at[pl.ds(0, 2), pair], in_recv.at[k, 4 * nz + dz])

        @pl.when(takes_outer)
        def _():
            take(landing_out.at[pl.ds(0, 2), pair], in_recv.at[k, 5 * nz + dz])

    def close_inputs(k, sent, cells_in, landing, landing_out):
        wait_sends(sent)
        for dz in range(nz):
            wait_sends(beside_copies(k, dz, cells_in, landing))

            @pl.when(takes_outer)
            def _():
                wait_sends(beside_outer(k, dz, landing_out))

    def start_all(copies):
        for copy in copies:
            copy.start()

    def wait_sends(copies):
        for copy in copies:
            copy.wait_send()

    me = (z * nh + h) * 2 + w
    local_size = 4.0 * fl * rl * cols
    total_size = local_size * devices

    def red_start(k, first, second):
        rb[k, me] = pack_pair(first, second)
        slot = rb.at[k, me]
        for_each_device(lambda where: remote(slot, slot, red_send.at[k], red_recv.at[k], where).start())

    def red_wait(k):
        take(rb.at[k, pl.ds(0, devices - 1)], red_recv.at[k])

    def moments_end(k):
        red_wait(k)
        rows = rb[k]
        mean, _ = unpack_pair(jnp.sum(rows, axis=0) / devices)
        low = lanes_low(rows)
        off = rows - jnp.where(lanes_low(mean), mean, 0.0)[None]
        between, within = unpack_pair(jnp.sum(jnp.where(low, off * off, off), axis=0))
        return mean, within + local_size * between

    def sums_end(k):
        red_wait(k)
        return unpack_pair(jnp.sum(rb[k], axis=0) / total_size)

    def turn(source, target):
        for f in range(fl):
            for r in range(rl):
                target[f, r] = jnp.transpose(source[:, f, r, :].astype(F32)).astype(BF16)

    loads[0].wait()
    turn(x_raw, xl)
    build_edges(xl, xe)
    zero8 = jnp.zeros((8, CH), F32)

    def x_sum(n, total):
        return total + fold_rows(xl[n // rl, n % rl].astype(F32))

    local_mean = group_sum(total_row(lax.fori_loop(0, fl * rl, x_sum, zero8))) / local_size

    def x_spread(n, total):
        off = xl[n // rl, n % rl].astype(F32) - local_mean
        return total + fold_rows(off * off)

    local_spread = group_sum(total_row(lax.fori_loop(0, fl * rl, x_spread, zero8)))

    loads[1].wait()
    turn(c_raw, cl)
    build_edges(cl, ce)
    loads[2].wait()
    loads[3].wait()
    for kt in range(3):
        for kr in range(3):
            for kc in range(3):
                tap = 9 * kt + 3 * kr + kc
                back = ((2 - kr) * 3 + (2 - kc)) * CH
                for source, target in ((w1, wb1), (w2, wb2)):
                    target[back : back + CH, kt * CH : (kt + 1) * CH] = source[:, tap * CH : (tap + 1) * CH]
    for kt in range(3):
        for kr in range(3):
            for kc in range(3):
                tap = 9 * kt + 3 * kr + kc
                ahead = (kr * 3 + kc) * CH
                block = w1[:, tap * CH : (tap + 1) * CH].astype(F32)
                wf1[ahead : ahead + CH, (2 - kt) * CH : (3 - kt) * CH] = jnp.transpose(block).astype(BF16)
    pl.semaphore_wait(barrier, devices - 1)
    x_sent = start_inputs(0, xl, xr, xe, xeb, xex)
    red_start(0, local_mean, local_spread)
    c_sent = start_inputs(1, cl, cr, ce, ceb, cex)
    zero_cells = jnp.zeros((cells, CH), F32)

    def clear(n, _):
        hid[n] = zero_cells
        g2[n] = zero_cells
        g1[n] = zero_cells
        return 0

    lax.fori_loop(0, frames + 2, clear, 0)
    zero_t = jnp.zeros((2 * CH, cells), BF16)
    act_t[0 : 2 * CH] = zero_t
    hg_t[frames * CH : (frames + 2) * CH] = zero_t

    row_place = lax.broadcasted_iota(jnp.int32, (strip, CH), 0)
    left_ok = jnp.logical_not(jnp.logical_and(w == 0, z == 0))
    right_ok = jnp.logical_not(jnp.logical_and(w == 1, z == nz - 1))

    def row_ok(r):
        if r == 0:
            return h > 0
        if r == rl + 1:
            return h < nh - 1
        return None

    def row_source(r):
        if r == 0:
            return 0, rl - 1
        if r == rl + 1:
            return 2, 0
        return 1, r - 1

    def store_stack(stack, f, r, value, left, right):
        ok = row_ok(r)
        left = jnp.where(left_ok if ok is None else jnp.logical_and(left_ok, ok), left, 0.0)
        right = jnp.where(right_ok if ok is None else jnp.logical_and(right_ok, ok), right, 0.0)
        if ok is not None:
            value = jnp.where(ok, value, 0.0)
        before = jnp.where(row_place == 0, left, pltpu.roll(value, 1, 0))
        after = jnp.where(row_place == strip - 1, right, pltpu.roll(value, strip - 1, 0))
        stack[f, r, :, 0:CH] = before.astype(BF16)
        stack[f, r, :, CH : 2 * CH] = value.astype(BF16)
        stack[f, r, :, 2 * CH : 3 * CH] = after.astype(BF16)

    edge_place = lax.broadcasted_iota(jnp.int32, (16, CH), 0)
    outer_mask = jnp.logical_and(takes_outer, edge_place % 2 == 1 - w)

    def input_stack(stack, source, landing, landing_out, apply, start):
        def step(f, _):
            edges = []
            for d in range(3):
                tile = jnp.where(outer_mask, landing_out[d, f].astype(F32), landing[d, f].astype(F32))
                edges.append(apply(tile))
            for r in range(rl + 2):
                d, row = row_source(r)
                tile = edges[d]
                store_stack(
                    stack, f, r, apply(source[f, r].astype(F32)),
                    tile[2 * row : 2 * row + 1], tile[2 * row + 1 : 2 * row + 2],
                )
            return 0

        lax.fori_loop(start, start + fl, step, 0)

    def window(stack, f):
        return [stack[f, kr : kr + rl].reshape(cells, 3 * CH) for kr in range(3)]

    def convolve(stack, weight, target, first=0, last=None):
        def step(f, _):
            product = jnp.dot(
                jnp.concatenate(window(stack, f), axis=1), weight[...], preferred_element_type=F32
            )
            for j in range(3):
                target[f + j] += product[:, j * CH : (j + 1) * CH]
            return 0

        lax.fori_loop(first, frames if last is None else last, step, 0)

    def weight_part(turned, stack, kr):
        left = jnp.concatenate([turned[f * CH : (f + 3) * CH, :] for f in range(frames)], axis=1)
        right = stack[:, kr : kr + rl].reshape(frames * cells, 3 * CH)
        return jnp.dot(left, right, preferred_element_type=F32)

    def peer(axis, j):
        if axis == "z":
            return dev(j, 0, 0)
        if axis == "x":
            return (z, lax.rem(hx + j, nx) * ny + hy, w)
        return (z, hx * ny + lax.rem(hy + j, ny), w)

    coords = {"z": z, "x": hx, "y": hy}
    orders = (("z", "y", "x"), ("y", "x", "z"), ("x", "z", "y"))
    half = 8
    span = half // ns
    tiles = span * 9
    piece = -(-tiles // ns)
    outs = (o1_ref, o2_ref)
    stage_at = {"core": 0, "a1": 1, "a2": 2, "a3": 3, "g2": 4, "g1": 5, "gc": 6}

    def sems(g, p, stage):
        return ar_send.at[g], ar_recv.at[g, p, stage_at[stage]]

    def arrived(g, p, stage, ref):
        take(ref, ar_recv.at[g, p, stage_at[stage]])

    def core_copy(g, p):
        return remote(a.at[g, p, pl.ds((1 - w) * half, half)], r0.at[g, p], *sems(g, p, "core"), dev(0, 0, 1))

    def core_start(g, p):
        core_copy(g, p).start()

    def a1_copies(g, p):
        axis = orders[p][0]
        return [
            remote(
                b1.at[g, p, pl.ds(lax.rem(coords[axis] + j, ns) * span, span)], r1.at[g, p, j - 1],
                *sems(g, p, "a1"), peer(axis, j),
            )
            for j in range(1, ns)
        ]

    def a1_start(g, p):
        arrived(g, p, "core", r0.at[g, p])
        b1[g, p] = a[g, p, pl.ds(w * half, half)] + r0[g, p]
        start_all(a1_copies(g, p))

    def a2_copies(g, p):
        axis = orders[p][1]
        return [
            remote(
                b2.at[g, p, pl.ds(lax.rem(coords[axis] + j, ns) * piece, piece)], r2.at[g, p, j - 1],
                *sems(g, p, "a2"), peer(axis, j),
            )
            for j in range(1, ns)
        ]

    def a2_start(g, p):
        arrived(g, p, "a1", r1.at[g, p])
        value = b1[g, p, pl.ds(coords[orders[p][0]] * span, span)]
        for j in range(ns - 1):
            value = value + r1[g, p, j]
        b2[g, p, 0:tiles] = value.reshape(tiles, 8, CH)
        if piece * ns > tiles:
            b2[g, p, tiles:] = jnp.zeros((piece * ns - tiles, 8, CH), F32)
        start_all(a2_copies(g, p))

    def a3_copies(g, p):
        axis = orders[p][2]
        slot = r3.at[g, p, coords[axis]]
        return [remote(slot, slot, *sems(g, p, "a3"), peer(axis, j)) for j in range(1, ns)]

    def a3_start(g, p):
        arrived(g, p, "a2", r2.at[g, p])
        value = b2[g, p, pl.ds(coords[orders[p][1]] * piece, piece)]
        for j in range(ns - 1):
            value = value + r2[g, p, j]
        r3[g, p, coords[orders[p][2]]] = value
        start_all(a3_copies(g, p))

    def g2_copies(g, p):
        axis = orders[p][1]
        part = g3.at[g, p, pl.ds(coords[axis] * piece, piece)]
        return [remote(part, part, *sems(g, p, "g2"), peer(axis, j)) for j in range(1, ns)]

    def g2_start(g, p):
        arrived(g, p, "a3", r3.at[g, p, pl.ds(0, ns - 1)])
        value = r3[g, p, 0]
        for n in range(1, ns):
            value = value + r3[g, p, n]
        g3[g, p, pl.ds(coords[orders[p][1]] * piece, piece)] = value
        start_all(g2_copies(g, p))

    def out_span(g, p, n):
        return outs[g].at[p, pl.ds(w * half + n * span, span)]

    def g1_copies(g, p):
        axis = orders[p][0]
        part = out_span(g, p, coords[axis])
        return [remote(part, part, *sems(g, p, "g1"), peer(axis, j)) for j in range(1, ns)]

    def gc_copy(g, p, j):
        part = out_span(g, p, lax.rem(coords[orders[p][0]] + ns - j, ns))
        return remote(part, part, *sems(g, p, "gc"), dev(0, 0, 1))

    def g1_start(g, p):
        arrived(g, p, "g2", g3.at[g, p, pl.ds(0, (ns - 1) * piece)])
        outs[g][p, pl.ds(w * half + coords[orders[p][0]] * span, span)] = g3[g, p, 0:tiles].reshape(span, 9, 8, CH)
        start_all(g1_copies(g, p))
        gc_copy(g, p, 0).start()

    def gc_start(g, p):
        arrived(g, p, "g1", outs[g].at[p, pl.ds(0, (ns - 1) * span)])
        for j in range(1, ns):
            gc_copy(g, p, j).start()

    def store_copy(g):
        return pltpu.make_async_copy((fin1, fin2)[g], (o1_hbm, o2_hbm)[g], store_sem.at[1 + g])

    def gc_end(g, p):
        arrived(g, p, "gc", outs[g].at[p, pl.ds(0, half)])
        for kt in range(3):
            for kc in range(3):
                block = outs[g][p, :, kt * 3 + kc].reshape(CH, CH)
                tap = 9 * kt + 3 * p + kc
                (fin1, fin2)[g][:, tap * CH : (tap + 1) * CH] = block if g == 0 else jnp.transpose(block)

    def ar_close(g):
        for p in range(3):
            wait_sends([core_copy(g, p)] + a1_copies(g, p) + a2_copies(g, p) + a3_copies(g, p))
            wait_sends(g2_copies(g, p) + g1_copies(g, p) + [gc_copy(g, p, j) for j in range(ns)])

    def each(stage, g):
        for p in range(3):
            stage(g, p)

    for dz in near_first:
        hand_on(0, dz, xr, xeb, xex)
    mean1, spread1 = moments_end(0)
    picks = lax.broadcasted_iota(jnp.int32, (CH // 4, CH), 1) // 4 == lax.broadcasted_iota(jnp.int32, (CH // 4, CH), 0)
    spread_exponent = jnp.dot(
        jnp.broadcast_to(exponent_ref[...].astype(F32), (8, CH // 4)), picks.astype(F32), preferred_element_type=F32
    )
    scale = jnp.exp2(spread_exponent[0:1])
    inv1 = 1.0 / jnp.sqrt(spread1 * (scale * scale) / total_size + EPS)
    factor1 = scale * inv1
    gain1, shift1 = gain1_ref[...], shift1_ref[...]
    gain2, shift2 = gain2_ref[...], shift2_ref[...]

    def rounded(value):
        return value.astype(BF16).astype(F32)

    def act_first(value):
        pre = (value - mean1) * factor1 * gain1 + shift1
        return rounded(pre * sigmoid(pre))

    for dz in near_first:
        wait_pair(0, dz, xr, xeb, xex)
        start = pair_from(dz)
        input_stack(s1, xr, xeb, xex, act_first, start)
        convolve(s1, wf1, hid, start, start + fl)
        hand_on(1, dz, cr, ceb, cex)

    def hid_sum(n, total):
        return total + fold_rows(hid[n])

    mean_l = group_sum(total_row(lax.fori_loop(0, frames, hid_sum, zero8))) / local_size

    def hid_spread(n, total):
        off = hid[n] - mean_l
        return total + fold_rows(off * off)

    red_start(1, mean_l, group_sum(total_row(lax.fori_loop(0, frames, hid_spread, zero8))))

    for dz in near_first:
        wait_pair(1, dz, cr, ceb, cex)
        start = pair_from(dz)
        input_stack(sc, cr, ceb, cex, lambda value: value, start)
        convolve(sc, wb2, g2, start, start + fl)
    mean2, spread2 = moments_end(1)
    inv2 = 1.0 / jnp.sqrt(spread2 / total_size + EPS)

    def second(n, totals):
        first_total, second_total = totals
        normed = (hid[n] - mean2) * inv2
        pre = normed * gain2 + shift2
        sig = sigmoid(pre)
        act_t[pl.ds(pl.multiple_of((n + 2) * CH, CH), CH), :] = jnp.transpose(pre * sig).astype(BF16)
        scaled = g2[n + 2] * (sig * (1.0 + pre * (1.0 - sig))) * gain2
        nrm[n] = normed
        g2[n + 2] = scaled
        return first_total + fold_rows(scaled), second_total + fold_rows(scaled * normed)

    t1, t2 = lax.fori_loop(0, frames, second, (zero8, zero8))
    red_start(2, group_sum(total_row(t1)), group_sum(total_row(t2)))

    def put_second(kr):
        block = weight_part(act_t, sc, kr)
        for kt in range(3):
            for kc in range(3):
                part = block[kt * CH : (kt + 1) * CH, kc * CH : (kc + 1) * CH]
                a[1, 2 - kr, :, kt * 3 + (2 - kc)] = part.reshape(16, 8, CH)
        core_start(1, 2 - kr)

    for kr in range(3):
        put_second(kr)
    each(a1_start, 1)
    m1, m2 = sums_end(2)

    def hidden(n, _):
        value = inv2 * (g2[n + 2] - m1 - nrm[n] * m2)
        hg_t[pl.ds(pl.multiple_of(n * CH, CH), CH), :] = jnp.transpose(value).astype(BF16)
        narrow = value.astype(BF16)
        hg[n, 1 : rl + 1] = narrow.reshape(rl, strip, CH)
        wide = narrow.astype(F32).reshape(rl, strip, CH)
        lefts = jnp.zeros((16, CH), F32)
        rights = jnp.zeros((16, CH), F32)
        for r in range(rl):
            lefts = jnp.where(edge_place == r, wide[r, 0:1], lefts)
            rights = jnp.where(edge_place == r, wide[r, strip - 1 : strip], rights)
        eh[0, n] = lefts.astype(BF16)
        eh[1, n] = rights.astype(BF16)
        return 0

    lax.fori_loop(0, frames, hidden, 0)

    line = w * nz + z

    def beside(ds, dh):
        place = lax.rem(line + ds + 2 * nz, 2 * nz)
        return (lax.rem(place, nz), lax.rem(h + dh + nh, nh), place // nz)

    halo = [
        remote(hg.at[:, pl.ds(rl, 1)], hg.at[:, pl.ds(0, 1)], halo_send.at[0], halo_recv.at[0], dev(0, 1, 0)),
        remote(hg.at[:, pl.ds(1, 1)], hg.at[:, pl.ds(rl + 1, 1)], halo_send.at[0], halo_recv.at[0], dev(0, -1, 0)),
    ]
    for n, dh in enumerate((0, 1, -1)):
        halo.append(remote(eh.at[0], heb.at[1 - dh, 1], halo_send.at[0], halo_recv.at[1], beside(-1, dh)))
        halo.append(remote(eh.at[1], heb.at[1 - dh, 0], halo_send.at[0], halo_recv.at[1], beside(1, dh)))
    start_all(halo)

    def put_first(kr):
        block = weight_part(hg_t, s1, kr)
        for j in range(3):
            for kc in range(3):
                part = block[j * CH : (j + 1) * CH, kc * CH : (kc + 1) * CH]
                a[0, kr, :, (2 - j) * 3 + kc] = part.reshape(16, 8, CH)
        core_start(0, kr)

    put_first(0)
    put_first(1)
    a1_start(0, 0)
    put_first(2)
    a1_start(0, 1)
    a1_start(0, 2)
    each(a2_start, 1)
    take(hg.at[:, pl.ds(0, 2)], halo_recv.at[0])
    take(heb, halo_recv.at[1])

    def halo_stack(f, _):
        lefts = [heb[d, 0, f].astype(F32) for d in range(3)]
        rights = [heb[d, 1, f].astype(F32) for d in range(3)]
        for r in range(rl + 2):
            d, row = row_source(r)
            store_stack(sh, f, r, hg[f, r].astype(F32), lefts[d][row : row + 1], rights[d][row : row + 1])
        return 0

    lax.fori_loop(0, frames, halo_stack, 0)

    def first(f, totals):
        first_total, second_total = totals
        for r in range(rl):
            normed = (xr[f, r + 1].astype(F32) - mean1) * factor1
            pre = normed * gain1 + shift1
            sig = sigmoid(pre)
            scaled = g1[f + 2, r * strip : (r + 1) * strip] * (sig * (1.0 + pre * (1.0 - sig))) * gain1
            s_out[f, r] = scaled.astype(BF16)
            first_total = first_total + fold_rows(scaled)
            second_total = second_total + fold_rows(scaled * normed)
        return first_total, second_total

    back_from = s_in.at[:, :, pl.ds(pl.multiple_of(z * strip, strip), strip), :]
    back_copies = []

    def send_back(q):
        source = s_out.at[pl.ds(q * fl, fl)]
        far = remote(source, back_from, back_send.at[0], back_recv.at[0], (q, h, w))
        back_copies.append(far)

        @pl.when(z == q)
        def _():
            pltpu.make_async_copy(source, back_from, back_recv.at[0]).start()

        @pl.when(z != q)
        def _():
            far.start()

    convolve(sh, wb1, g1, 0, 2)
    each(a2_start, 0)
    each(a3_start, 1)
    totals = (zero8, zero8)
    for q in range(nz):
        if q * fl + 2 < frames:
            convolve(sh, wb1, g1, q * fl + 2, q * fl + fl + 2)
        totals = lax.fori_loop(q * fl, q * fl + fl, first, totals)
        send_back(q)
        if q == nz // 2 - 1:
            each(a3_start, 0)
            each(g2_start, 1)
    t1, t2 = totals
    red_start(3, group_sum(total_row(t1)), group_sum(total_row(t2)))
    each(g2_start, 0)
    each(g1_start, 1)
    each(g1_start, 0)
    m1, m2 = sums_end(3)
    take(s_in, back_recv.at[0])

    def out_copy(f):
        return pltpu.make_async_copy(out_ref.at[:, f], out_hbm.at[:, f], store_sem.at[0])

    for f in range(fl):
        for r in range(rl):
            normed = (xl[f, r].astype(F32) - mean1) * factor1
            value = cl[f, r].astype(F32) + inv1 * (s_in[f, r].astype(F32) - m1 - normed * m2)
            out_ref[:, f, r, :] = jnp.transpose(value)
        out_copy(f).start()
    each(gc_start, 1)
    each(gc_end, 1)
    store_copy(1).start()
    close_inputs(0, x_sent, xr, xeb, xex)
    close_inputs(1, c_sent, cr, ceb, cex)
    for k in range(4):
        take(rb.at[k, pl.ds(0, devices - 1)], red_send.at[k])
    wait_sends(halo)
    for q in range(nz):

        @pl.when(z != q)
        def _():
            back_copies[q].wait_send()

    ar_close(1)
    each(gc_start, 0)
    each(gc_end, 0)
    store_copy(0).start()
    ar_close(0)
    for f in range(fl):
        out_copy(f).wait()
    store_copy(0).wait()
    store_copy(1).wait()


def copy_body(*refs):
    sources, targets, held = refs[0:3], refs[3:6], refs[6:9]
    load_sem, store_sem = refs[9:]
    loads = [pltpu.make_async_copy(sources[n], held[n], load_sem.at[n]) for n in range(3)]
    stores = [pltpu.make_async_copy(held[n], targets[n], store_sem.at[n]) for n in range(3)]
    for copy in loads:
        copy.start()
    for n in range(3):
        loads[n].wait()
        stores[n].start()
    for copy in stores:
        copy.wait()


def shards(sizes, latent, exponents, cotangent, conv_first, conv_second, gain_first, shift_first, gain_second, shift_second):
    nz, nh, nx, ny = sizes
    channels, fl, rl, cols = latent.shape
    strip = cols // nz
    frames = fl * nz
    cells = rl * strip
    ns = nx
    span = 8 // ns
    tiles = span * 9
    piece = -(-tiles // ns)
    vmem = pl.BlockSpec(memory_space=pltpu.VMEM)
    any_space = pl.BlockSpec(memory_space=pl.ANY)
    part = (3, 16, 9, 8, CH)
    wide = (frames, rl + 2, strip, 3 * CH)
    scratch = [
        pltpu.VMEM((CH, fl, rl, cols), BF16),
        pltpu.VMEM((CH, fl, rl, cols), BF16),
        pltpu.VMEM((fl, rl, cols, CH), BF16),
        pltpu.VMEM((fl, rl, cols, CH), BF16),
        pltpu.VMEM((CH, 27 * CH), BF16),
        pltpu.VMEM((CH, 27 * CH), BF16),
        pltpu.VMEM((CH, fl, rl, cols), F32),
        pltpu.VMEM(part, F32),
        pltpu.VMEM(part, F32),
        pltpu.VMEM((CH, 27 * CH), F32),
        pltpu.VMEM((CH, 27 * CH), F32),
        pltpu.VMEM((frames, rl + 2, strip, CH), BF16),
        pltpu.VMEM((frames, rl + 2, strip, CH), BF16),
        pltpu.VMEM((nz + 1, fl, 16, CH), BF16),
        pltpu.VMEM((nz + 1, fl, 16, CH), BF16),
        pltpu.VMEM((3, frames, 16, CH), BF16),
        pltpu.VMEM((3, frames, 16, CH), BF16),
        pltpu.VMEM((3, frames, 16, CH), BF16),
        pltpu.VMEM((3, frames, 16, CH), BF16),
        pltpu.VMEM(wide, BF16),
        pltpu.VMEM(wide, BF16),
        pltpu.VMEM(wide, BF16),
        pltpu.VMEM((frames + 2, cells, CH), F32),
        pltpu.VMEM((frames + 2, cells, CH), F32),
        pltpu.VMEM((frames + 2, cells, CH), F32),
        pltpu.VMEM((frames, cells, CH), F32),
        pltpu.VMEM(((frames + 2) * CH, cells), BF16),
        pltpu.VMEM(((frames + 2) * CH, cells), BF16),
        pltpu.VMEM((frames, rl + 2, strip, CH), BF16),
        pltpu.VMEM((2, frames, 16, CH), BF16),
        pltpu.VMEM((3, 2, frames, 16, CH), BF16),
        pltpu.VMEM((9 * CH, 3 * CH), BF16),
        pltpu.VMEM((9 * CH, 3 * CH), BF16),
        pltpu.VMEM((9 * CH, 3 * CH), BF16),
        pltpu.VMEM((frames, rl, strip, CH), BF16),
        pltpu.VMEM((fl, rl, cols, CH), BF16),
        pltpu.VMEM((4, 2 * nz * nh, 1, CH), F32),
        pltpu.VMEM((2, 3, 16, 9, 8, CH), F32),
        pltpu.VMEM((2, 3, 8, 9, 8, CH), F32),
        pltpu.VMEM((2, 3, 8, 9, 8, CH), F32),
        pltpu.VMEM((2, 3, ns - 1, span, 9, 8, CH), F32),
        pltpu.VMEM((2, 3, piece * ns, 8, CH), F32),
        pltpu.VMEM((2, 3, ns - 1, piece, 8, CH), F32),
        pltpu.VMEM((2, 3, ns, piece, 8, CH), F32),
        pltpu.VMEM((2, 3, piece * ns, 8, CH), F32),
        pltpu.SemaphoreType.DMA((4,)),
        pltpu.SemaphoreType.DMA((3,)),
        pltpu.SemaphoreType.DMA((2,)),
        pltpu.SemaphoreType.DMA((2, 6 * nz)),
        pltpu.SemaphoreType.DMA((4,)),
        pltpu.SemaphoreType.DMA((4,)),
        pltpu.SemaphoreType.DMA((1,)),
        pltpu.SemaphoreType.DMA((2,)),
        pltpu.SemaphoreType.DMA((1,)),
        pltpu.SemaphoreType.DMA((1,)),
        pltpu.SemaphoreType.DMA((2,)),
        pltpu.SemaphoreType.DMA((2, 3, 7)),
    ]
    results = pl.pallas_call(
        functools.partial(body, sizes),
        out_shape=(
            jax.ShapeDtypeStruct((CH, fl, rl, cols), F32),
            jax.ShapeDtypeStruct((CH, 27 * CH), F32),
            jax.ShapeDtypeStruct((CH, 27 * CH), F32),
        ),
        in_specs=[any_space] * 4 + [vmem] * 5,
        out_specs=(any_space,) * 3,
        scratch_shapes=scratch,
        compiler_params=pltpu.CompilerParams(
            collective_id=0, has_side_effects=True, vmem_limit_bytes=60 * 1024 * 1024
        ),
    )(
        latent, cotangent, conv_first, conv_second, exponents[None],
        gain_first[None], shift_first[None], gain_second[None], shift_second[None],
    )
    return pl.pallas_call(
        copy_body,
        out_shape=[jax.ShapeDtypeStruct(value.shape, F32) for value in results],
        in_specs=[any_space] * 3,
        out_specs=[any_space] * 3,
        scratch_shapes=[pltpu.VMEM(value.shape, F32) for value in results]
        + [pltpu.SemaphoreType.DMA((3,)), pltpu.SemaphoreType.DMA((3,))],
        compiler_params=pltpu.CompilerParams(vmem_limit_bytes=60 * 1024 * 1024),
    )(*results)


def solution(mesh):
    nz, nh = mesh.shape["tm"], mesh.shape["height"]
    nx = int(round(nh**0.5))
    placed = P(None, "tm", "height", "width")
    return jax.shard_map(
        functools.partial(shards, (nz, nh, nx, nh // nx)),
        mesh=mesh,
        in_specs=(placed, P(), placed, P(), P(), P(), P(), P(), P()),
        out_specs=(placed, P(), P()),
        check_vma=False,
    )
```

```python
import functools

import jax
import jax.numpy as jnp
from jax import lax
from jax.experimental import pallas as pl
from jax.experimental.pallas import tpu as pltpu
from jax.sharding import PartitionSpec as P

MESH = pl.DeviceIdType.MESH
EPS = 1e-05
CH = 128
F32 = jnp.float32
BF16 = jnp.bfloat16


def group_sum(row):
    lane = lax.broadcasted_iota(jnp.int32, row.shape, 1)
    pair = row + jnp.where(lane % 2 == 0, pltpu.roll(row, CH - 1, 1), pltpu.roll(row, 1, 1))
    return pair + jnp.where(lane % 4 < 2, pltpu.roll(pair, CH - 2, 1), pltpu.roll(pair, 2, 1))


def fold_rows(cells):
    return jnp.sum(cells.reshape(-1, 8, CH), axis=0)


def total_row(partial):
    return jnp.sum(partial, axis=0, keepdims=True)


def lanes_low(row):
    return lax.broadcasted_iota(jnp.int32, row.shape, row.ndim - 1) % 4 < 2


def pack_pair(first, second):
    return jnp.where(lanes_low(first), first, second)


def unpack_pair(row):
    low = lanes_low(row)
    return jnp.where(low, row, pltpu.roll(row, 2, 1)), jnp.where(low, pltpu.roll(row, CH - 2, 1), row)


def far_first(n, size):
    if size == 4:
        return (2 + 3 * n + 3 * ((n * (n - 1)) // 2)) % 4
    return size - 1 - n


def sigmoid(value):
    return 1.0 / (1.0 + jnp.exp(-value))


def body(
    sizes,
    x_hbm, c_hbm, w1_hbm, w2_hbm, exponent_ref, gain1_ref, shift1_ref, gain2_ref, shift2_ref,
    out_ref, fin1, fin2,
    x_raw, c_raw, xl, cl, w1, w2, o1_ref, o2_ref,
    xr, cr, xe, ce, xeb, ceb, xex, cex, s1, sc, sh, hid, g2, g1, nrm, act_t, hg_t, hg, eh, heb,
    wf1, wb1, wb2, s_out, s_in, rb, a, r0, b1, r1, b2, r2, r3, g3,
    load_sem, in_send, in_recv, red_send, red_recv, halo_send, halo_recv, back_send, back_recv,
    ar_send, ar_recv,
):
    nz, nh, nx, ny = sizes
    ns = nx
    fl, rl, cols = xl.shape[0], xl.shape[1], xl.shape[2]
    strip = cols // nz
    frames = fl * nz
    cells = rl * strip
    z, h, w = lax.axis_index("tm"), lax.axis_index("height"), lax.axis_index("width")
    hx, hy = h // ny, h % ny

    def dev(dz, dh, dw):
        return (lax.rem(z + dz + nz, nz), lax.rem(h + dh + nh, nh), lax.rem(w + dw, 2))

    loads = [
        pltpu.make_async_copy(source, target, load_sem.at[n])
        for n, (source, target) in enumerate(((x_hbm, x_raw), (c_hbm, c_raw), (w1_hbm, w1), (w2_hbm, w2)))
    ]
    for copy in loads:
        copy.start()

    heights = [(ox, oy) for ox in range(nx) for oy in range(ny)]
    heights.sort(key=lambda place: -(min(place[0], nx - place[0]) + min(place[1], ny - place[1])))
    targets_h = [lax.rem(hx + ox, nx) * ny + lax.rem(hy + oy, ny) for ox, oy in heights]

    def for_each_device(act):
        def step(n, _):
            dz, dw = far_first(n // 2, nz), 1 - n % 2
            zt, wt = lax.rem(z + dz, nz), lax.rem(w + dw, 2)
            for ht in targets_h[:-1]:
                act((zt, ht, wt))

            @pl.when(n < 2 * nz - 1)
            def _():
                act((zt, h, wt))

            return 0

        lax.fori_loop(0, 2 * nz, step, 0)

    devices = 2 * nz * nh
    barrier = pltpu.get_barrier_semaphore()
    for dz in reversed(range(nz)):
        for dw in (1, 0):
            zt, wt = lax.rem(z + dz, nz), lax.rem(w + dw, 2)
            for ht in targets_h if (dz, dw) != (0, 0) else targets_h[:-1]:
                pl.semaphore_signal(barrier, inc=1, device_id=(zt, ht, wt), device_id_type=MESH)

    def take(ref, sem):
        pltpu.make_async_copy(ref, ref, sem).wait()

    def remote(src, dst, send, recv, where):
        return pltpu.make_async_remote_copy(
            src_ref=src, dst_ref=dst, send_sem=send, recv_sem=recv, device_id=where, device_id_type=MESH
        )

    own_frames = pl.ds(z * fl, fl)

    def strip_copies(k, src, dst, edges, landing):
        copies = []
        for dz in sorted(range(nz), key=lambda dz: -min(dz, nz - dz)):
            q = lax.rem(z + dz, nz)
            pieces = (
                (src.at[:, :, pl.ds(pl.multiple_of(q * strip, strip), strip), :],
                 dst.at[own_frames, pl.ds(1, rl)], in_recv.at[k, dz]),
                (edges.at[q], landing.at[1, own_frames], in_recv.at[k, nz + dz]),
            )
            for source, target, recv in pieces:
                if dz == 0:
                    copies.append((False, pltpu.make_async_copy(source, target, recv)))
                else:
                    copies.append((True, remote(source, target, in_send.at[k], recv, dev(dz, 0, 0))))
        return copies

    def build_edges(src, edges):
        def at(f, r, col):
            start = (col // 16) * 16
            return src[f, r, start : start + 16, :].astype(F32)[col % 16 : col % 16 + 1]

        place = lax.broadcasted_iota(jnp.int32, (16, CH), 0)
        for f in range(fl):
            for q in range(nz):
                tile = jnp.zeros((16, CH), F32)
                for r in range(rl):
                    if q > 0:
                        tile = jnp.where(place == 2 * r, at(f, r, q * strip - 1), tile)
                    if q < nz - 1:
                        tile = jnp.where(place == 2 * r + 1, at(f, r, (q + 1) * strip), tile)
                edges[q, f] = tile.astype(BF16)
            tile = jnp.zeros((16, CH), F32)
            for r in range(rl):
                outer = jnp.where(w == 0, at(f, r, cols - 1), at(f, r, 0))
                tile = jnp.where(place // 2 == r, outer, tile)
            edges[nz, f] = tile.astype(BF16)

    outer_q = (nz - 1) * w
    takes_outer = z == (nz - 1) * (1 - w)

    def outer_copy(k, edges, landing_out):
        recv = in_recv.at[k, 2 * nz + lax.rem(outer_q - z + nz, nz)]
        return remote(edges.at[nz], landing_out.at[1, own_frames], in_send.at[k], recv, (outer_q, h, 1 - w))

    def start_inputs(k, src, dst, edges, landing, landing_out):
        copies = strip_copies(k, src, dst, edges, landing)
        for _, copy in copies:
            copy.start()
        outer = outer_copy(k, edges, landing_out)
        outer.start()
        return [copy for far, copy in copies if far] + [outer]

    near_first = sorted(range(nz), key=lambda dz: min(dz, nz - dz))

    def pair_from(dz):
        return lax.rem(z - dz + nz, nz) * fl

    def beside_copies(k, dz, cells_in, landing):
        pair = pl.ds(pair_from(dz), fl)
        copies = []
        for dh, r_from, r_to in ((1, rl, 0), (-1, 1, rl + 1)):
            where = dev(0, dh, 0)
            copies.append(
                remote(cells_in.at[pair, pl.ds(r_from, 1)], cells_in.at[pair, pl.ds(r_to, 1)],
                       in_send.at[k], in_recv.at[k, 3 * nz + dz], where)
            )
            copies.append(
                remote(landing.at[1, pair], landing.at[1 - dh, pair], in_send.at[k], in_recv.at[k, 4 * nz + dz], where)
            )
        return copies

    def beside_outer(k, dz, landing_out):
        pair = pl.ds(pair_from(dz), fl)
        return [
            remote(landing_out.at[1, pair], landing_out.at[1 - dh, pair],
                   in_send.at[k], in_recv.at[k, 5 * nz + dz], dev(0, dh, 0))
            for dh in (1, -1)
        ]

    def hand_on(k, dz, cells_in, landing, landing_out):
        pair = pl.ds(pair_from(dz), fl)
        take(cells_in.at[pair, pl.ds(1, rl)], in_recv.at[k, dz])
        take(landing.at[1, pair], in_recv.at[k, nz + dz])
        start_all(beside_copies(k, dz, cells_in, landing))

        @pl.when(takes_outer)
        def _():
            take(landing_out.at[1, pair], in_recv.at[k, 2 * nz + dz])
            start_all(beside_outer(k, dz, landing_out))

    def wait_pair(k, dz, cells_in, landing, landing_out):
        pair = pl.ds(pair_from(dz), fl)
        take(cells_in.at[pair, pl.ds(0, 2)], in_recv.at[k, 3 * nz + dz])
        take(landing.at[pl.ds(0, 2), pair], in_recv.at[k, 4 * nz + dz])

        @pl.when(takes_outer)
        def _():
            take(landing_out.at[pl.ds(0, 2), pair], in_recv.at[k, 5 * nz + dz])

    def close_inputs(k, sent, cells_in, landing, landing_out):
        wait_sends(sent)
        for dz in range(nz):
            wait_sends(beside_copies(k, dz, cells_in, landing))

            @pl.when(takes_outer)
            def _():
                wait_sends(beside_outer(k, dz, landing_out))

    def start_all(copies):
        for copy in copies:
            copy.start()

    def wait_sends(copies):
        for copy in copies:
            copy.wait_send()

    me = (z * nh + h) * 2 + w
    local_size = 4.0 * fl * rl * cols
    total_size = local_size * devices

    def red_start(k, first, second):
        rb[k, me] = pack_pair(first, second)
        slot = rb.at[k, me]
        for_each_device(lambda where: remote(slot, slot, red_send.at[k], red_recv.at[k], where).start())

    def red_wait(k):
        take(rb.at[k, pl.ds(0, devices - 1)], red_recv.at[k])

    def moments_end(k):
        red_wait(k)
        rows = rb[k]
        mean, _ = unpack_pair(jnp.sum(rows, axis=0) / devices)
        low = lanes_low(rows)
        off = rows - jnp.where(lanes_low(mean), mean, 0.0)[None]
        between, within = unpack_pair(jnp.sum(jnp.where(low, off * off, off), axis=0))
        return mean, within + local_size * between

    def sums_end(k):
        red_wait(k)
        return unpack_pair(jnp.sum(rb[k], axis=0) / total_size)

    def turn(source, target):
        for f in range(fl):
            for r in range(rl):
                target[f, r] = jnp.transpose(source[:, f, r, :].astype(F32)).astype(BF16)

    loads[0].wait()
    turn(x_raw, xl)
    build_edges(xl, xe)
    zero8 = jnp.zeros((8, CH), F32)

    def x_sum(n, total):
        return total + fold_rows(xl[n // rl, n % rl].astype(F32))

    local_mean = group_sum(total_row(lax.fori_loop(0, fl * rl, x_sum, zero8))) / local_size

    def x_spread(n, total):
        off = xl[n // rl, n % rl].astype(F32) - local_mean
        return total + fold_rows(off * off)

    local_spread = group_sum(total_row(lax.fori_loop(0, fl * rl, x_spread, zero8)))

    loads[1].wait()
    turn(c_raw, cl)
    build_edges(cl, ce)
    loads[2].wait()
    loads[3].wait()
    for kt in range(3):
        for kr in range(3):
            for kc in range(3):
                tap = 9 * kt + 3 * kr + kc
                back = ((2 - kr) * 3 + (2 - kc)) * CH
                for source, target in ((w1, wb1), (w2, wb2)):
                    target[back : back + CH, kt * CH : (kt + 1) * CH] = source[:, tap * CH : (tap + 1) * CH]
    for kt in range(3):
        for kr in range(3):
            for kc in range(3):
                tap = 9 * kt + 3 * kr + kc
                ahead = (kr * 3 + kc) * CH
                block = w1[:, tap * CH : (tap + 1) * CH].astype(F32)
                wf1[ahead : ahead + CH, (2 - kt) * CH : (3 - kt) * CH] = jnp.transpose(block).astype(BF16)
    pl.semaphore_wait(barrier, devices - 1)
    x_sent = start_inputs(0, xl, xr, xe, xeb, xex)
    hand_on(0, 0, xr, xeb, xex)
    red_start(0, local_mean, local_spread)
    c_sent = start_inputs(1, cl, cr, ce, ceb, cex)
    zero_cells = jnp.zeros((cells, CH), F32)

    def clear(n, _):
        hid[n] = zero_cells
        g2[n] = zero_cells
        g1[n] = zero_cells
        return 0

    lax.fori_loop(0, frames + 2, clear, 0)
    zero_t = jnp.zeros((2 * CH, cells), BF16)
    act_t[0 : 2 * CH] = zero_t
    hg_t[frames * CH : (frames + 2) * CH] = zero_t

    row_place = lax.broadcasted_iota(jnp.int32, (strip, CH), 0)
    left_ok = jnp.logical_not(jnp.logical_and(w == 0, z == 0))
    right_ok = jnp.logical_not(jnp.logical_and(w == 1, z == nz - 1))

    def row_ok(r):
        if r == 0:
            return h > 0
        if r == rl + 1:
            return h < nh - 1
        return None

    def row_source(r):
        if r == 0:
            return 0, rl - 1
        if r == rl + 1:
            return 2, 0
        return 1, r - 1

    def store_stack(stack, f, r, value, left, right):
        ok = row_ok(r)
        left = jnp.where(left_ok if ok is None else jnp.logical_and(left_ok, ok), left, 0.0)
        right = jnp.where(right_ok if ok is None else jnp.logical_and(right_ok, ok), right, 0.0)
        if ok is not None:
            value = jnp.where(ok, value, 0.0)
        before = jnp.where(row_place == 0, left, pltpu.roll(value, 1, 0))
        after = jnp.where(row_place == strip - 1, right, pltpu.roll(value, strip - 1, 0))
        stack[f, r, :, 0:CH] = before.astype(BF16)
        stack[f, r, :, CH : 2 * CH] = value.astype(BF16)
        stack[f, r, :, 2 * CH : 3 * CH] = after.astype(BF16)

    edge_place = lax.broadcasted_iota(jnp.int32, (16, CH), 0)
    outer_mask = jnp.logical_and(takes_outer, edge_place % 2 == 1 - w)

    def input_stack(stack, source, landing, landing_out, apply, start):
        def step(f, _):
            edges = []
            for d in range(3):
                tile = jnp.where(outer_mask, landing_out[d, f].astype(F32), landing[d, f].astype(F32))
                edges.append(apply(tile))
            for r in range(rl + 2):
                d, row = row_source(r)
                tile = edges[d]
                store_stack(
                    stack, f, r, apply(source[f, r].astype(F32)),
                    tile[2 * row : 2 * row + 1], tile[2 * row + 1 : 2 * row + 2],
                )
            return 0

        lax.fori_loop(start, start + fl, step, 0)

    def window(stack, f):
        return [stack[f, kr : kr + rl].reshape(cells, 3 * CH) for kr in range(3)]

    def convolve(stack, weight, target, first=0, last=None):
        def step(f, _):
            product = jnp.dot(
                jnp.concatenate(window(stack, f), axis=1), weight[...], preferred_element_type=F32
            )
            for j in range(3):
                target[f + j] += product[:, j * CH : (j + 1) * CH]
            return 0

        lax.fori_loop(first, frames if last is None else last, step, 0)

    def weight_part(turned, stack, kr):
        left = jnp.concatenate([turned[f * CH : (f + 3) * CH, :] for f in range(frames)], axis=1)
        right = stack[:, kr : kr + rl].reshape(frames * cells, 3 * CH)
        return jnp.dot(left, right, preferred_element_type=F32)

    def peer(axis, j):
        if axis == "z":
            return dev(j, 0, 0)
        if axis == "x":
            return (z, lax.rem(hx + j, nx) * ny + hy, w)
        return (z, hx * ny + lax.rem(hy + j, ny), w)

    coords = {"z": z, "x": hx, "y": hy}
    orders = (("z", "y", "x"), ("y", "x", "z"), ("x", "z", "y"))
    half = 8
    span = half // ns
    tiles = span * 9
    piece = -(-tiles // ns)
    outs = (o1_ref, o2_ref)
    stage_at = {"core": 0, "a1": 1, "a2": 2, "a3": 3, "g2": 4, "g1": 5, "gc": 6}

    def sems(g, p, stage):
        return ar_send.at[g], ar_recv.at[g, p, stage_at[stage]]

    def arrived(g, p, stage, ref):
        take(ref, ar_recv.at[g, p, stage_at[stage]])

    def core_copy(g, p):
        return remote(a.at[g, p, pl.ds((1 - w) * half, half)], r0.at[g, p], *sems(g, p, "core"), dev(0, 0, 1))

    def core_start(g, p):
        core_copy(g, p).start()

    def a1_copies(g, p):
        axis = orders[p][0]
        return [
            remote(
                b1.at[g, p, pl.ds(lax.rem(coords[axis] + j, ns) * span, span)], r1.at[g, p, j - 1],
                *sems(g, p, "a1"), peer(axis, j),
            )
            for j in range(1, ns)
        ]

    def a1_start(g, p):
        arrived(g, p, "core", r0.at[g, p])
        b1[g, p] = a[g, p, pl.ds(w * half, half)] + r0[g, p]
        start_all(a1_copies(g, p))

    def a2_copies(g, p):
        axis = orders[p][1]
        return [
            remote(
                b2.at[g, p, pl.ds(lax.rem(coords[axis] + j, ns) * piece, piece)], r2.at[g, p, j - 1],
                *sems(g, p, "a2"), peer(axis, j),
            )
            for j in range(1, ns)
        ]

    def a2_start(g, p):
        arrived(g, p, "a1", r1.at[g, p])
        value = b1[g, p, pl.ds(coords[orders[p][0]] * span, span)]
        for j in range(ns - 1):
            value = value + r1[g, p, j]
        b2[g, p, 0:tiles] = value.reshape(tiles, 8, CH)
        if piece * ns > tiles:
            b2[g, p, tiles:] = jnp.zeros((piece * ns - tiles, 8, CH), F32)
        start_all(a2_copies(g, p))

    def a3_copies(g, p):
        axis = orders[p][2]
        slot = r3.at[g, p, coords[axis]]
        return [remote(slot, slot, *sems(g, p, "a3"), peer(axis, j)) for j in range(1, ns)]

    def a3_start(g, p):
        arrived(g, p, "a2", r2.at[g, p])
        value = b2[g, p, pl.ds(coords[orders[p][1]] * piece, piece)]
        for j in range(ns - 1):
            value = value + r2[g, p, j]
        r3[g, p, coords[orders[p][2]]] = value
        start_all(a3_copies(g, p))

    def g2_copies(g, p):
        axis = orders[p][1]
        part = g3.at[g, p, pl.ds(coords[axis] * piece, piece)]
        return [remote(part, part, *sems(g, p, "g2"), peer(axis, j)) for j in range(1, ns)]

    def g2_start(g, p):
        arrived(g, p, "a3", r3.at[g, p, pl.ds(0, ns - 1)])
        value = r3[g, p, 0]
        for n in range(1, ns):
            value = value + r3[g, p, n]
        g3[g, p, pl.ds(coords[orders[p][1]] * piece, piece)] = value
        start_all(g2_copies(g, p))

    def out_span(g, p, n):
        return outs[g].at[p, pl.ds(w * half + n * span, span)]

    def g1_copies(g, p):
        axis = orders[p][0]
        part = out_span(g, p, coords[axis])
        return [remote(part, part, *sems(g, p, "g1"), peer(axis, j)) for j in range(1, ns)]

    def gc_copy(g, p, j):
        part = out_span(g, p, lax.rem(coords[orders[p][0]] + ns - j, ns))
        return remote(part, part, *sems(g, p, "gc"), dev(0, 0, 1))

    def g1_start(g, p):
        arrived(g, p, "g2", g3.at[g, p, pl.ds(0, (ns - 1) * piece)])
        outs[g][p, pl.ds(w * half + coords[orders[p][0]] * span, span)] = g3[g, p, 0:tiles].reshape(span, 9, 8, CH)
        start_all(g1_copies(g, p))
        gc_copy(g, p, 0).start()

    def gc_start(g, p):
        arrived(g, p, "g1", outs[g].at[p, pl.ds(0, (ns - 1) * span)])
        for j in range(1, ns):
            gc_copy(g, p, j).start()

    def gc_end(g, p):
        arrived(g, p, "gc", outs[g].at[p, pl.ds(0, half)])
        for kt in range(3):
            for kc in range(3):
                block = outs[g][p, :, kt * 3 + kc].reshape(CH, CH)
                tap = 9 * kt + 3 * p + kc
                (fin1, fin2)[g][:, tap * CH : (tap + 1) * CH] = block if g == 0 else jnp.transpose(block)

    def ar_close(g):
        for p in range(3):
            wait_sends([core_copy(g, p)] + a1_copies(g, p) + a2_copies(g, p) + a3_copies(g, p))
            wait_sends(g2_copies(g, p) + g1_copies(g, p) + [gc_copy(g, p, j) for j in range(ns)])

    def each(stage, g):
        for p in range(3):
            stage(g, p)

    for dz in near_first[1:]:
        hand_on(0, dz, xr, xeb, xex)
    hand_on(1, 0, cr, ceb, cex)
    mean1, spread1 = moments_end(0)
    picks = lax.broadcasted_iota(jnp.int32, (CH // 4, CH), 1) // 4 == lax.broadcasted_iota(jnp.int32, (CH // 4, CH), 0)
    spread_exponent = jnp.dot(
        jnp.broadcast_to(exponent_ref[...].astype(F32), (8, CH // 4)), picks.astype(F32), preferred_element_type=F32
    )
    scale = jnp.exp2(spread_exponent[0:1])
    inv1 = 1.0 / jnp.sqrt(spread1 * (scale * scale) / total_size + EPS)
    factor1 = scale * inv1
    gain1, shift1 = gain1_ref[...], shift1_ref[...]
    gain2, shift2 = gain2_ref[...], shift2_ref[...]

    def rounded(value):
        return value.astype(BF16).astype(F32)

    def act_first(value):
        pre = (value - mean1) * factor1 * gain1 + shift1
        return rounded(pre * sigmoid(pre))

    for n, dz in enumerate(near_first):
        wait_pair(0, dz, xr, xeb, xex)
        start = pair_from(dz)
        input_stack(s1, xr, xeb, xex, act_first, start)
        convolve(s1, wf1, hid, start, start + fl)
        for later in (near_first[1:-1], near_first[-1:], [])[min(n, 2)]:
            hand_on(1, later, cr, ceb, cex)

    def hid_sum(n, total):
        return total + fold_rows(hid[n])

    mean_l = group_sum(total_row(lax.fori_loop(0, frames, hid_sum, zero8))) / local_size

    def hid_spread(n, total):
        off = hid[n] - mean_l
        return total + fold_rows(off * off)

    red_start(1, mean_l, group_sum(total_row(lax.fori_loop(0, frames, hid_spread, zero8))))

    for dz in near_first:
        wait_pair(1, dz, cr, ceb, cex)
        start = pair_from(dz)
        input_stack(sc, cr, ceb, cex, lambda value: value, start)
        convolve(sc, wb2, g2, start, start + fl)
    mean2, spread2 = moments_end(1)
    inv2 = 1.0 / jnp.sqrt(spread2 / total_size + EPS)

    def second(n, totals):
        first_total, second_total = totals
        normed = (hid[n] - mean2) * inv2
        pre = normed * gain2 + shift2
        sig = sigmoid(pre)
        act_t[pl.ds(pl.multiple_of((n + 2) * CH, CH), CH), :] = jnp.transpose(pre * sig).astype(BF16)
        scaled = g2[n + 2] * (sig * (1.0 + pre * (1.0 - sig))) * gain2
        nrm[n] = normed
        g2[n + 2] = scaled
        return first_total + fold_rows(scaled), second_total + fold_rows(scaled * normed)

    t1, t2 = lax.fori_loop(0, frames, second, (zero8, zero8))
    red_start(2, group_sum(total_row(t1)), group_sum(total_row(t2)))

    def put_second(kr):
        block = weight_part(act_t, sc, kr)
        for kt in range(3):
            for kc in range(3):
                part = block[kt * CH : (kt + 1) * CH, kc * CH : (kc + 1) * CH]
                a[1, 2 - kr, :, kt * 3 + (2 - kc)] = part.reshape(16, 8, CH)
        core_start(1, 2 - kr)

    for kr in range(3):
        put_second(kr)
    m1, m2 = sums_end(2)

    def hidden(n, _):
        value = inv2 * (g2[n + 2] - m1 - nrm[n] * m2)
        hg_t[pl.ds(pl.multiple_of(n * CH, CH), CH), :] = jnp.transpose(value).astype(BF16)
        narrow = value.astype(BF16)
        hg[n, 1 : rl + 1] = narrow.reshape(rl, strip, CH)
        wide = narrow.astype(F32).reshape(rl, strip, CH)
        lefts = jnp.zeros((16, CH), F32)
        rights = jnp.zeros((16, CH), F32)
        for r in range(rl):
            lefts = jnp.where(edge_place == r, wide[r, 0:1], lefts)
            rights = jnp.where(edge_place == r, wide[r, strip - 1 : strip], rights)
        eh[0, n] = lefts.astype(BF16)
        eh[1, n] = rights.astype(BF16)
        return 0

    lax.fori_loop(0, frames, hidden, 0)

    line = w * nz + z

    def beside(ds, dh):
        place = lax.rem(line + ds + 2 * nz, 2 * nz)
        return (lax.rem(place, nz), lax.rem(h + dh + nh, nh), place // nz)

    halo = [
        remote(hg.at[:, pl.ds(rl, 1)], hg.at[:, pl.ds(0, 1)], halo_send.at[0], halo_recv.at[0], dev(0, 1, 0)),
        remote(hg.at[:, pl.ds(1, 1)], hg.at[:, pl.ds(rl + 1, 1)], halo_send.at[0], halo_recv.at[0], dev(0, -1, 0)),
    ]
    for n, dh in enumerate((0, 1, -1)):
        halo.append(remote(eh.at[0], heb.at[1 - dh, 1], halo_send.at[0], halo_recv.at[1], beside(-1, dh)))
        halo.append(remote(eh.at[1], heb.at[1 - dh, 0], halo_send.at[0], halo_recv.at[1], beside(1, dh)))
    start_all(halo)
    each(a1_start, 1)

    def put_first(kr):
        block = weight_part(hg_t, s1, kr)
        for j in range(3):
            for kc in range(3):
                part = block[j * CH : (j + 1) * CH, kc * CH : (kc + 1) * CH]
                a[0, kr, :, (2 - j) * 3 + kc] = part.reshape(16, 8, CH)
        core_start(0, kr)

    put_first(0)
    put_first(1)
    a1_start(0, 0)
    put_first(2)
    a1_start(0, 1)
    a1_start(0, 2)
    each(a2_start, 1)
    take(hg.at[:, pl.ds(0, 2)], halo_recv.at[0])
    take(heb, halo_recv.at[1])

    def halo_stack(f, _):
        lefts = [heb[d, 0, f].astype(F32) for d in range(3)]
        rights = [heb[d, 1, f].astype(F32) for d in range(3)]
        for r in range(rl + 2):
            d, row = row_source(r)
            store_stack(sh, f, r, hg[f, r].astype(F32), lefts[d][row : row + 1], rights[d][row : row + 1])
        return 0

    lax.fori_loop(0, frames, halo_stack, 0)

    def first(f, totals):
        first_total, second_total = totals
        for r in range(rl):
            normed = (xr[f, r + 1].astype(F32) - mean1) * factor1
            pre = normed * gain1 + shift1
            sig = sigmoid(pre)
            scaled = g1[f + 2, r * strip : (r + 1) * strip] * (sig * (1.0 + pre * (1.0 - sig))) * gain1
            s_out[f, r] = scaled.astype(BF16)
            first_total = first_total + fold_rows(scaled)
            second_total = second_total + fold_rows(scaled * normed)
        return first_total, second_total

    back_from = s_in.at[:, :, pl.ds(pl.multiple_of(z * strip, strip), strip), :]
    back_copies = []

    def send_back(q):
        source = s_out.at[pl.ds(q * fl, fl)]
        far = remote(source, back_from, back_send.at[0], back_recv.at[0], (q, h, w))
        back_copies.append(far)

        @pl.when(z == q)
        def _():
            pltpu.make_async_copy(source, back_from, back_recv.at[0]).start()

        @pl.when(z != q)
        def _():
            far.start()

    convolve(sh, wb1, g1, 0, 2)
    each(a2_start, 0)
    each(a3_start, 1)
    totals = (zero8, zero8)
    for q in range(nz):
        if q * fl + 2 < frames:
            convolve(sh, wb1, g1, q * fl + 2, q * fl + fl + 2)
        totals = lax.fori_loop(q * fl, q * fl + fl, first, totals)
        send_back(q)
        if q == nz // 2 - 1:
            each(a3_start, 0)
            each(g2_start, 1)
    t1, t2 = totals
    red_start(3, group_sum(total_row(t1)), group_sum(total_row(t2)))
    each(g2_start, 0)
    each(g1_start, 1)
    each(g1_start, 0)
    m1, m2 = sums_end(3)
    take(s_in, back_recv.at[0])

    for f in range(fl):
        for r in range(rl):
            normed = (xl[f, r].astype(F32) - mean1) * factor1
            value = cl[f, r].astype(F32) + inv1 * (s_in[f, r].astype(F32) - m1 - normed * m2)
            out_ref[:, f, r, :] = jnp.transpose(value)
    each(gc_start, 1)
    each(gc_end, 1)
    close_inputs(0, x_sent, xr, xeb, xex)
    close_inputs(1, c_sent, cr, ceb, cex)
    for k in range(4):
        take(rb.at[k, pl.ds(0, devices - 1)], red_send.at[k])
    wait_sends(halo)
    for q in range(nz):

        @pl.when(z != q)
        def _():
            back_copies[q].wait_send()

    ar_close(1)
    each(gc_start, 0)
    each(gc_end, 0)
    ar_close(0)


def copy_body(*refs):
    sources, targets, store_sem = refs[0:3], refs[3:6], refs[6]
    stores = [pltpu.make_async_copy(sources[n], targets[n], store_sem.at[n]) for n in range(3)]
    for copy in stores:
        copy.start()
    for copy in stores:
        copy.wait()


def shards(sizes, latent, exponents, cotangent, conv_first, conv_second, gain_first, shift_first, gain_second, shift_second):
    nz, nh, nx, ny = sizes
    channels, fl, rl, cols = latent.shape
    strip = cols // nz
    frames = fl * nz
    cells = rl * strip
    ns = nx
    span = 8 // ns
    tiles = span * 9
    piece = -(-tiles // ns)
    vmem = pl.BlockSpec(memory_space=pltpu.VMEM)
    any_space = pl.BlockSpec(memory_space=pl.ANY)
    part = (3, 16, 9, 8, CH)
    wide = (frames, rl + 2, strip, 3 * CH)
    scratch = [
        pltpu.VMEM((CH, fl, rl, cols), BF16),
        pltpu.VMEM((CH, fl, rl, cols), BF16),
        pltpu.VMEM((fl, rl, cols, CH), BF16),
        pltpu.VMEM((fl, rl, cols, CH), BF16),
        pltpu.VMEM((CH, 27 * CH), BF16),
        pltpu.VMEM((CH, 27 * CH), BF16),
        pltpu.VMEM(part, F32),
        pltpu.VMEM(part, F32),
        pltpu.VMEM((frames, rl + 2, strip, CH), BF16),
        pltpu.VMEM((frames, rl + 2, strip, CH), BF16),
        pltpu.VMEM((nz + 1, fl, 16, CH), BF16),
        pltpu.VMEM((nz + 1, fl, 16, CH), BF16),
        pltpu.VMEM((3, frames, 16, CH), BF16),
        pltpu.VMEM((3, frames, 16, CH), BF16),
        pltpu.VMEM((3, frames, 16, CH), BF16),
        pltpu.VMEM((3, frames, 16, CH), BF16),
        pltpu.VMEM(wide, BF16),
        pltpu.VMEM(wide, BF16),
        pltpu.VMEM(wide, BF16),
        pltpu.VMEM((frames + 2, cells, CH), F32),
        pltpu.VMEM((frames + 2, cells, CH), F32),
        pltpu.VMEM((frames + 2, cells, CH), F32),
        pltpu.VMEM((frames, cells, CH), F32),
        pltpu.VMEM(((frames + 2) * CH, cells), BF16),
        pltpu.VMEM(((frames + 2) * CH, cells), BF16),
        pltpu.VMEM((frames, rl + 2, strip, CH), BF16),
        pltpu.VMEM((2, frames, 16, CH), BF16),
        pltpu.VMEM((3, 2, frames, 16, CH), BF16),
        pltpu.VMEM((9 * CH, 3 * CH), BF16),
        pltpu.VMEM((9 * CH, 3 * CH), BF16),
        pltpu.VMEM((9 * CH, 3 * CH), BF16),
        pltpu.VMEM((frames, rl, strip, CH), BF16),
        pltpu.VMEM((fl, rl, cols, CH), BF16),
        pltpu.VMEM((4, 2 * nz * nh, 1, CH), F32),
        pltpu.VMEM((2, 3, 16, 9, 8, CH), F32),
        pltpu.VMEM((2, 3, 8, 9, 8, CH), F32),
        pltpu.VMEM((2, 3, 8, 9, 8, CH), F32),
        pltpu.VMEM((2, 3, ns - 1, span, 9, 8, CH), F32),
        pltpu.VMEM((2, 3, piece * ns, 8, CH), F32),
        pltpu.VMEM((2, 3, ns - 1, piece, 8, CH), F32),
        pltpu.VMEM((2, 3, ns, piece, 8, CH), F32),
        pltpu.VMEM((2, 3, piece * ns, 8, CH), F32),
        pltpu.SemaphoreType.DMA((4,)),
        pltpu.SemaphoreType.DMA((2,)),
        pltpu.SemaphoreType.DMA((2, 6 * nz)),
        pltpu.SemaphoreType.DMA((4,)),
        pltpu.SemaphoreType.DMA((4,)),
        pltpu.SemaphoreType.DMA((1,)),
        pltpu.SemaphoreType.DMA((2,)),
        pltpu.SemaphoreType.DMA((1,)),
        pltpu.SemaphoreType.DMA((1,)),
        pltpu.SemaphoreType.DMA((2,)),
        pltpu.SemaphoreType.DMA((2, 3, 7)),
    ]
    results = pl.pallas_call(
        functools.partial(body, sizes),
        out_shape=(
            pltpu.VMEM((CH, fl, rl, cols), F32),
            pltpu.VMEM((CH, 27 * CH), F32),
            pltpu.VMEM((CH, 27 * CH), F32),
        ),
        in_specs=[any_space] * 4 + [vmem] * 5,
        out_specs=(vmem,) * 3,
        scratch_shapes=scratch,
        compiler_params=pltpu.CompilerParams(
            collective_id=0, has_side_effects=True, vmem_limit_bytes=48 * 1024 * 1024
        ),
    )(
        latent, cotangent, conv_first, conv_second, exponents[None],
        gain_first[None], shift_first[None], gain_second[None], shift_second[None],
    )
    return pl.pallas_call(
        copy_body,
        out_shape=[jax.ShapeDtypeStruct(value.shape, F32) for value in results],
        in_specs=[vmem] * 3,
        out_specs=[any_space] * 3,
        scratch_shapes=[pltpu.SemaphoreType.DMA((3,))],
        compiler_params=pltpu.CompilerParams(vmem_limit_bytes=8 * 1024 * 1024),
    )(*results)


def solution(mesh):
    nz, nh = mesh.shape["tm"], mesh.shape["height"]
    nx = int(round(nh**0.5))
    placed = P(None, "tm", "height", "width")
    return jax.shard_map(
        functools.partial(shards, (nz, nh, nx, nh // nx)),
        mesh=mesh,
        in_specs=(placed, P(), placed, P(), P(), P(), P(), P(), P()),
        out_specs=(placed, P(), P()),
        check_vma=False,
    )
```

```python
import functools

import jax
import jax.numpy as jnp
from jax import lax
from jax.experimental import pallas as pl
from jax.experimental.pallas import tpu as pltpu
from jax.sharding import PartitionSpec as P

MESH = pl.DeviceIdType.MESH
EPS = 1e-05
CH = 128
F32 = jnp.float32
BF16 = jnp.bfloat16


def group_sum(row):
    lane = lax.broadcasted_iota(jnp.int32, row.shape, 1)
    pair = row + jnp.where(lane % 2 == 0, pltpu.roll(row, CH - 1, 1), pltpu.roll(row, 1, 1))
    return pair + jnp.where(lane % 4 < 2, pltpu.roll(pair, CH - 2, 1), pltpu.roll(pair, 2, 1))


def fold_rows(cells):
    return jnp.sum(cells.reshape(-1, 8, CH), axis=0)


def total_row(partial):
    return jnp.sum(partial, axis=0, keepdims=True)


def lanes_low(row):
    return lax.broadcasted_iota(jnp.int32, row.shape, row.ndim - 1) % 4 < 2


def pack_pair(first, second):
    return jnp.where(lanes_low(first), first, second)


def unpack_pair(row):
    low = lanes_low(row)
    return jnp.where(low, row, pltpu.roll(row, 2, 1)), jnp.where(low, pltpu.roll(row, CH - 2, 1), row)


def far_first(n, size):
    if size == 4:
        return (2 + 3 * n + 3 * ((n * (n - 1)) // 2)) % 4
    return size - 1 - n


def sigmoid(value):
    return 1.0 / (1.0 + jnp.exp(-value))


def body(
    sizes,
    x_hbm, c_hbm, w1_hbm, w2_hbm, exponent_ref, gain1_ref, shift1_ref, gain2_ref, shift2_ref,
    out_ref, fin1, fin2,
    x_raw, c_raw, xl, cl, w1, w2, o1_ref, o2_ref,
    xr, cr, xe, ce, xeb, ceb, xex, cex, s1, sc, sh, hid, g2, g1, nrm, act_t, hg_t, hg, eh, heb,
    wf1, wb1, wb2, s_out, s_in, rb, a, r0, b1, r1, b2, r2, r3, g3,
    load_sem, in_send, in_recv, red_send, red_recv, halo_send, halo_recv, back_send, back_recv,
    ar_send, ar_recv,
):
    nz, nh, nx, ny = sizes
    ns = nx
    fl, rl, cols = xl.shape[0], xl.shape[1], xl.shape[2]
    strip = cols // nz
    frames = fl * nz
    cells = rl * strip
    z, h, w = lax.axis_index("tm"), lax.axis_index("height"), lax.axis_index("width")
    hx, hy = h // ny, h % ny

    def dev(dz, dh, dw):
        return (lax.rem(z + dz + nz, nz), lax.rem(h + dh + nh, nh), lax.rem(w + dw, 2))

    loads = [
        pltpu.make_async_copy(source, target, load_sem.at[n])
        for n, (source, target) in enumerate(((x_hbm, x_raw), (c_hbm, c_raw), (w1_hbm, w1), (w2_hbm, w2)))
    ]
    for copy in loads:
        copy.start()

    heights = [(ox, oy) for ox in range(nx) for oy in range(ny)]
    heights.sort(key=lambda place: -(min(place[0], nx - place[0]) + min(place[1], ny - place[1])))
    targets_h = [lax.rem(hx + ox, nx) * ny + lax.rem(hy + oy, ny) for ox, oy in heights]

    def for_each_device(act):
        def step(n, _):
            dz, dw = far_first(n // 2, nz), 1 - n % 2
            zt, wt = lax.rem(z + dz, nz), lax.rem(w + dw, 2)
            for ht in targets_h[:-1]:
                act((zt, ht, wt))

            @pl.when(n < 2 * nz - 1)
            def _():
                act((zt, h, wt))

            return 0

        lax.fori_loop(0, 2 * nz, step, 0)

    devices = 2 * nz * nh
    barrier = pltpu.get_barrier_semaphore()
    for dz in reversed(range(nz)):
        for dw in (1, 0):
            zt, wt = lax.rem(z + dz, nz), lax.rem(w + dw, 2)
            for ht in targets_h if (dz, dw) != (0, 0) else targets_h[:-1]:
                pl.semaphore_signal(barrier, inc=1, device_id=(zt, ht, wt), device_id_type=MESH)

    def take(ref, sem):
        pltpu.make_async_copy(ref, ref, sem).wait()

    def remote(src, dst, send, recv, where):
        return pltpu.make_async_remote_copy(
            src_ref=src, dst_ref=dst, send_sem=send, recv_sem=recv, device_id=where, device_id_type=MESH
        )

    own_frames = pl.ds(z * fl, fl)

    def strip_copies(k, src, dst, edges, landing):
        copies = []
        for dz in sorted(range(nz), key=lambda dz: -min(dz, nz - dz)):
            q = lax.rem(z + dz, nz)
            pieces = (
                (src.at[:, :, pl.ds(pl.multiple_of(q * strip, strip), strip), :],
                 dst.at[own_frames, pl.ds(1, rl)], in_recv.at[k, dz]),
                (edges.at[q], landing.at[1, own_frames], in_recv.at[k, nz + dz]),
            )
            for source, target, recv in pieces:
                if dz == 0:
                    copies.append((False, pltpu.make_async_copy(source, target, recv)))
                else:
                    copies.append((True, remote(source, target, in_send.at[k], recv, dev(dz, 0, 0))))
        return copies

    def build_edges(src, edges):
        def at(f, r, col):
            start = (col // 16) * 16
            return src[f, r, start : start + 16, :].astype(F32)[col % 16 : col % 16 + 1]

        place = lax.broadcasted_iota(jnp.int32, (16, CH), 0)
        for f in range(fl):
            for q in range(nz):
                tile = jnp.zeros((16, CH), F32)
                for r in range(rl):
                    if q > 0:
                        tile = jnp.where(place == 2 * r, at(f, r, q * strip - 1), tile)
                    if q < nz - 1:
                        tile = jnp.where(place == 2 * r + 1, at(f, r, (q + 1) * strip), tile)
                edges[q, f] = tile.astype(BF16)
            tile = jnp.zeros((16, CH), F32)
            for r in range(rl):
                outer = jnp.where(w == 0, at(f, r, cols - 1), at(f, r, 0))
                tile = jnp.where(place // 2 == r, outer, tile)
            edges[nz, f] = tile.astype(BF16)

    outer_q = (nz - 1) * w
    takes_outer = z == (nz - 1) * (1 - w)

    def outer_copy(k, edges, landing_out):
        recv = in_recv.at[k, 2 * nz + lax.rem(outer_q - z + nz, nz)]
        return remote(edges.at[nz], landing_out.at[1, own_frames], in_send.at[k], recv, (outer_q, h, 1 - w))

    def start_inputs(k, src, dst, edges, landing, landing_out):
        copies = strip_copies(k, src, dst, edges, landing)
        for _, copy in copies:
            copy.start()
        outer = outer_copy(k, edges, landing_out)
        outer.start()
        return [copy for far, copy in copies if far] + [outer]

    near_first = sorted(range(nz), key=lambda dz: min(dz, nz - dz))

    def pair_from(dz):
        return lax.rem(z - dz + nz, nz) * fl

    def beside_copies(k, dz, cells_in, landing):
        pair = pl.ds(pair_from(dz), fl)
        copies = []
        for dh, r_from, r_to in ((1, rl, 0), (-1, 1, rl + 1)):
            where = dev(0, dh, 0)
            copies.append(
                remote(cells_in.at[pair, pl.ds(r_from, 1)], cells_in.at[pair, pl.ds(r_to, 1)],
                       in_send.at[k], in_recv.at[k, 3 * nz + dz], where)
            )
            copies.append(
                remote(landing.at[1, pair], landing.at[1 - dh, pair], in_send.at[k], in_recv.at[k, 4 * nz + dz], where)
            )
        return copies

    def beside_outer(k, dz, landing_out):
        pair = pl.ds(pair_from(dz), fl)
        return [
            remote(landing_out.at[1, pair], landing_out.at[1 - dh, pair],
                   in_send.at[k], in_recv.at[k, 5 * nz + dz], dev(0, dh, 0))
            for dh in (1, -1)
        ]

    def hand_on(k, dz, cells_in, landing, landing_out):
        pair = pl.ds(pair_from(dz), fl)
        take(cells_in.at[pair, pl.ds(1, rl)], in_recv.at[k, dz])
        take(landing.at[1, pair], in_recv.at[k, nz + dz])
        start_all(beside_copies(k, dz, cells_in, landing))

        @pl.when(takes_outer)
        def _():
            take(landing_out.at[1, pair], in_recv.at[k, 2 * nz + dz])
            start_all(beside_outer(k, dz, landing_out))

    def wait_pair(k, dz, cells_in, landing, landing_out):
        pair = pl.ds(pair_from(dz), fl)
        take(cells_in.at[pair, pl.ds(0, 2)], in_recv.at[k, 3 * nz + dz])
        take(landing.at[pl.ds(0, 2), pair], in_recv.at[k, 4 * nz + dz])

        @pl.when(takes_outer)
        def _():
            take(landing_out.at[pl.ds(0, 2), pair], in_recv.at[k, 5 * nz + dz])

    def close_inputs(k, sent, cells_in, landing, landing_out):
        wait_sends(sent)
        for dz in range(nz):
            wait_sends(beside_copies(k, dz, cells_in, landing))

            @pl.when(takes_outer)
            def _():
                wait_sends(beside_outer(k, dz, landing_out))

    def start_all(copies):
        for copy in copies:
            copy.start()

    def wait_sends(copies):
        for copy in copies:
            copy.wait_send()

    me = (z * nh + h) * 2 + w
    local_size = 4.0 * fl * rl * cols
    total_size = local_size * devices

    def red_start(k, first, second):
        rb[k, me] = pack_pair(first, second)
        slot = rb.at[k, me]
        for_each_device(lambda where: remote(slot, slot, red_send.at[k], red_recv.at[k], where).start())

    def red_wait(k):
        take(rb.at[k, pl.ds(0, devices - 1)], red_recv.at[k])

    def moments_end(k):
        red_wait(k)
        rows = rb[k]
        mean, _ = unpack_pair(jnp.sum(rows, axis=0) / devices)
        low = lanes_low(rows)
        off = rows - jnp.where(lanes_low(mean), mean, 0.0)[None]
        between, within = unpack_pair(jnp.sum(jnp.where(low, off * off, off), axis=0))
        return mean, within + local_size * between

    def sums_end(k):
        red_wait(k)
        return unpack_pair(jnp.sum(rb[k], axis=0) / total_size)

    def turn(source, target):
        for f in range(fl):
            for r in range(rl):
                target[f, r] = jnp.transpose(source[:, f, r, :].astype(F32)).astype(BF16)

    loads[0].wait()
    turn(x_raw, xl)
    build_edges(xl, xe)
    zero8 = jnp.zeros((8, CH), F32)

    def x_sum(n, total):
        return total + fold_rows(xl[n // rl, n % rl].astype(F32))

    local_mean = group_sum(total_row(lax.fori_loop(0, fl * rl, x_sum, zero8))) / local_size

    def x_spread(n, total):
        off = xl[n // rl, n % rl].astype(F32) - local_mean
        return total + fold_rows(off * off)

    local_spread = group_sum(total_row(lax.fori_loop(0, fl * rl, x_spread, zero8)))

    loads[1].wait()
    turn(c_raw, cl)
    build_edges(cl, ce)
    loads[2].wait()
    loads[3].wait()
    for kt in range(3):
        for kr in range(3):
            for kc in range(3):
                tap = 9 * kt + 3 * kr + kc
                back = ((2 - kr) * 3 + (2 - kc)) * CH
                for source, target in ((w1, wb1), (w2, wb2)):
                    target[back : back + CH, kt * CH : (kt + 1) * CH] = source[:, tap * CH : (tap + 1) * CH]
    for kt in range(3):
        for kr in range(3):
            for kc in range(3):
                tap = 9 * kt + 3 * kr + kc
                ahead = (kr * 3 + kc) * CH
                block = w1[:, tap * CH : (tap + 1) * CH].astype(F32)
                wf1[ahead : ahead + CH, (2 - kt) * CH : (3 - kt) * CH] = jnp.transpose(block).astype(BF16)
    pl.semaphore_wait(barrier, devices - 1)
    x_sent = start_inputs(0, xl, xr, xe, xeb, xex)
    red_start(0, local_mean, local_spread)
    c_sent = start_inputs(1, cl, cr, ce, ceb, cex)
    hand_on(0, 0, xr, xeb, xex)
    zero_cells = jnp.zeros((cells, CH), F32)

    def clear(n, _):
        hid[n] = zero_cells
        g2[n] = zero_cells
        g1[n] = zero_cells
        return 0

    lax.fori_loop(0, frames + 2, clear, 0)
    zero_t = jnp.zeros((2 * CH, cells), BF16)
    act_t[0 : 2 * CH] = zero_t
    hg_t[frames * CH : (frames + 2) * CH] = zero_t

    row_place = lax.broadcasted_iota(jnp.int32, (strip, CH), 0)
    left_ok = jnp.logical_not(jnp.logical_and(w == 0, z == 0))
    right_ok = jnp.logical_not(jnp.logical_and(w == 1, z == nz - 1))

    def row_ok(r):
        if r == 0:
            return h > 0
        if r == rl + 1:
            return h < nh - 1
        return None

    def row_source(r):
        if r == 0:
            return 0, rl - 1
        if r == rl + 1:
            return 2, 0
        return 1, r - 1

    def store_stack(stack, f, r, value, left, right):
        ok = row_ok(r)
        left = jnp.where(left_ok if ok is None else jnp.logical_and(left_ok, ok), left, 0.0)
        right = jnp.where(right_ok if ok is None else jnp.logical_and(right_ok, ok), right, 0.0)
        if ok is not None:
            value = jnp.where(ok, value, 0.0)
        before = jnp.where(row_place == 0, left, pltpu.roll(value, 1, 0))
        after = jnp.where(row_place == strip - 1, right, pltpu.roll(value, strip - 1, 0))
        stack[f, r, :, 0:CH] = before.astype(BF16)
        stack[f, r, :, CH : 2 * CH] = value.astype(BF16)
        stack[f, r, :, 2 * CH : 3 * CH] = after.astype(BF16)

    edge_place = lax.broadcasted_iota(jnp.int32, (16, CH), 0)
    outer_mask = jnp.logical_and(takes_outer, edge_place % 2 == 1 - w)

    def input_stack(stack, source, landing, landing_out, apply, start):
        def step(f, _):
            edges = []
            for d in range(3):
                tile = jnp.where(outer_mask, landing_out[d, f].astype(F32), landing[d, f].astype(F32))
                edges.append(apply(tile))
            for r in range(rl + 2):
                d, row = row_source(r)
                tile = edges[d]
                store_stack(
                    stack, f, r, apply(source[f, r].astype(F32)),
                    tile[2 * row : 2 * row + 1], tile[2 * row + 1 : 2 * row + 2],
                )
            return 0

        lax.fori_loop(start, start + fl, step, 0)

    def window(stack, f):
        return [stack[f, kr : kr + rl].reshape(cells, 3 * CH) for kr in range(3)]

    def convolve(stack, weight, target, first=0, last=None):
        def step(f, _):
            product = jnp.dot(
                jnp.concatenate(window(stack, f), axis=1), weight[...], preferred_element_type=F32
            )
            for j in range(3):
                target[f + j] += product[:, j * CH : (j + 1) * CH]
            return 0

        lax.fori_loop(first, frames if last is None else last, step, 0)

    def weight_part(turned, stack, kr):
        left = jnp.concatenate([turned[f * CH : (f + 3) * CH, :] for f in range(frames)], axis=1)
        right = stack[:, kr : kr + rl].reshape(frames * cells, 3 * CH)
        return jnp.dot(left, right, preferred_element_type=F32)

    def peer(axis, j):
        if axis == "z":
            return dev(j, 0, 0)
        if axis == "x":
            return (z, lax.rem(hx + j, nx) * ny + hy, w)
        return (z, hx * ny + lax.rem(hy + j, ny), w)

    coords = {"z": z, "x": hx, "y": hy}
    orders = (("z", "y", "x"), ("y", "x", "z"), ("x", "z", "y"))
    half = 8
    span = half // ns
    tiles = span * 9
    piece = -(-tiles // ns)
    outs = (o1_ref, o2_ref)
    stage_at = {"core": 0, "a1": 1, "a2": 2, "a3": 3, "g2": 4, "g1": 5, "gc": 6}

    def sems(g, p, stage):
        return ar_send.at[g], ar_recv.at[g, p, stage_at[stage]]

    def arrived(g, p, stage, ref):
        take(ref, ar_recv.at[g, p, stage_at[stage]])

    def core_copy(g, p):
        return remote(a.at[g, p, pl.ds((1 - w) * half, half)], r0.at[g, p], *sems(g, p, "core"), dev(0, 0, 1))

    def core_start(g, p):
        core_copy(g, p).start()

    def a1_copies(g, p):
        axis = orders[p][0]
        return [
            remote(
                b1.at[g, p, pl.ds(lax.rem(coords[axis] + j, ns) * span, span)], r1.at[g, p, j - 1],
                *sems(g, p, "a1"), peer(axis, j),
            )
            for j in range(1, ns)
        ]

    def a1_start(g, p):
        arrived(g, p, "core", r0.at[g, p])
        b1[g, p] = a[g, p, pl.ds(w * half, half)] + r0[g, p]
        start_all(a1_copies(g, p))

    def a2_copies(g, p):
        axis = orders[p][1]
        return [
            remote(
                b2.at[g, p, pl.ds(lax.rem(coords[axis] + j, ns) * piece, piece)], r2.at[g, p, j - 1],
                *sems(g, p, "a2"), peer(axis, j),
            )
            for j in range(1, ns)
        ]

    def a2_start(g, p):
        arrived(g, p, "a1", r1.at[g, p])
        value = b1[g, p, pl.ds(coords[orders[p][0]] * span, span)]
        for j in range(ns - 1):
            value = value + r1[g, p, j]
        b2[g, p, 0:tiles] = value.reshape(tiles, 8, CH)
        if piece * ns > tiles:
            b2[g, p, tiles:] = jnp.zeros((piece * ns - tiles, 8, CH), F32)
        start_all(a2_copies(g, p))

    def a3_copies(g, p):
        axis = orders[p][2]
        slot = r3.at[g, p, coords[axis]]
        return [remote(slot, slot, *sems(g, p, "a3"), peer(axis, j)) for j in range(1, ns)]

    def a3_start(g, p):
        arrived(g, p, "a2", r2.at[g, p])
        value = b2[g, p, pl.ds(coords[orders[p][1]] * piece, piece)]
        for j in range(ns - 1):
            value = value + r2[g, p, j]
        r3[g, p, coords[orders[p][2]]] = value
        start_all(a3_copies(g, p))

    def g2_copies(g, p):
        axis = orders[p][1]
        part = g3.at[g, p, pl.ds(coords[axis] * piece, piece)]
        return [remote(part, part, *sems(g, p, "g2"), peer(axis, j)) for j in range(1, ns)]

    def g2_start(g, p):
        arrived(g, p, "a3", r3.at[g, p, pl.ds(0, ns - 1)])
        value = r3[g, p, 0]
        for n in range(1, ns):
            value = value + r3[g, p, n]
        g3[g, p, pl.ds(coords[orders[p][1]] * piece, piece)] = value
        start_all(g2_copies(g, p))

    def out_span(g, p, n):
        return outs[g].at[p, pl.ds(w * half + n * span, span)]

    def g1_copies(g, p):
        axis = orders[p][0]
        part = out_span(g, p, coords[axis])
        return [remote(part, part, *sems(g, p, "g1"), peer(axis, j)) for j in range(1, ns)]

    def gc_copy(g, p, j):
        part = out_span(g, p, lax.rem(coords[orders[p][0]] + ns - j, ns))
        return remote(part, part, *sems(g, p, "gc"), dev(0, 0, 1))

    def g1_start(g, p):
        arrived(g, p, "g2", g3.at[g, p, pl.ds(0, (ns - 1) * piece)])
        outs[g][p, pl.ds(w * half + coords[orders[p][0]] * span, span)] = g3[g, p, 0:tiles].reshape(span, 9, 8, CH)
        start_all(g1_copies(g, p))
        gc_copy(g, p, 0).start()

    def gc_start(g, p):
        arrived(g, p, "g1", outs[g].at[p, pl.ds(0, (ns - 1) * span)])
        for j in range(1, ns):
            gc_copy(g, p, j).start()

    def gc_end(g, p):
        arrived(g, p, "gc", outs[g].at[p, pl.ds(0, half)])
        for kt in range(3):
            for kc in range(3):
                block = outs[g][p, :, kt * 3 + kc].reshape(CH, CH)
                tap = 9 * kt + 3 * p + kc
                (fin1, fin2)[g][:, tap * CH : (tap + 1) * CH] = block if g == 0 else jnp.transpose(block)

    def ar_close(g):
        for p in range(3):
            wait_sends([core_copy(g, p)] + a1_copies(g, p) + a2_copies(g, p) + a3_copies(g, p))
            wait_sends(g2_copies(g, p) + g1_copies(g, p) + [gc_copy(g, p, j) for j in range(ns)])

    def each(stage, g):
        for p in range(3):
            stage(g, p)

    for dz in near_first[1:]:
        hand_on(0, dz, xr, xeb, xex)
    mean1, spread1 = moments_end(0)
    picks = lax.broadcasted_iota(jnp.int32, (CH // 4, CH), 1) // 4 == lax.broadcasted_iota(jnp.int32, (CH // 4, CH), 0)
    spread_exponent = jnp.dot(
        jnp.broadcast_to(exponent_ref[...].astype(F32), (8, CH // 4)), picks.astype(F32), preferred_element_type=F32
    )
    scale = jnp.exp2(spread_exponent[0:1])
    inv1 = 1.0 / jnp.sqrt(spread1 * (scale * scale) / total_size + EPS)
    factor1 = scale * inv1
    gain1, shift1 = gain1_ref[...], shift1_ref[...]
    gain2, shift2 = gain2_ref[...], shift2_ref[...]

    def rounded(value):
        return value.astype(BF16).astype(F32)

    def act_first(value):
        pre = (value - mean1) * factor1 * gain1 + shift1
        return rounded(pre * sigmoid(pre))

    for n, dz in enumerate(near_first):
        wait_pair(0, dz, xr, xeb, xex)
        start = pair_from(dz)
        input_stack(s1, xr, xeb, xex, act_first, start)
        convolve(s1, wf1, hid, start, start + fl)
        hand_on(1, dz, cr, ceb, cex)

    def hid_sum(n, total):
        return total + fold_rows(hid[n])

    mean_l = group_sum(total_row(lax.fori_loop(0, frames, hid_sum, zero8))) / local_size

    def hid_spread(n, total):
        off = hid[n] - mean_l
        return total + fold_rows(off * off)

    red_start(1, mean_l, group_sum(total_row(lax.fori_loop(0, frames, hid_spread, zero8))))

    for dz in near_first:
        wait_pair(1, dz, cr, ceb, cex)
        start = pair_from(dz)
        input_stack(sc, cr, ceb, cex, lambda value: value, start)
        convolve(sc, wb2, g2, start, start + fl)
    mean2, spread2 = moments_end(1)
    inv2 = 1.0 / jnp.sqrt(spread2 / total_size + EPS)

    def second(n, totals):
        first_total, second_total = totals
        normed = (hid[n] - mean2) * inv2
        pre = normed * gain2 + shift2
        sig = sigmoid(pre)
        act_t[pl.ds(pl.multiple_of((n + 2) * CH, CH), CH), :] = jnp.transpose(pre * sig).astype(BF16)
        scaled = g2[n + 2] * (sig * (1.0 + pre * (1.0 - sig))) * gain2
        nrm[n] = normed
        g2[n + 2] = scaled
        return first_total + fold_rows(scaled), second_total + fold_rows(scaled * normed)

    t1, t2 = lax.fori_loop(0, frames, second, (zero8, zero8))
    red_start(2, group_sum(total_row(t1)), group_sum(total_row(t2)))

    def put_second(kr):
        block = weight_part(act_t, sc, kr)
        for kt in range(3):
            for kc in range(3):
                part = block[kt * CH : (kt + 1) * CH, kc * CH : (kc + 1) * CH]
                a[1, 2 - kr, :, kt * 3 + (2 - kc)] = part.reshape(16, 8, CH)
        core_start(1, 2 - kr)

    for kr in range(3):
        put_second(kr)
    each(a1_start, 1)
    m1, m2 = sums_end(2)

    def hidden(n, _):
        value = inv2 * (g2[n + 2] - m1 - nrm[n] * m2)
        hg_t[pl.ds(pl.multiple_of(n * CH, CH), CH), :] = jnp.transpose(value).astype(BF16)
        narrow = value.astype(BF16)
        hg[n, 1 : rl + 1] = narrow.reshape(rl, strip, CH)
        wide = narrow.astype(F32).reshape(rl, strip, CH)
        lefts = jnp.zeros((16, CH), F32)
        rights = jnp.zeros((16, CH), F32)
        for r in range(rl):
            lefts = jnp.where(edge_place == r, wide[r, 0:1], lefts)
            rights = jnp.where(edge_place == r, wide[r, strip - 1 : strip], rights)
        eh[0, n] = lefts.astype(BF16)
        eh[1, n] = rights.astype(BF16)
        return 0

    lax.fori_loop(0, frames, hidden, 0)

    line = w * nz + z

    def beside(ds, dh):
        place = lax.rem(line + ds + 2 * nz, 2 * nz)
        return (lax.rem(place, nz), lax.rem(h + dh + nh, nh), place // nz)

    halo = [
        remote(hg.at[:, pl.ds(rl, 1)], hg.at[:, pl.ds(0, 1)], halo_send.at[0], halo_recv.at[0], dev(0, 1, 0)),
        remote(hg.at[:, pl.ds(1, 1)], hg.at[:, pl.ds(rl + 1, 1)], halo_send.at[0], halo_recv.at[0], dev(0, -1, 0)),
    ]
    for n, dh in enumerate((0, 1, -1)):
        halo.append(remote(eh.at[0], heb.at[1 - dh, 1], halo_send.at[0], halo_recv.at[1], beside(-1, dh)))
        halo.append(remote(eh.at[1], heb.at[1 - dh, 0], halo_send.at[0], halo_recv.at[1], beside(1, dh)))
    start_all(halo)

    def put_first(kr):
        block = weight_part(hg_t, s1, kr)
        for j in range(3):
            for kc in range(3):
                part = block[j * CH : (j + 1) * CH, kc * CH : (kc + 1) * CH]
                a[0, kr, :, (2 - j) * 3 + kc] = part.reshape(16, 8, CH)
        core_start(0, kr)

    put_first(0)
    put_first(1)
    a1_start(0, 0)
    put_first(2)
    a1_start(0, 1)
    a1_start(0, 2)
    each(a2_start, 1)
    take(hg.at[:, pl.ds(0, 2)], halo_recv.at[0])
    take(heb, halo_recv.at[1])

    def halo_stack(f, _):
        lefts = [heb[d, 0, f].astype(F32) for d in range(3)]
        rights = [heb[d, 1, f].astype(F32) for d in range(3)]
        for r in range(rl + 2):
            d, row = row_source(r)
            store_stack(sh, f, r, hg[f, r].astype(F32), lefts[d][row : row + 1], rights[d][row : row + 1])
        return 0

    lax.fori_loop(0, frames, halo_stack, 0)

    def first(f, totals):
        first_total, second_total = totals
        for r in range(rl):
            normed = (xr[f, r + 1].astype(F32) - mean1) * factor1
            pre = normed * gain1 + shift1
            sig = sigmoid(pre)
            scaled = g1[f + 2, r * strip : (r + 1) * strip] * (sig * (1.0 + pre * (1.0 - sig))) * gain1
            s_out[f, r] = scaled.astype(BF16)
            first_total = first_total + fold_rows(scaled)
            second_total = second_total + fold_rows(scaled * normed)
        return first_total, second_total

    back_from = s_in.at[:, :, pl.ds(pl.multiple_of(z * strip, strip), strip), :]
    back_copies = []

    def send_back(q):
        source = s_out.at[pl.ds(q * fl, fl)]
        far = remote(source, back_from, back_send.at[0], back_recv.at[0], (q, h, w))
        back_copies.append(far)

        @pl.when(z == q)
        def _():
            pltpu.make_async_copy(source, back_from, back_recv.at[0]).start()

        @pl.when(z != q)
        def _():
            far.start()

    convolve(sh, wb1, g1, 0, 2)
    each(a2_start, 0)
    each(a3_start, 1)
    totals = (zero8, zero8)
    for q in range(nz):
        if q * fl + 2 < frames:
            convolve(sh, wb1, g1, q * fl + 2, q * fl + fl + 2)
        totals = lax.fori_loop(q * fl, q * fl + fl, first, totals)
        send_back(q)
        if q == nz // 2 - 1:
            each(a3_start, 0)
            each(g2_start, 1)
    t1, t2 = totals
    red_start(3, group_sum(total_row(t1)), group_sum(total_row(t2)))
    each(g2_start, 0)
    each(g1_start, 1)
    each(g1_start, 0)
    m1, m2 = sums_end(3)
    take(s_in, back_recv.at[0])

    for f in range(fl):
        for r in range(rl):
            normed = (xl[f, r].astype(F32) - mean1) * factor1
            value = cl[f, r].astype(F32) + inv1 * (s_in[f, r].astype(F32) - m1 - normed * m2)
            out_ref[:, f, r, :] = jnp.transpose(value)
    each(gc_start, 1)
    each(gc_end, 1)
    close_inputs(0, x_sent, xr, xeb, xex)
    close_inputs(1, c_sent, cr, ceb, cex)
    for k in range(4):
        take(rb.at[k, pl.ds(0, devices - 1)], red_send.at[k])
    wait_sends(halo)
    for q in range(nz):

        @pl.when(z != q)
        def _():
            back_copies[q].wait_send()

    ar_close(1)
    each(gc_start, 0)
    each(gc_end, 0)
    ar_close(0)


def copy_body(*refs):
    sources, targets, store_sem = refs[0:3], refs[3:6], refs[6]
    stores = [pltpu.make_async_copy(sources[n], targets[n], store_sem.at[n]) for n in range(3)]
    for copy in stores:
        copy.start()
    for copy in stores:
        copy.wait()


def shards(sizes, latent, exponents, cotangent, conv_first, conv_second, gain_first, shift_first, gain_second, shift_second):
    nz, nh, nx, ny = sizes
    channels, fl, rl, cols = latent.shape
    strip = cols // nz
    frames = fl * nz
    cells = rl * strip
    ns = nx
    span = 8 // ns
    tiles = span * 9
    piece = -(-tiles // ns)
    vmem = pl.BlockSpec(memory_space=pltpu.VMEM)
    any_space = pl.BlockSpec(memory_space=pl.ANY)
    part = (3, 16, 9, 8, CH)
    wide = (frames, rl + 2, strip, 3 * CH)
    scratch = [
        pltpu.VMEM((CH, fl, rl, cols), BF16),
        pltpu.VMEM((CH, fl, rl, cols), BF16),
        pltpu.VMEM((fl, rl, cols, CH), BF16),
        pltpu.VMEM((fl, rl, cols, CH), BF16),
        pltpu.VMEM((CH, 27 * CH), BF16),
        pltpu.VMEM((CH, 27 * CH), BF16),
        pltpu.VMEM(part, F32),
        pltpu.VMEM(part, F32),
        pltpu.VMEM((frames, rl + 2, strip, CH), BF16),
        pltpu.VMEM((frames, rl + 2, strip, CH), BF16),
        pltpu.VMEM((nz + 1, fl, 16, CH), BF16),
        pltpu.VMEM((nz + 1, fl, 16, CH), BF16),
        pltpu.VMEM((3, frames, 16, CH), BF16),
        pltpu.VMEM((3, frames, 16, CH), BF16),
        pltpu.VMEM((3, frames, 16, CH), BF16),
        pltpu.VMEM((3, frames, 16, CH), BF16),
        pltpu.VMEM(wide, BF16),
        pltpu.VMEM(wide, BF16),
        pltpu.VMEM(wide, BF16),
        pltpu.VMEM((frames + 2, cells, CH), F32),
        pltpu.VMEM((frames + 2, cells, CH), F32),
        pltpu.VMEM((frames + 2, cells, CH), F32),
        pltpu.VMEM((frames, cells, CH), F32),
        pltpu.VMEM(((frames + 2) * CH, cells), BF16),
        pltpu.VMEM(((frames + 2) * CH, cells), BF16),
        pltpu.VMEM((frames, rl + 2, strip, CH), BF16),
        pltpu.VMEM((2, frames, 16, CH), BF16),
        pltpu.VMEM((3, 2, frames, 16, CH), BF16),
        pltpu.VMEM((9 * CH, 3 * CH), BF16),
        pltpu.VMEM((9 * CH, 3 * CH), BF16),
        pltpu.VMEM((9 * CH, 3 * CH), BF16),
        pltpu.VMEM((frames, rl, strip, CH), BF16),
        pltpu.VMEM((fl, rl, cols, CH), BF16),
        pltpu.VMEM((4, 2 * nz * nh, 1, CH), F32),
        pltpu.VMEM((2, 3, 16, 9, 8, CH), F32),
        pltpu.VMEM((2, 3, 8, 9, 8, CH), F32),
        pltpu.VMEM((2, 3, 8, 9, 8, CH), F32),
        pltpu.VMEM((2, 3, ns - 1, span, 9, 8, CH), F32),
        pltpu.VMEM((2, 3, piece * ns, 8, CH), F32),
        pltpu.VMEM((2, 3, ns - 1, piece, 8, CH), F32),
        pltpu.VMEM((2, 3, ns, piece, 8, CH), F32),
        pltpu.VMEM((2, 3, piece * ns, 8, CH), F32),
        pltpu.SemaphoreType.DMA((4,)),
        pltpu.SemaphoreType.DMA((2,)),
        pltpu.SemaphoreType.DMA((2, 6 * nz)),
        pltpu.SemaphoreType.DMA((4,)),
        pltpu.SemaphoreType.DMA((4,)),
        pltpu.SemaphoreType.DMA((1,)),
        pltpu.SemaphoreType.DMA((2,)),
        pltpu.SemaphoreType.DMA((1,)),
        pltpu.SemaphoreType.DMA((1,)),
        pltpu.SemaphoreType.DMA((2,)),
        pltpu.SemaphoreType.DMA((2, 3, 7)),
    ]
    results = pl.pallas_call(
        functools.partial(body, sizes),
        out_shape=(
            pltpu.VMEM((CH, fl, rl, cols), F32),
            pltpu.VMEM((CH, 27 * CH), F32),
            pltpu.VMEM((CH, 27 * CH), F32),
        ),
        in_specs=[any_space] * 4 + [vmem] * 5,
        out_specs=(vmem,) * 3,
        scratch_shapes=scratch,
        compiler_params=pltpu.CompilerParams(
            collective_id=0, has_side_effects=True, vmem_limit_bytes=58 * 1024 * 1024
        ),
    )(
        latent, cotangent, conv_first, conv_second, exponents[None],
        gain_first[None], shift_first[None], gain_second[None], shift_second[None],
    )
    return pl.pallas_call(
        copy_body,
        out_shape=[jax.ShapeDtypeStruct(value.shape, F32) for value in results],
        in_specs=[vmem] * 3,
        out_specs=[any_space] * 3,
        scratch_shapes=[pltpu.SemaphoreType.DMA((3,))],
        compiler_params=pltpu.CompilerParams(vmem_limit_bytes=8 * 1024 * 1024),
    )(*results)


def solution(mesh):
    nz, nh = mesh.shape["tm"], mesh.shape["height"]
    nx = int(round(nh**0.5))
    placed = P(None, "tm", "height", "width")
    return jax.shard_map(
        functools.partial(shards, (nz, nh, nx, nh // nx)),
        mesh=mesh,
        in_specs=(placed, P(), placed, P(), P(), P(), P(), P(), P()),
        out_specs=(placed, P(), P()),
        check_vma=False,
    )
```

```python
import functools

import jax
import jax.numpy as jnp
from jax import lax
from jax.experimental import pallas as pl
from jax.experimental.pallas import tpu as pltpu
from jax.sharding import PartitionSpec as P

MESH = pl.DeviceIdType.MESH
EPS = 1e-05
CH = 128
F32 = jnp.float32
BF16 = jnp.bfloat16


def group_sum(row):
    lane = lax.broadcasted_iota(jnp.int32, row.shape, 1)
    pair = row + jnp.where(lane % 2 == 0, pltpu.roll(row, CH - 1, 1), pltpu.roll(row, 1, 1))
    return pair + jnp.where(lane % 4 < 2, pltpu.roll(pair, CH - 2, 1), pltpu.roll(pair, 2, 1))


def fold_rows(cells):
    return jnp.sum(cells.reshape(-1, 8, CH), axis=0)


def total_row(partial):
    return jnp.sum(partial, axis=0, keepdims=True)


def lanes_low(row):
    return lax.broadcasted_iota(jnp.int32, row.shape, row.ndim - 1) % 4 < 2


def pack_pair(first, second):
    return jnp.where(lanes_low(first), first, second)


def unpack_pair(row):
    low = lanes_low(row)
    return jnp.where(low, row, pltpu.roll(row, 2, 1)), jnp.where(low, pltpu.roll(row, CH - 2, 1), row)


def far_first(n, size):
    if size == 4:
        return (2 + 3 * n + 3 * ((n * (n - 1)) // 2)) % 4
    return size - 1 - n


def sigmoid(value):
    return 1.0 / (1.0 + jnp.exp(-value))


def body(
    sizes,
    x_hbm, c_hbm, w1_hbm, w2_hbm, exponent_ref, gain1_ref, shift1_ref, gain2_ref, shift2_ref,
    out_ref, fin1, fin2,
    x_raw, c_raw, xl, cl, w1, w2, o1_ref, o2_ref,
    xr, cr, xe, ce, xeb, ceb, xex, cex, s1, sc, sh, hid, g2, g1, nrm, act_t, hg_t, hg, eh, heb,
    wf1, wb1, wb2, s_out, s_in, rb, a, r0, b1, r1, b2, r2, r3, g3,
    load_sem, in_send, in_recv, red_send, red_recv, halo_send, halo_recv, back_send, back_recv,
    ar_send, ar_recv,
):
    nz, nh, nx, ny = sizes
    ns = nx
    fl, rl, cols = xl.shape[0], xl.shape[1], xl.shape[2]
    strip = cols // nz
    frames = fl * nz
    cells = rl * strip
    z, h, w = lax.axis_index("tm"), lax.axis_index("height"), lax.axis_index("width")
    hx, hy = h // ny, h % ny

    def dev(dz, dh, dw):
        return (lax.rem(z + dz + nz, nz), lax.rem(h + dh + nh, nh), lax.rem(w + dw, 2))

    loads = [
        pltpu.make_async_copy(source, target, load_sem.at[n])
        for n, (source, target) in enumerate(((x_hbm, x_raw), (c_hbm, c_raw), (w1_hbm, w1), (w2_hbm, w2)))
    ]
    for copy in loads:
        copy.start()

    heights = [(ox, oy) for ox in range(nx) for oy in range(ny)]
    heights.sort(key=lambda place: -(min(place[0], nx - place[0]) + min(place[1], ny - place[1])))
    targets_h = [lax.rem(hx + ox, nx) * ny + lax.rem(hy + oy, ny) for ox, oy in heights]

    def for_each_device(act):
        def step(n, _):
            dz, dw = far_first(n // 2, nz), 1 - n % 2
            zt, wt = lax.rem(z + dz, nz), lax.rem(w + dw, 2)
            for ht in targets_h[:-1]:
                act((zt, ht, wt))

            @pl.when(n < 2 * nz - 1)
            def _():
                act((zt, h, wt))

            return 0

        lax.fori_loop(0, 2 * nz, step, 0)

    devices = 2 * nz * nh
    barrier = pltpu.get_barrier_semaphore()
    for dz in reversed(range(nz)):
        for dw in (1, 0):
            zt, wt = lax.rem(z + dz, nz), lax.rem(w + dw, 2)
            for ht in targets_h if (dz, dw) != (0, 0) else targets_h[:-1]:
                pl.semaphore_signal(barrier, inc=1, device_id=(zt, ht, wt), device_id_type=MESH)

    def take(ref, sem):
        pltpu.make_async_copy(ref, ref, sem).wait()

    def remote(src, dst, send, recv, where):
        return pltpu.make_async_remote_copy(
            src_ref=src, dst_ref=dst, send_sem=send, recv_sem=recv, device_id=where, device_id_type=MESH
        )

    own_frames = pl.ds(z * fl, fl)

    def strip_copies(k, src, dst, edges, landing):
        copies = []
        for dz in sorted(range(nz), key=lambda dz: -min(dz, nz - dz)):
            q = lax.rem(z + dz, nz)
            pieces = (
                (src.at[:, :, pl.ds(pl.multiple_of(q * strip, strip), strip), :],
                 dst.at[own_frames, pl.ds(1, rl)], in_recv.at[k, dz]),
                (edges.at[q], landing.at[1, own_frames], in_recv.at[k, nz + dz]),
            )
            for source, target, recv in pieces:
                if dz == 0:
                    copies.append((False, pltpu.make_async_copy(source, target, recv)))
                else:
                    copies.append((True, remote(source, target, in_send.at[k], recv, dev(dz, 0, 0))))
        return copies

    def build_edges(src, edges):
        def at(f, r, col):
            start = (col // 16) * 16
            return src[f, r, start : start + 16, :].astype(F32)[col % 16 : col % 16 + 1]

        place = lax.broadcasted_iota(jnp.int32, (16, CH), 0)
        for f in range(fl):
            for q in range(nz):
                tile = jnp.zeros((16, CH), F32)
                for r in range(rl):
                    if q > 0:
                        tile = jnp.where(place == 2 * r, at(f, r, q * strip - 1), tile)
                    if q < nz - 1:
                        tile = jnp.where(place == 2 * r + 1, at(f, r, (q + 1) * strip), tile)
                edges[q, f] = tile.astype(BF16)
            tile = jnp.zeros((16, CH), F32)
            for r in range(rl):
                outer = jnp.where(w == 0, at(f, r, cols - 1), at(f, r, 0))
                tile = jnp.where(place // 2 == r, outer, tile)
            edges[nz, f] = tile.astype(BF16)

    outer_q = (nz - 1) * w
    takes_outer = z == (nz - 1) * (1 - w)

    def outer_copy(k, edges, landing_out):
        recv = in_recv.at[k, 2 * nz + lax.rem(outer_q - z + nz, nz)]
        return remote(edges.at[nz], landing_out.at[1, own_frames], in_send.at[k], recv, (outer_q, h, 1 - w))

    def start_inputs(k, src, dst, edges, landing, landing_out):
        copies = strip_copies(k, src, dst, edges, landing)
        for _, copy in copies:
            copy.start()
        outer = outer_copy(k, edges, landing_out)
        outer.start()
        return [copy for far, copy in copies if far] + [outer]

    near_first = sorted(range(nz), key=lambda dz: min(dz, nz - dz))

    def pair_from(dz):
        return lax.rem(z - dz + nz, nz) * fl

    def beside_copies(k, dz, cells_in, landing):
        pair = pl.ds(pair_from(dz), fl)
        copies = []
        for dh, r_from, r_to in ((1, rl, 0), (-1, 1, rl + 1)):
            where = dev(0, dh, 0)
            copies.append(
                remote(cells_in.at[pair, pl.ds(r_from, 1)], cells_in.at[pair, pl.ds(r_to, 1)],
                       in_send.at[k], in_recv.at[k, 3 * nz + dz], where)
            )
            copies.append(
                remote(landing.at[1, pair], landing.at[1 - dh, pair], in_send.at[k], in_recv.at[k, 4 * nz + dz], where)
            )
        return copies

    def beside_outer(k, dz, landing_out):
        pair = pl.ds(pair_from(dz), fl)
        return [
            remote(landing_out.at[1, pair], landing_out.at[1 - dh, pair],
                   in_send.at[k], in_recv.at[k, 5 * nz + dz], dev(0, dh, 0))
            for dh in (1, -1)
        ]

    def hand_on(k, dz, cells_in, landing, landing_out):
        pair = pl.ds(pair_from(dz), fl)
        take(cells_in.at[pair, pl.ds(1, rl)], in_recv.at[k, dz])
        take(landing.at[1, pair], in_recv.at[k, nz + dz])
        start_all(beside_copies(k, dz, cells_in, landing))

        @pl.when(takes_outer)
        def _():
            take(landing_out.at[1, pair], in_recv.at[k, 2 * nz + dz])
            start_all(beside_outer(k, dz, landing_out))

    def wait_pair(k, dz, cells_in, landing, landing_out):
        pair = pl.ds(pair_from(dz), fl)
        take(cells_in.at[pair, pl.ds(0, 2)], in_recv.at[k, 3 * nz + dz])
        take(landing.at[pl.ds(0, 2), pair], in_recv.at[k, 4 * nz + dz])

        @pl.when(takes_outer)
        def _():
            take(landing_out.at[pl.ds(0, 2), pair], in_recv.at[k, 5 * nz + dz])

    def close_inputs(k, sent, cells_in, landing, landing_out):
        wait_sends(sent)
        for dz in range(nz):
            wait_sends(beside_copies(k, dz, cells_in, landing))

            @pl.when(takes_outer)
            def _():
                wait_sends(beside_outer(k, dz, landing_out))

    def start_all(copies):
        for copy in copies:
            copy.start()

    def wait_sends(copies):
        for copy in copies:
            copy.wait_send()

    me = (z * nh + h) * 2 + w
    local_size = 4.0 * fl * rl * cols
    total_size = local_size * devices

    def red_start(k, first, second):
        rb[k, me] = pack_pair(first, second)
        slot = rb.at[k, me]
        for_each_device(lambda where: remote(slot, slot, red_send.at[k], red_recv.at[k], where).start())

    def red_wait(k):
        take(rb.at[k, pl.ds(0, devices - 1)], red_recv.at[k])

    def moments_end(k):
        red_wait(k)
        rows = rb[k]
        mean, _ = unpack_pair(jnp.sum(rows, axis=0) / devices)
        low = lanes_low(rows)
        off = rows - jnp.where(lanes_low(mean), mean, 0.0)[None]
        between, within = unpack_pair(jnp.sum(jnp.where(low, off * off, off), axis=0))
        return mean, within + local_size * between

    def sums_end(k):
        red_wait(k)
        return unpack_pair(jnp.sum(rb[k], axis=0) / total_size)

    def turn(source, target):
        for f in range(fl):
            for r in range(rl):
                target[f, r] = jnp.transpose(source[:, f, r, :].astype(F32)).astype(BF16)

    loads[0].wait()
    turn(x_raw, xl)
    build_edges(xl, xe)
    zero8 = jnp.zeros((8, CH), F32)

    def x_sum(n, total):
        return total + fold_rows(xl[n // rl, n % rl].astype(F32))

    local_mean = group_sum(total_row(lax.fori_loop(0, fl * rl, x_sum, zero8))) / local_size

    def x_spread(n, total):
        off = xl[n // rl, n % rl].astype(F32) - local_mean
        return total + fold_rows(off * off)

    local_spread = group_sum(total_row(lax.fori_loop(0, fl * rl, x_spread, zero8)))

    loads[1].wait()
    turn(c_raw, cl)
    build_edges(cl, ce)
    loads[2].wait()
    loads[3].wait()
    for kt in range(3):
        for kr in range(3):
            for kc in range(3):
                tap = 9 * kt + 3 * kr + kc
                back = ((2 - kr) * 3 + (2 - kc)) * CH
                for source, target in ((w1, wb1), (w2, wb2)):
                    target[back : back + CH, kt * CH : (kt + 1) * CH] = source[:, tap * CH : (tap + 1) * CH]
    for kt in range(3):
        for kr in range(3):
            for kc in range(3):
                tap = 9 * kt + 3 * kr + kc
                ahead = (kr * 3 + kc) * CH
                block = w1[:, tap * CH : (tap + 1) * CH].astype(F32)
                wf1[ahead : ahead + CH, (2 - kt) * CH : (3 - kt) * CH] = jnp.transpose(block).astype(BF16)
    pl.semaphore_wait(barrier, devices - 1)
    x_sent = start_inputs(0, xl, xr, xe, xeb, xex)
    red_start(0, local_mean, local_spread)
    c_sent = start_inputs(1, cl, cr, ce, ceb, cex)
    hand_on(0, 0, xr, xeb, xex)
    zero_cells = jnp.zeros((cells, CH), F32)

    def clear(n, _):
        hid[n] = zero_cells
        g2[n] = zero_cells
        g1[n] = zero_cells
        return 0

    lax.fori_loop(0, frames + 2, clear, 0)
    zero_t = jnp.zeros((2 * CH, cells), BF16)
    act_t[0 : 2 * CH] = zero_t
    hg_t[frames * CH : (frames + 2) * CH] = zero_t

    row_place = lax.broadcasted_iota(jnp.int32, (strip, CH), 0)
    left_ok = jnp.logical_not(jnp.logical_and(w == 0, z == 0))
    right_ok = jnp.logical_not(jnp.logical_and(w == 1, z == nz - 1))

    def row_ok(r):
        if r == 0:
            return h > 0
        if r == rl + 1:
            return h < nh - 1
        return None

    def row_source(r):
        if r == 0:
            return 0, rl - 1
        if r == rl + 1:
            return 2, 0
        return 1, r - 1

    def store_stack(stack, f, r, value, left, right):
        ok = row_ok(r)
        left = jnp.where(left_ok if ok is None else jnp.logical_and(left_ok, ok), left, 0.0)
        right = jnp.where(right_ok if ok is None else jnp.logical_and(right_ok, ok), right, 0.0)
        if ok is not None:
            value = jnp.where(ok, value, 0.0)
        before = jnp.where(row_place == 0, left, pltpu.roll(value, 1, 0))
        after = jnp.where(row_place == strip - 1, right, pltpu.roll(value, strip - 1, 0))
        stack[f, r, :, 0:CH] = before.astype(BF16)
        stack[f, r, :, CH : 2 * CH] = value.astype(BF16)
        stack[f, r, :, 2 * CH : 3 * CH] = after.astype(BF16)

    edge_place = lax.broadcasted_iota(jnp.int32, (16, CH), 0)
    outer_mask = jnp.logical_and(takes_outer, edge_place % 2 == 1 - w)

    def input_stack(stack, source, landing, landing_out, apply, start):
        def step(f, _):
            edges = []
            for d in range(3):
                tile = jnp.where(outer_mask, landing_out[d, f].astype(F32), landing[d, f].astype(F32))
                edges.append(apply(tile))
            for r in range(rl + 2):
                d, row = row_source(r)
                tile = edges[d]
                store_stack(
                    stack, f, r, apply(source[f, r].astype(F32)),
                    tile[2 * row : 2 * row + 1], tile[2 * row + 1 : 2 * row + 2],
                )
            return 0

        lax.fori_loop(start, start + fl, step, 0)

    def window(stack, f):
        return [stack[f, kr : kr + rl].reshape(cells, 3 * CH) for kr in range(3)]

    def convolve(stack, weight, target, first=0, last=None):
        def step(f, _):
            product = jnp.dot(
                jnp.concatenate(window(stack, f), axis=1), weight[...], preferred_element_type=F32
            )
            for j in range(3):
                target[f + j] += product[:, j * CH : (j + 1) * CH]
            return 0

        lax.fori_loop(first, frames if last is None else last, step, 0)

    def weight_part(turned, stack, kr):
        left = jnp.concatenate([turned[f * CH : (f + 3) * CH, :] for f in range(frames)], axis=1)
        right = stack[:, kr : kr + rl].reshape(frames * cells, 3 * CH)
        return jnp.dot(left, right, preferred_element_type=F32)

    def peer(axis, j):
        if axis == "z":
            return dev(j, 0, 0)
        if axis == "x":
            return (z, lax.rem(hx + j, nx) * ny + hy, w)
        return (z, hx * ny + lax.rem(hy + j, ny), w)

    coords = {"z": z, "x": hx, "y": hy}
    orders = (("z", "y", "x"), ("y", "x", "z"), ("x", "z", "y"))
    half = 8
    span = half // ns
    tiles = span * 9
    piece = -(-tiles // ns)
    outs = (o1_ref, o2_ref)
    stage_at = {"core": 0, "a1": 1, "a2": 2, "a3": 3, "g2": 4, "g1": 5, "gc": 6}

    def sems(g, p, stage):
        return ar_send.at[g], ar_recv.at[g, p, stage_at[stage]]

    def arrived(g, p, stage, ref):
        take(ref, ar_recv.at[g, p, stage_at[stage]])

    def core_copy(g, p):
        return remote(a.at[g, p, pl.ds((1 - w) * half, half)], r0.at[g, p], *sems(g, p, "core"), dev(0, 0, 1))

    def core_start(g, p):
        core_copy(g, p).start()

    def a1_copies(g, p):
        axis = orders[p][0]
        return [
            remote(
                b1.at[g, p, pl.ds(lax.rem(coords[axis] + j, ns) * span, span)], r1.at[g, p, j - 1],
                *sems(g, p, "a1"), peer(axis, j),
            )
            for j in range(1, ns)
        ]

    def a1_start(g, p):
        arrived(g, p, "core", r0.at[g, p])
        b1[g, p] = a[g, p, pl.ds(w * half, half)] + r0[g, p]
        start_all(a1_copies(g, p))

    def a2_copies(g, p):
        axis = orders[p][1]
        return [
            remote(
                b2.at[g, p, pl.ds(lax.rem(coords[axis] + j, ns) * piece, piece)], r2.at[g, p, j - 1],
                *sems(g, p, "a2"), peer(axis, j),
            )
            for j in range(1, ns)
        ]

    def a2_start(g, p):
        arrived(g, p, "a1", r1.at[g, p])
        value = b1[g, p, pl.ds(coords[orders[p][0]] * span, span)]
        for j in range(ns - 1):
            value = value + r1[g, p, j]
        b2[g, p, 0:tiles] = value.reshape(tiles, 8, CH)
        if piece * ns > tiles:
            b2[g, p, tiles:] = jnp.zeros((piece * ns - tiles, 8, CH), F32)
        start_all(a2_copies(g, p))

    def a3_copies(g, p):
        axis = orders[p][2]
        slot = r3.at[g, p, coords[axis]]
        return [remote(slot, slot, *sems(g, p, "a3"), peer(axis, j)) for j in range(1, ns)]

    def a3_start(g, p):
        arrived(g, p, "a2", r2.at[g, p])
        value = b2[g, p, pl.ds(coords[orders[p][1]] * piece, piece)]
        for j in range(ns - 1):
            value = value + r2[g, p, j]
        r3[g, p, coords[orders[p][2]]] = value
        start_all(a3_copies(g, p))

    def g2_copies(g, p):
        axis = orders[p][1]
        part = g3.at[g, p, pl.ds(coords[axis] * piece, piece)]
        return [remote(part, part, *sems(g, p, "g2"), peer(axis, j)) for j in range(1, ns)]

    def g2_start(g, p):
        arrived(g, p, "a3", r3.at[g, p, pl.ds(0, ns - 1)])
        value = r3[g, p, 0]
        for n in range(1, ns):
            value = value + r3[g, p, n]
        g3[g, p, pl.ds(coords[orders[p][1]] * piece, piece)] = value
        start_all(g2_copies(g, p))

    def out_span(g, p, n):
        return outs[g].at[p, pl.ds(w * half + n * span, span)]

    def g1_copies(g, p):
        axis = orders[p][0]
        part = out_span(g, p, coords[axis])
        return [remote(part, part, *sems(g, p, "g1"), peer(axis, j)) for j in range(1, ns)]

    def gc_copy(g, p, j):
        part = out_span(g, p, lax.rem(coords[orders[p][0]] + ns - j, ns))
        return remote(part, part, *sems(g, p, "gc"), dev(0, 0, 1))

    def g1_start(g, p):
        arrived(g, p, "g2", g3.at[g, p, pl.ds(0, (ns - 1) * piece)])
        outs[g][p, pl.ds(w * half + coords[orders[p][0]] * span, span)] = g3[g, p, 0:tiles].reshape(span, 9, 8, CH)
        start_all(g1_copies(g, p))
        gc_copy(g, p, 0).start()

    def gc_start(g, p):
        arrived(g, p, "g1", outs[g].at[p, pl.ds(0, (ns - 1) * span)])
        for j in range(1, ns):
            gc_copy(g, p, j).start()

    def settle(p, side):
        rows = pl.ds(pl.multiple_of(side * half * 8, half * 8), half * 8)
        for kt in range(3):
            for kc in range(3):
                tap = 9 * kt + 3 * p + kc
                block = o1_ref[p, pl.ds(side * half, half), kt * 3 + kc].reshape(half * 8, CH)
                fin1[rows, tap * CH : (tap + 1) * CH] = block

    def gc_end(g, p):
        arrived(g, p, "gc", outs[g].at[p, pl.ds(0, half)])
        if g == 0:
            settle(p, 1 - w)
            return
        for kt in range(3):
            for kc in range(3):
                tap = 9 * kt + 3 * p + kc
                fin2[:, tap * CH : (tap + 1) * CH] = jnp.transpose(outs[g][p, :, kt * 3 + kc].reshape(CH, CH))

    def ar_close(g):
        for p in range(3):
            wait_sends([core_copy(g, p)] + a1_copies(g, p) + a2_copies(g, p) + a3_copies(g, p))
            wait_sends(g2_copies(g, p) + g1_copies(g, p) + [gc_copy(g, p, j) for j in range(ns)])

    def each(stage, g):
        for p in range(3):
            stage(g, p)

    for dz in near_first[1:]:
        hand_on(0, dz, xr, xeb, xex)
    mean1, spread1 = moments_end(0)
    picks = lax.broadcasted_iota(jnp.int32, (CH // 4, CH), 1) // 4 == lax.broadcasted_iota(jnp.int32, (CH // 4, CH), 0)
    spread_exponent = jnp.dot(
        jnp.broadcast_to(exponent_ref[...].astype(F32), (8, CH // 4)), picks.astype(F32), preferred_element_type=F32
    )
    scale = jnp.exp2(spread_exponent[0:1])
    inv1 = 1.0 / jnp.sqrt(spread1 * (scale * scale) / total_size + EPS)
    factor1 = scale * inv1
    gain1, shift1 = gain1_ref[...], shift1_ref[...]
    gain2, shift2 = gain2_ref[...], shift2_ref[...]

    def rounded(value):
        return value.astype(BF16).astype(F32)

    def act_first(value):
        pre = (value - mean1) * factor1 * gain1 + shift1
        return rounded(pre * sigmoid(pre))

    for n, dz in enumerate(near_first):
        wait_pair(0, dz, xr, xeb, xex)
        start = pair_from(dz)
        input_stack(s1, xr, xeb, xex, act_first, start)
        convolve(s1, wf1, hid, start, start + fl)
        hand_on(1, dz, cr, ceb, cex)

    def hid_sum(n, total):
        return total + fold_rows(hid[n])

    mean_l = group_sum(total_row(lax.fori_loop(0, frames, hid_sum, zero8))) / local_size

    def hid_spread(n, total):
        off = hid[n] - mean_l
        return total + fold_rows(off * off)

    red_start(1, mean_l, group_sum(total_row(lax.fori_loop(0, frames, hid_spread, zero8))))

    for dz in near_first:
        wait_pair(1, dz, cr, ceb, cex)
        start = pair_from(dz)
        input_stack(sc, cr, ceb, cex, lambda value: value, start)
        convolve(sc, wb2, g2, start, start + fl)
    mean2, spread2 = moments_end(1)
    inv2 = 1.0 / jnp.sqrt(spread2 / total_size + EPS)

    def second(n, totals):
        first_total, second_total = totals
        normed = (hid[n] - mean2) * inv2
        pre = normed * gain2 + shift2
        sig = sigmoid(pre)
        act_t[pl.ds(pl.multiple_of((n + 2) * CH, CH), CH), :] = jnp.transpose(pre * sig).astype(BF16)
        scaled = g2[n + 2] * (sig * (1.0 + pre * (1.0 - sig))) * gain2
        nrm[n] = normed
        g2[n + 2] = scaled
        return first_total + fold_rows(scaled), second_total + fold_rows(scaled * normed)

    t1, t2 = lax.fori_loop(0, frames, second, (zero8, zero8))
    red_start(2, group_sum(total_row(t1)), group_sum(total_row(t2)))

    def put_second(kr):
        block = weight_part(act_t, sc, kr)
        for kt in range(3):
            for kc in range(3):
                part = block[kt * CH : (kt + 1) * CH, kc * CH : (kc + 1) * CH]
                a[1, 2 - kr, :, kt * 3 + (2 - kc)] = part.reshape(16, 8, CH)
        core_start(1, 2 - kr)

    for kr in range(3):
        put_second(kr)
    each(a1_start, 1)
    m1, m2 = sums_end(2)

    def hidden(n, _):
        value = inv2 * (g2[n + 2] - m1 - nrm[n] * m2)
        hg_t[pl.ds(pl.multiple_of(n * CH, CH), CH), :] = jnp.transpose(value).astype(BF16)
        narrow = value.astype(BF16)
        hg[n, 1 : rl + 1] = narrow.reshape(rl, strip, CH)
        wide = narrow.astype(F32).reshape(rl, strip, CH)
        lefts = jnp.zeros((16, CH), F32)
        rights = jnp.zeros((16, CH), F32)
        for r in range(rl):
            lefts = jnp.where(edge_place == r, wide[r, 0:1], lefts)
            rights = jnp.where(edge_place == r, wide[r, strip - 1 : strip], rights)
        eh[0, n] = lefts.astype(BF16)
        eh[1, n] = rights.astype(BF16)
        return 0

    lax.fori_loop(0, frames, hidden, 0)

    line = w * nz + z

    def beside(ds, dh):
        place = lax.rem(line + ds + 2 * nz, 2 * nz)
        return (lax.rem(place, nz), lax.rem(h + dh + nh, nh), place // nz)

    halo = [
        remote(hg.at[:, pl.ds(rl, 1)], hg.at[:, pl.ds(0, 1)], halo_send.at[0], halo_recv.at[0], dev(0, 1, 0)),
        remote(hg.at[:, pl.ds(1, 1)], hg.at[:, pl.ds(rl + 1, 1)], halo_send.at[0], halo_recv.at[0], dev(0, -1, 0)),
    ]
    for n, dh in enumerate((0, 1, -1)):
        halo.append(remote(eh.at[0], heb.at[1 - dh, 1], halo_send.at[0], halo_recv.at[1], beside(-1, dh)))
        halo.append(remote(eh.at[1], heb.at[1 - dh, 0], halo_send.at[0], halo_recv.at[1], beside(1, dh)))
    start_all(halo)

    def put_first(kr):
        block = weight_part(hg_t, s1, kr)
        for j in range(3):
            for kc in range(3):
                part = block[j * CH : (j + 1) * CH, kc * CH : (kc + 1) * CH]
                a[0, kr, :, (2 - j) * 3 + kc] = part.reshape(16, 8, CH)
        core_start(0, kr)

    put_first(0)
    put_first(1)
    a1_start(0, 0)
    put_first(2)
    a1_start(0, 1)
    a1_start(0, 2)
    each(a2_start, 1)
    take(hg.at[:, pl.ds(0, 2)], halo_recv.at[0])
    take(heb, halo_recv.at[1])

    def halo_stack(f, _):
        lefts = [heb[d, 0, f].astype(F32) for d in range(3)]
        rights = [heb[d, 1, f].astype(F32) for d in range(3)]
        for r in range(rl + 2):
            d, row = row_source(r)
            store_stack(sh, f, r, hg[f, r].astype(F32), lefts[d][row : row + 1], rights[d][row : row + 1])
        return 0

    lax.fori_loop(0, frames, halo_stack, 0)

    def first(f, totals):
        first_total, second_total = totals
        for r in range(rl):
            normed = (xr[f, r + 1].astype(F32) - mean1) * factor1
            pre = normed * gain1 + shift1
            sig = sigmoid(pre)
            scaled = g1[f + 2, r * strip : (r + 1) * strip] * (sig * (1.0 + pre * (1.0 - sig))) * gain1
            s_out[f, r] = scaled.astype(BF16)
            first_total = first_total + fold_rows(scaled)
            second_total = second_total + fold_rows(scaled * normed)
        return first_total, second_total

    back_from = s_in.at[:, :, pl.ds(pl.multiple_of(z * strip, strip), strip), :]
    back_copies = []

    def send_back(q):
        source = s_out.at[pl.ds(q * fl, fl)]
        far = remote(source, back_from, back_send.at[0], back_recv.at[0], (q, h, w))
        back_copies.append(far)

        @pl.when(z == q)
        def _():
            pltpu.make_async_copy(source, back_from, back_recv.at[0]).start()

        @pl.when(z != q)
        def _():
            far.start()

    convolve(sh, wb1, g1, 0, 2)
    each(a2_start, 0)
    each(a3_start, 1)
    totals = (zero8, zero8)
    for q in range(nz):
        if q * fl + 2 < frames:
            convolve(sh, wb1, g1, q * fl + 2, q * fl + fl + 2)
        totals = lax.fori_loop(q * fl, q * fl + fl, first, totals)
        send_back(q)
        if q == nz // 2 - 1:
            each(a3_start, 0)
            each(g2_start, 1)
    t1, t2 = totals
    red_start(3, group_sum(total_row(t1)), group_sum(total_row(t2)))
    each(g2_start, 0)
    each(g1_start, 1)
    each(g1_start, 0)
    m1, m2 = sums_end(3)
    take(s_in, back_recv.at[0])

    for f in range(fl):
        for r in range(rl):
            normed = (xl[f, r].astype(F32) - mean1) * factor1
            value = cl[f, r].astype(F32) + inv1 * (s_in[f, r].astype(F32) - m1 - normed * m2)
            out_ref[:, f, r, :] = jnp.transpose(value)
    each(gc_start, 1)
    each(gc_end, 1)
    close_inputs(0, x_sent, xr, xeb, xex)
    close_inputs(1, c_sent, cr, ceb, cex)
    for k in range(4):
        take(rb.at[k, pl.ds(0, devices - 1)], red_send.at[k])
    wait_sends(halo)
    for q in range(nz):

        @pl.when(z != q)
        def _():
            back_copies[q].wait_send()

    ar_close(1)
    each(gc_start, 0)
    for p in range(3):
        settle(p, w)
    each(gc_end, 0)
    ar_close(0)


def copy_body(*refs):
    sources, targets, store_sem = refs[0:3], refs[3:6], refs[6]
    stores = [pltpu.make_async_copy(sources[n], targets[n], store_sem.at[n]) for n in range(3)]
    for copy in stores:
        copy.start()
    for copy in stores:
        copy.wait()


def shards(sizes, latent, exponents, cotangent, conv_first, conv_second, gain_first, shift_first, gain_second, shift_second):
    nz, nh, nx, ny = sizes
    channels, fl, rl, cols = latent.shape
    strip = cols // nz
    frames = fl * nz
    cells = rl * strip
    ns = nx
    span = 8 // ns
    tiles = span * 9
    piece = -(-tiles // ns)
    vmem = pl.BlockSpec(memory_space=pltpu.VMEM)
    any_space = pl.BlockSpec(memory_space=pl.ANY)
    part = (3, 16, 9, 8, CH)
    wide = (frames, rl + 2, strip, 3 * CH)
    scratch = [
        pltpu.VMEM((CH, fl, rl, cols), BF16),
        pltpu.VMEM((CH, fl, rl, cols), BF16),
        pltpu.VMEM((fl, rl, cols, CH), BF16),
        pltpu.VMEM((fl, rl, cols, CH), BF16),
        pltpu.VMEM((CH, 27 * CH), BF16),
        pltpu.VMEM((CH, 27 * CH), BF16),
        pltpu.VMEM(part, F32),
        pltpu.VMEM(part, F32),
        pltpu.VMEM((frames, rl + 2, strip, CH), BF16),
        pltpu.VMEM((frames, rl + 2, strip, CH), BF16),
        pltpu.VMEM((nz + 1, fl, 16, CH), BF16),
        pltpu.VMEM((nz + 1, fl, 16, CH), BF16),
        pltpu.VMEM((3, frames, 16, CH), BF16),
        pltpu.VMEM((3, frames, 16, CH), BF16),
        pltpu.VMEM((3, frames, 16, CH), BF16),
        pltpu.VMEM((3, frames, 16, CH), BF16),
        pltpu.VMEM(wide, BF16),
        pltpu.VMEM(wide, BF16),
        pltpu.VMEM(wide, BF16),
        pltpu.VMEM((frames + 2, cells, CH), F32),
        pltpu.VMEM((frames + 2, cells, CH), F32),
        pltpu.VMEM((frames + 2, cells, CH), F32),
        pltpu.VMEM((frames, cells, CH), F32),
        pltpu.VMEM(((frames + 2) * CH, cells), BF16),
        pltpu.VMEM(((frames + 2) * CH, cells), BF16),
        pltpu.VMEM((frames, rl + 2, strip, CH), BF16),
        pltpu.VMEM((2, frames, 16, CH), BF16),
        pltpu.VMEM((3, 2, frames, 16, CH), BF16),
        pltpu.VMEM((9 * CH, 3 * CH), BF16),
        pltpu.VMEM((9 * CH, 3 * CH), BF16),
        pltpu.VMEM((9 * CH, 3 * CH), BF16),
        pltpu.VMEM((frames, rl, strip, CH), BF16),
        pltpu.VMEM((fl, rl, cols, CH), BF16),
        pltpu.VMEM((4, 2 * nz * nh, 1, CH), F32),
        pltpu.VMEM((2, 3, 16, 9, 8, CH), F32),
        pltpu.VMEM((2, 3, 8, 9, 8, CH), F32),
        pltpu.VMEM((2, 3, 8, 9, 8, CH), F32),
        pltpu.VMEM((2, 3, ns - 1, span, 9, 8, CH), F32),
        pltpu.VMEM((2, 3, piece * ns, 8, CH), F32),
        pltpu.VMEM((2, 3, ns - 1, piece, 8, CH), F32),
        pltpu.VMEM((2, 3, ns, piece, 8, CH), F32),
        pltpu.VMEM((2, 3, piece * ns, 8, CH), F32),
        pltpu.SemaphoreType.DMA((4,)),
        pltpu.SemaphoreType.DMA((2,)),
        pltpu.SemaphoreType.DMA((2, 6 * nz)),
        pltpu.SemaphoreType.DMA((4,)),
        pltpu.SemaphoreType.DMA((4,)),
        pltpu.SemaphoreType.DMA((1,)),
        pltpu.SemaphoreType.DMA((2,)),
        pltpu.SemaphoreType.DMA((1,)),
        pltpu.SemaphoreType.DMA((1,)),
        pltpu.SemaphoreType.DMA((2,)),
        pltpu.SemaphoreType.DMA((2, 3, 7)),
    ]
    results = pl.pallas_call(
        functools.partial(body, sizes),
        out_shape=(
            pltpu.VMEM((CH, fl, rl, cols), F32),
            pltpu.VMEM((CH, 27 * CH), F32),
            pltpu.VMEM((CH, 27 * CH), F32),
        ),
        in_specs=[any_space] * 4 + [vmem] * 5,
        out_specs=(vmem,) * 3,
        scratch_shapes=scratch,
        compiler_params=pltpu.CompilerParams(
            collective_id=0, has_side_effects=True, vmem_limit_bytes=58 * 1024 * 1024
        ),
    )(
        latent, cotangent, conv_first, conv_second, exponents[None],
        gain_first[None], shift_first[None], gain_second[None], shift_second[None],
    )
    return pl.pallas_call(
        copy_body,
        out_shape=[jax.ShapeDtypeStruct(value.shape, F32) for value in results],
        in_specs=[vmem] * 3,
        out_specs=[any_space] * 3,
        scratch_shapes=[pltpu.SemaphoreType.DMA((3,))],
        compiler_params=pltpu.CompilerParams(vmem_limit_bytes=8 * 1024 * 1024),
    )(*results)


def solution(mesh):
    nz, nh = mesh.shape["tm"], mesh.shape["height"]
    nx = int(round(nh**0.5))
    placed = P(None, "tm", "height", "width")
    return jax.shard_map(
        functools.partial(shards, (nz, nh, nx, nh // nx)),
        mesh=mesh,
        in_specs=(placed, P(), placed, P(), P(), P(), P(), P(), P()),
        out_specs=(placed, P(), P()),
        check_vma=False,
    )
```
